128 devices in a mesh: group: 32 (over x, z, core), expert: 4 (over y).
Axes of the slice: x: 4, y: 4, z: 4, core: 2. Of those that a mesh axis runs over, the one named last changes fastest.
Arguments:
- tokens: bfloat16 [16384, 1024], P(('group', 'expert')), may hold values from -6 to 6
- routes: int32 [1, 16384, 8], P(None, ('group', 'expert')), may hold values from 0 to 11, all different within a row
- slot_order: int32 [1, 128, 128], P(None, ('group', 'expert')), may hold values from 0 to 127, each once within a row
- prefix: int32 [32], P('group'), may hold values from 51 to 256
- attn_gain: float32 [1, 1024], replicated, may hold values from 0.5 to 1.5
- w_query: bfloat16 [1, 1024, 1024], replicated, may hold values from -0.25 to 0.25
- w_key: bfloat16 [1, 1024, 512], replicated, may hold values from -0.25 to 0.25
- w_value: bfloat16 [1, 1024, 512], replicated, may hold values from -0.1875 to 0.1875
- w_out: bfloat16 [1, 1024, 1024], replicated, may hold values from -0.75 to 0.75
- ffn_gain: float32 [1, 1024], replicated, may hold values from 0.5 to 1.5
- w_router: bfloat16 [1, 1024, 12], replicated, may hold values from -0.09375 to 0.09375
- w_gate: bfloat16 [1, 12, 1024, 512], P(None, 'expert'), may hold values from -0.1875 to 0.1875
- w_up: bfloat16 [1, 12, 1024, 512], P(None, 'expert'), may hold values from -0.1875 to 0.1875
- w_down: bfloat16 [1, 12, 512, 1024], P(None, 'expert'), may hold values from -0.5 to 0.5
- cotangent: float32 [16384, 1024], P(('group', 'expert')), may hold values from -6 to 6
Outputs:
- hidden_out: float32 [16384, 1024], P(('group', 'expert'))
- input_grad: float32 [16384, 1024], P(('group', 'expert'))
- grad_attn_gain: float32 [1, 1024], P(None, ('group', 'expert'))
- grad_query: float32 [1, 1024, 1024], P(None, ('group', 'expert'))
- grad_key: float32 [1, 1024, 512], P(None, ('group', 'expert'))
- grad_value: float32 [1, 1024, 512], P(None, ('group', 'expert'))
- grad_out: float32 [1, 1024, 1024], P(None, None, ('group', 'expert'))
- grad_ffn_gain: float32 [1, 1024], P(None, ('group', 'expert'))
- grad_router: float32 [1, 1024, 12], P(None, ('group', 'expert'))
- grad_gate: float32 [1, 12, 1024, 512], P(None, 'expert', 'group')
- grad_up: float32 [1, 12, 1024, 512], P(None, 'expert', 'group')
- grad_down: float32 [1, 12, 512, 1024], P(None, 'expert', None, 'group')
The draws below stay inside these ranges and needn't reach their ends.
Inputs may be any that keep to these rules, and one draw needn't show every extreme that they name: `routes`: each row names 8 different experts. `slot_order`: each device's row of 128 entries in each layer is a permutation.
All inputs are finite; a program needn't handle non-finite values.
Results may differ from the reference program's by a relative error of at most 0.02.
Values may be sent and summed in bfloat16 or wider, within the bound.
A program may use at most 128 MiB of HBM per device.

```python
from functools import partial
import jax
import jax.numpy as jnp
from jax import lax

D = 1024
HEADS = 16
KV_HEADS = 8
HEAD = 64
EFF = 512
TOP = 8
LAYERS = 1
TOK_DEV = 128
EXPERTS = 12
SEQ = 512
TOKENS = 16384
CAP = 96
N_GROUP = 32
N_EXPERT = 4


def plant(drawn, key, low, top_value):
    shape = drawn.shape
    index_at = [jax.random.randint(jax.random.fold_in(key, axis), (), 0, shape[axis]) for axis in range(len(shape))]
    drawn = drawn.at[tuple(index_at)].set(low)
    longest = shape.index(max(shape))
    index_at[longest] = (index_at[longest] + 1) % shape[longest]
    return drawn.at[tuple(index_at)].set(top_value)


def block_scale(own_key, extent, shards, least, high):
    loudness, own = 1.0, jax.random.fold_in(own_key, 6)
    for position, shards_of in shards:
        heights = jnp.exp(jax.random.uniform(jax.random.fold_in(own, position), (shards_of,), jnp.float32, least / len(shards), high / len(shards)))
        loudness = loudness * jnp.repeat(heights, extent[position] // shards_of).reshape([-1 if axis == position else 1 for axis in range(len(extent))])
    return loudness


def picks_of(stream_key, rows, number_of, top, lift):
    order = jax.random.permutation(jax.random.fold_in(stream_key, 1), number_of)
    favour = order
    for power in range(3):
        favour = favour * favour // number_of
    favour = favour * lift // number_of
    chance = jax.random.randint(jax.random.fold_in(stream_key, 2), (rows, number_of), 0, 4096) + favour
    holders = jax.random.permutation(jax.random.fold_in(stream_key, 3), rows)[jnp.arange(number_of) % rows]
    chance = jnp.where(jnp.arange(rows)[:, None] == holders[None, :], 1 << 14, chance)
    priority = chance * number_of + jnp.arange(number_of)
    return lax.top_k(priority.astype(jnp.int32), top)[1].astype(jnp.int32)


def scatter_about(rng, shape, scale, bound, cuts=(), kind=jnp.bfloat16):
    entries = scale * jax.random.normal(rng, shape, jnp.float32)
    if cuts:
        entries = entries * block_scale(rng, shape, cuts, -0.22, 0.18)
    return jnp.clip(entries, -bound, bound).astype(kind)


def setup_inputs(seed: int = 0) -> dict:
    arg_keys = jax.random.split(jax.random.key(seed), 16)
    tokens = scatter_about(arg_keys[0], (TOKENS, D), 1.0, 6.0, ((0, 128),))
    routes = picks_of(arg_keys[1], LAYERS * TOKENS, EXPERTS, TOP, 5461).reshape((LAYERS, TOKENS, TOP))
    slot_order = jax.vmap(lambda own: jax.random.permutation(own, TOK_DEV))(jax.random.split(arg_keys[2], LAYERS * (N_GROUP * N_EXPERT))).reshape((LAYERS, N_GROUP * N_EXPERT, TOK_DEV)).astype(jnp.int32)
    prefix = plant(jax.random.randint(arg_keys[3], (N_GROUP,), SEQ // 10, SEQ // 2 + 1), jax.random.fold_in(arg_keys[3], 1), SEQ // 10, (SEQ // 2 + 1) - 1).astype(jnp.int32)
    attn_gain = jnp.clip(1.0 + 0.1 * jax.random.normal(arg_keys[4], (LAYERS, D), jnp.float32), 0.5, 1.5)
    w_query = scatter_about(arg_keys[5], (LAYERS, D, HEADS * HEAD), (D // 2) ** -0.5, 0.25)
    w_key = scatter_about(arg_keys[6], (LAYERS, D, KV_HEADS * HEAD), (D // 2) ** -0.5, 0.25)
    w_value = scatter_about(arg_keys[7], (LAYERS, D, KV_HEADS * HEAD), D ** -0.5, 0.1875)
    w_out = scatter_about(arg_keys[8], (LAYERS, HEADS * HEAD, D), (HEADS * HEAD // 16) ** -0.5, 0.75)
    ffn_gain = jnp.clip(1.0 + 0.1 * jax.random.normal(arg_keys[9], (LAYERS, D), jnp.float32), 0.5, 1.5)
    w_router = scatter_about(arg_keys[10], (LAYERS, D, EXPERTS), (4 * D) ** -0.5, 0.09375)
    w_gate = scatter_about(arg_keys[11], (LAYERS, EXPERTS, D, EFF), D ** -0.5, 0.1875, ((1, 4),))
    w_up = scatter_about(arg_keys[12], (LAYERS, EXPERTS, D, EFF), D ** -0.5, 0.1875, ((1, 4),))
    w_down = scatter_about(arg_keys[13], (LAYERS, EXPERTS, EFF, D), (EFF // 4) ** -0.5, 0.5, ((1, 4),))
    cotangent = scatter_about(arg_keys[14], (TOKENS, D), 1.0, 6.0, ((0, 128),), jnp.float32)
    return dict(tokens=tokens, routes=routes, slot_order=slot_order, prefix=prefix, attn_gain=attn_gain, w_query=w_query, w_key=w_key, w_value=w_value, w_out=w_out, ffn_gain=ffn_gain, w_router=w_router, w_gate=w_gate, w_up=w_up, w_down=w_down, cotangent=cotangent)


@jax.custom_vjp
def low(v):
    return lax.optimization_barrier(v.astype(jnp.bfloat16)).astype(jnp.float32)

@jax.custom_vjp
def low_back(v):
    return v

def low_keep(v):
    return (low(v), None)

def low_pass(kept, grad):
    return (grad,)

def back_keep(v):
    return (v, None)

def back_low(kept, grad):
    return (low(grad),)
low.defvjp(low_keep, low_pass)
low_back.defvjp(back_keep, back_low)
norm_eps = 1e-06
highest = lax.Precision.HIGHEST

def rms_scale(values, gain):
    return values * lax.rsqrt(lax.optimization_barrier(jnp.mean(values * values, axis=-1, keepdims=True)) + norm_eps) * gain

def rotate(tensor, places):
    half_width = tensor.shape[-1] // 2
    inverse = 10000.0 ** (-jnp.arange(half_width, dtype=jnp.float32) / half_width)
    angles = places.astype(jnp.float32)[:, None] * inverse[None, :]
    cosine = jnp.cos(angles)[:, None, :]
    sine_part = jnp.sin(angles)[:, None, :]
    first_half = tensor[..., :half_width]
    second = tensor[..., half_width:]
    return jnp.concatenate([first_half * cosine - second * sine_part, second * cosine + first_half * sine_part], axis=-1)

def route_tables(chosen, rank_rows, experts, capacity):
    token_count, top_count = chosen.shape
    pick_table = (chosen[:, :, None] == jnp.arange(experts, dtype=jnp.int32)[None, None, :]).astype(jnp.int32)
    member = lax.optimization_barrier(jnp.sum(pick_table, axis=1))
    earlier = (rank_rows[None, :] < rank_rows[:, None]).astype(jnp.float32)
    before = jnp.dot(earlier, member.astype(jnp.float32), precision=highest).astype(jnp.int32)
    slot_index = lax.optimization_barrier(jnp.sum(pick_table * before[:, None, :], axis=2))
    kept_pair = slot_index < capacity
    flat_index = jnp.where(kept_pair, chosen * capacity + slot_index, 0).astype(jnp.int32)
    owner_row = jnp.arange(token_count * top_count, dtype=jnp.int32) // top_count
    matches = (flat_index.reshape(-1)[:, None] == jnp.arange(experts * capacity, dtype=jnp.int32)[None, :]) & kept_pair.reshape(-1)[:, None]
    source = lax.optimization_barrier(jnp.sum(jnp.where(matches, owner_row[:, None], 0), axis=0)).astype(jnp.int32)
    filled = jnp.any(matches, axis=0)
    return (pick_table, kept_pair, flat_index, source, filled, matches)

def pick_rows(rows, index_rows):
    return jnp.take(rows, index_rows, axis=0)

def one_layer(current, weights, chosen, rank_rows, prefix_len):
    length = current.shape[0]
    places = jnp.arange(length, dtype=jnp.int32)
    normed = low(rms_scale(current, weights['attn_gain']))
    query_lin = low_back(jnp.dot(normed, weights['w_query'], precision=highest))
    queries = low(rotate(query_lin.reshape(length, HEADS, HEAD), places))
    key_lin = low_back(jnp.dot(normed, weights['w_key'], precision=highest))
    key_rows = low(rotate(key_lin.reshape(length, KV_HEADS, HEAD), places))
    value_rows = low(low_back(jnp.dot(normed, weights['w_value'], precision=highest))).reshape(length, KV_HEADS, HEAD)
    grouped = queries.reshape(length, KV_HEADS, HEADS // KV_HEADS, HEAD)
    raw_scores = low_back(jnp.einsum('ikgd,jkd->kgij', grouped, key_rows, precision=highest))
    visible = (places[None, :] < prefix_len) | (places[None, :] <= places[:, None])
    scores = jnp.where(visible, raw_scores * HEAD ** (-0.5), -1e+30)
    soft_probs = low(jax.nn.softmax(scores, axis=-1))
    mixed_heads = jnp.einsum('kgij,jkd->ikgd', soft_probs, value_rows, precision=highest)
    joined = low(low_back(mixed_heads.reshape(length, HEADS * HEAD)))
    middle = current + low_back(jnp.dot(joined, weights['w_out'], precision=highest))
    moe_in = low(rms_scale(middle, weights['ffn_gain']))
    logits = low_back(jnp.dot(moe_in, weights['w_router'], precision=highest))
    per_dev = moe_in.reshape(N_EXPERT, TOK_DEV, D)
    logit_dev = logits.reshape(N_EXPERT, TOK_DEV, EXPERTS)
    tables = jax.vmap(partial(route_tables, experts=EXPERTS, capacity=CAP))(chosen, rank_rows)
    pick_table, kept_pair, flat_index, source, filled, matches = tables
    selected = lax.optimization_barrier(jnp.sum(pick_table * logit_dev[:, :, None, :], axis=-1))
    gate_probs = jax.nn.softmax(selected, axis=-1)
    sent_rows = jax.vmap(pick_rows)(per_dev, source) * filled[:, :, None].astype(jnp.float32)
    sent_rows = low_back(sent_rows).reshape(N_EXPERT, EXPERTS, CAP, D)
    gate_lin = low_back(jnp.einsum('secd,edf->secf', sent_rows, weights['w_gate'], precision=highest))
    up_lin = low_back(jnp.einsum('secd,edf->secf', sent_rows, weights['w_up'], precision=highest))
    hidden_act = low(jax.nn.silu(gate_lin) * up_lin)
    returned = low(low_back(jnp.einsum('secf,efd->secd', hidden_act, weights['w_down'], precision=highest)))
    taken_rows = jax.vmap(pick_rows)(returned.reshape(N_EXPERT, EXPERTS * CAP, D), flat_index.reshape(N_EXPERT, TOK_DEV * TOP))
    taken_rows = taken_rows.reshape(N_EXPERT, TOK_DEV, TOP, D)
    weighting = gate_probs * kept_pair.astype(jnp.float32)
    mixture = lax.optimization_barrier(jnp.sum(weighting[..., None] * taken_rows, axis=2))
    return middle + mixture.reshape(length, D)

def reference(tokens, routes, slot_order, prefix, attn_gain, w_query, w_key, w_value, w_out, ffn_gain, w_router, w_gate, w_up, w_down, cotangent):
    param_names = ['attn_gain', 'w_query', 'w_key', 'w_value', 'w_out', 'ffn_gain', 'w_router', 'w_gate', 'w_up', 'w_down']
    arrays = [attn_gain, w_query, w_key, w_value, w_out, ffn_gain, w_router, w_gate, w_up, w_down]
    params = {name_key: array_in.astype(jnp.float32) for name_key, array_in in zip(param_names, arrays)}
    starts = tokens.astype(jnp.float32).reshape(N_GROUP, SEQ, D)
    chosen_all = routes.reshape(LAYERS, N_GROUP, N_EXPERT, TOK_DEV, TOP).transpose(1, 0, 2, 3, 4)
    ranks_all = slot_order.reshape(LAYERS, N_GROUP, N_EXPERT, TOK_DEV).transpose(1, 0, 2, 3)
    upstream = cotangent.reshape(N_GROUP, SEQ, D)

    def forward(current, weights, chosen, rank_rows, prefix_len):
        for layer_index in range(LAYERS):
            layer_weights = {name_key: weights[name_key][layer_index] for name_key in weights}
            current = one_layer(current, layer_weights, chosen[layer_index], rank_rows[layer_index], prefix_len)
        return current

    def scan_group(totals, slices):
        current, chosen, rank_rows, prefix_len, seed_grad = slices

        def closed(start_rows, weights):
            return forward(start_rows, weights, chosen, rank_rows, prefix_len)
        result, pullback = jax.vjp(closed, current, params)
        grad_in, grad_weights = pullback(seed_grad)
        return (jax.tree.map(jnp.add, totals, grad_weights), (result, grad_in))
    totals, (results, grad_ins) = lax.scan(scan_group, jax.tree.map(jnp.zeros_like, params), (starts, chosen_all, ranks_all, prefix, upstream))
    return (results.reshape(TOKENS, D), grad_ins.reshape(TOKENS, D), totals['attn_gain'], totals['w_query'], totals['w_key'], totals['w_value'], totals['w_out'], totals['ffn_gain'], totals['w_router'], totals['w_gate'], totals['w_up'], totals['w_down'])
```

```python
from functools import partial
from types import SimpleNamespace

import jax
import jax.numpy as jnp
from jax import lax
from jax.experimental import pallas as pl
from jax.experimental.pallas import tpu as pltpu
from jax.sharding import PartitionSpec as P

HEAD = 64
MESH = pl.DeviceIdType.MESH
EXPERT_UNITS = 9
UNITS = 16
WIDE = 512


def ring_places():
    group = lax.axis_index("group")
    return group // 8, (group // 2) % 4, group % 2, lax.axis_index("expert")


def group_of(x_at, z_at, core):
    return x_at * 8 + z_at * 2 + core


def sum32(first, second):
    return (first.astype(jnp.float32) + second.astype(jnp.float32)).astype(jnp.bfloat16)


def reduce_kernel(
    grads, expert_out, shared_out,
    pair_in, held, lo_in, hi_in, minus_in, plus_in, plus_out, minus_out,
    held_b, lo_in_b, hi_in_b, minus_in_b, plus_in_b, plus_out_b, minus_out_b,
    last, last_in, own_copy,
    send_sem, recv_sem, local_sem,
):
    x_at, z_at, core, y_at = ring_places()
    other = 1 - core
    spots = (x_at, z_at)

    def device(axis, offset):
        if axis == 0:
            return (group_of((x_at + offset) % 4, z_at, core), y_at)
        return (group_of(x_at, (z_at + offset) % 4, core), y_at)

    partner = (group_of(x_at, z_at, other), y_at)
    barrier = pltpu.get_barrier_semaphore()
    peers = [partner] + [device(axis, off) for axis in (0, 1) for off in (1, 3)]
    peers += [(lax.axis_index("group"), (y_at + off) % 4) for off in (1, 2, 3)]
    for peer in peers:
        pl.semaphore_signal(barrier, inc=1, device_id=peer, device_id_type=MESH)
    pl.semaphore_wait(barrier, len(peers))

    def remote(unit, kind, src, dst, target):
        return pltpu.make_async_remote_copy(
            src_ref=src, dst_ref=dst, send_sem=send_sem.at[kind, unit],
            recv_sem=recv_sem.at[kind, unit], device_id=target, device_id_type=MESH,
        )

    def pair_copy(unit):
        return remote(unit, 0, grads.at[unit, :, :, other], pair_in.at[unit], partner)

    def own_load(unit):
        return pltpu.make_async_copy(grads.at[unit, :, :, core], own_copy.at[unit], local_sem.at[unit])

    def each(body):
        def step(unit, carry):
            body(unit)
            return carry
        lax.fori_loop(0, UNITS, step, 0)

    def each_pair(body):
        def step(half, carry):
            body(half * 2, 0)
            body(half * 2 + 1, 1)
            return carry
        lax.fori_loop(0, UNITS // 2, step, 0)

    def start_pair(unit):
        pair_copy(unit).start()
        own_load(unit).start()

    each(start_pair)

    def block(unit, axis, index):
        return held.at[unit, index] if axis == 0 else held.at[unit, :, index]

    def a_far(unit, axis, way):
        far = (spots[axis] + 2) % 4
        lanes = pl.ds(0, WIDE // 2) if way == 0 else pl.ds(WIDE // 2, WIDE // 2)
        dst = lo_in if way == 0 else hi_in
        return remote(unit, 1 + way, block(unit, axis, far).at[:, :, lanes], dst.at[unit], device(axis, 1 if way == 0 else 3))

    def a_near(unit, axis, way):
        src, dst = (plus_out, minus_in) if way == 0 else (minus_out, plus_in)
        return remote(unit, 3 + way, src.at[unit], dst.at[unit], device(axis, 1 if way == 0 else 3))

    def stage_pair(unit, axis):
        pair_copy(unit).wait()
        own_load(unit).wait()
        for slab in range(4):
            held[unit, slab] = sum32(own_copy[unit, slab], pair_in[unit, slab])
        a_far(unit, axis, 0).start()
        a_far(unit, axis, 1).start()

    each_pair(stage_pair)

    def stage_far(unit, axis):
        half = WIDE // 2
        for way in (0, 1):
            a_far(unit, axis, way).wait()
            near = (spots[axis] + (1 if way == 0 else 3)) % 4
            mine = block(unit, axis, near)
            out, came = (plus_out, lo_in) if way == 0 else (minus_out, hi_in)
            first, second = (slice(0, half), slice(half, WIDE)) if way == 0 else (slice(half, WIDE), slice(0, half))
            out[unit, :, :, first] = sum32(mine[:, :, first], came[unit])
            out[unit, :, :, second] = mine[:, :, second]
            a_near(unit, axis, way).start()

    each_pair(stage_far)

    def b_far(unit, axis, way):
        far = (spots[1 - axis] + 2) % 4
        lanes = pl.ds(0, WIDE // 2) if way == 0 else pl.ds(WIDE // 2, WIDE // 2)
        dst = lo_in_b if way == 0 else hi_in_b
        return remote(unit, 5 + way, held_b.at[unit, far, :, lanes], dst.at[unit], device(1 - axis, 1 if way == 0 else 3))

    def b_near(unit, axis, way):
        src, dst = (plus_out_b, minus_in_b) if way == 0 else (minus_out_b, plus_in_b)
        return remote(unit, 7 + way, src.at[unit], dst.at[unit], device(1 - axis, 1 if way == 0 else 3))

    def stage_near(unit, axis):
        for way in (0, 1):
            a_near(unit, axis, way).wait()
        mine = block(unit, axis, spots[axis])
        total = mine[...].astype(jnp.float32) + minus_in[unit].astype(jnp.float32)
        held_b[unit] = (total + plus_in[unit].astype(jnp.float32)).astype(jnp.bfloat16)
        for way in (0, 1):
            b_far(unit, axis, way).start()

    each_pair(stage_near)

    def stage_far_b(unit, axis):
        half = WIDE // 2
        for way in (0, 1):
            b_far(unit, axis, way).wait()
            near = (spots[1 - axis] + (1 if way == 0 else 3)) % 4
            out, came = (plus_out_b, lo_in_b) if way == 0 else (minus_out_b, hi_in_b)
            first, second = (slice(0, half), slice(half, WIDE)) if way == 0 else (slice(half, WIDE), slice(0, half))
            out[unit, :, first] = sum32(held_b[unit, near, :, first], came[unit])
            out[unit, :, second] = held_b[unit, near, :, second]
            b_near(unit, axis, way).start()

    each_pair(stage_far_b)

    def across(unit, off):
        to = (y_at + off) % 4
        return remote(unit, 8 + off, last.at[unit, pl.ds(to * 8, 8)], last_in.at[off - 1, unit], (lax.axis_index("group"), to))

    def final_sum(unit, axis):
        for way in (0, 1):
            b_near(unit, axis, way).wait()
        total = held_b[unit, spots[1 - axis]].astype(jnp.float32) + minus_in_b[unit].astype(jnp.float32)
        return total + plus_in_b[unit].astype(jnp.float32)

    def stage_last(unit, axis):
        total = final_sum(unit, axis)
        last[unit] = total

        @pl.when(unit < EXPERT_UNITS)
        def _():
            expert_out[unit] = total

        @pl.when(unit >= EXPERT_UNITS)
        def _():
            for off in (1, 2, 3):
                across(unit, off).start()

    each_pair(stage_last)

    def finish(step, carry):
        unit = step + EXPERT_UNITS
        for off in (1, 2, 3):
            across(unit, off).wait()
        total = last[unit, pl.ds(pl.multiple_of(y_at * 8, 8), 8), :]
        for off in (1, 2, 3):
            total = total + last_in[off - 1, unit]
        shared_out[step] = total
        return carry

    lax.fori_loop(0, UNITS - EXPERT_UNITS, finish, 0)


def reduce_grads(grads):
    half = WIDE // 2
    low = jnp.bfloat16
    shapes = [
        pltpu.VMEM((UNITS, 4, 4, 32, WIDE), low),
        pltpu.VMEM((UNITS, 4, 4, 32, WIDE), low),
        pltpu.VMEM((UNITS, 4, 32, half), low),
        pltpu.VMEM((UNITS, 4, 32, half), low),
        pltpu.VMEM((UNITS, 4, 32, WIDE), low),
        pltpu.VMEM((UNITS, 4, 32, WIDE), low),
        pltpu.VMEM((UNITS, 4, 32, WIDE), low),
        pltpu.VMEM((UNITS, 4, 32, WIDE), low),
        pltpu.VMEM((UNITS, 4, 32, WIDE), low),
        pltpu.VMEM((UNITS, 32, half), low),
        pltpu.VMEM((UNITS, 32, half), low),
        pltpu.VMEM((UNITS, 32, WIDE), low),
        pltpu.VMEM((UNITS, 32, WIDE), low),
        pltpu.VMEM((UNITS, 32, WIDE), low),
        pltpu.VMEM((UNITS, 32, WIDE), low),
        pltpu.VMEM((UNITS, 32, WIDE), jnp.float32),
        pltpu.VMEM((3, UNITS, 8, WIDE), jnp.float32),
        pltpu.VMEM((UNITS, 4, 4, 32, WIDE), low),
        pltpu.SemaphoreType.DMA((12, UNITS)),
        pltpu.SemaphoreType.DMA((12, UNITS)),
        pltpu.SemaphoreType.DMA((UNITS,)),
    ]
    vmem = pl.BlockSpec(memory_space=pltpu.VMEM)
    return pl.pallas_call(
        reduce_kernel,
        out_shape=(
            jax.ShapeDtypeStruct((EXPERT_UNITS, 32, WIDE), jnp.float32),
            jax.ShapeDtypeStruct((UNITS - EXPERT_UNITS, 8, WIDE), jnp.float32),
        ),
        in_specs=[pl.BlockSpec(memory_space=pl.ANY)],
        out_specs=(vmem, vmem),
        scratch_shapes=shapes,
        compiler_params=pltpu.CompilerParams(
            collective_id=0, has_side_effects=True, vmem_limit_bytes=58 * 2**20
        ),
        name="reduce_grads",
    )(grads)


norm_eps = 1e-06
highest = lax.Precision.HIGHEST


def rms_scale(values, gain):
    return values * lax.rsqrt(jnp.mean(values * values, axis=-1, keepdims=True) + norm_eps) * gain


def rotate(tensor, places):
    half_width = tensor.shape[-1] // 2
    inverse = 10000.0 ** (-jnp.arange(half_width, dtype=jnp.float32) / half_width)
    angles = places.astype(jnp.float32)[:, None] * inverse[None, :]
    cosine = jnp.cos(angles)[:, None, :]
    sine_part = jnp.sin(angles)[:, None, :]
    first_half = tensor[..., :half_width]
    second = tensor[..., half_width:]
    return jnp.concatenate(
        [first_half * cosine - second * sine_part, second * cosine + first_half * sine_part],
        axis=-1,
    )


def route_tables(chosen, rank_rows, experts, capacity):
    token_count, top_count = chosen.shape
    pick_table = (chosen[:, :, None] == jnp.arange(experts, dtype=jnp.int32)[None, None, :]).astype(
        jnp.int32
    )
    member = jnp.sum(pick_table, axis=1)
    earlier = (rank_rows[None, :] < rank_rows[:, None]).astype(jnp.float32)
    before = jnp.dot(earlier, member.astype(jnp.float32), precision=highest).astype(jnp.int32)
    slot_index = jnp.sum(pick_table * before[:, None, :], axis=2)
    kept_pair = slot_index < capacity
    flat_index = jnp.where(kept_pair, chosen * capacity + slot_index, 0).astype(jnp.int32)
    owner_row = jnp.arange(token_count * top_count, dtype=jnp.int32) // top_count
    matches = (
        flat_index.reshape(-1)[:, None] == jnp.arange(experts * capacity, dtype=jnp.int32)[None, :]
    ) & kept_pair.reshape(-1)[:, None]
    source = jnp.sum(jnp.where(matches, owner_row[:, None], 0), axis=0)
    filled = jnp.any(matches, axis=0)
    return (pick_table, kept_pair, flat_index, source, filled, matches)


def attention_scores(queries, all_keys, visible, kv_heads):
    tok_count = queries.shape[0]
    key_span = all_keys.shape[0]
    grouped = queries.reshape(tok_count, kv_heads, -1, HEAD)
    raw_scores = jnp.einsum(
        "ikgd,jkd->kgij",
        grouped,
        all_keys.reshape(key_span, kv_heads, HEAD),
        preferred_element_type=jnp.float32,
    )
    return jnp.where(visible, raw_scores * HEAD ** (-0.5), -1e30)


def layer_forward(current, weights, chosen, rank_rows, places, visible, owners):
    tok_count, model_width = current.shape
    head_count = weights.w_query.shape[1] // HEAD
    kv_heads = weights.w_key.shape[1] // HEAD
    exp_dev = weights.w_gate.shape[0]
    experts = exp_dev * owners
    top_count = chosen.shape[1]
    capacity = (tok_count * top_count * 9 + 8 * experts - 1) // (8 * experts)
    normed = rms_scale(current, weights.attn_gain).astype(jnp.bfloat16)
    query_lin = jnp.dot(normed, weights.w_query, preferred_element_type=jnp.float32).reshape(
        tok_count, head_count, HEAD
    )
    queries = rotate(query_lin, places).astype(jnp.bfloat16)
    key_lin = jnp.dot(normed, weights.w_key, preferred_element_type=jnp.float32).reshape(
        tok_count, kv_heads, HEAD
    )
    key_rows = rotate(key_lin, places).astype(jnp.bfloat16).reshape(tok_count, kv_heads * HEAD)
    value_rows = jnp.dot(normed, weights.w_value, preferred_element_type=jnp.float32).astype(
        jnp.bfloat16
    )
    all_keys, all_values = (
        lax.all_gather(key_rows, "expert", axis=0, tiled=True),
        lax.all_gather(value_rows, "expert", axis=0, tiled=True),
    )
    key_span = all_keys.shape[0]
    scores = attention_scores(queries, all_keys, visible, kv_heads)
    log_total = jax.nn.logsumexp(scores, axis=-1, keepdims=True)
    soft_probs = jnp.exp(scores - log_total).astype(jnp.bfloat16)
    mixed_heads = jnp.einsum(
        "kgij,jkd->ikgd",
        soft_probs,
        all_values.reshape(key_span, kv_heads, HEAD),
        preferred_element_type=jnp.float32,
    )
    joined = mixed_heads.reshape(tok_count, head_count * HEAD).astype(jnp.bfloat16)
    middle = current + jnp.dot(joined, weights.w_out, preferred_element_type=jnp.float32)
    moe_in = rms_scale(middle, weights.ffn_gain).astype(jnp.bfloat16)
    logits = jnp.dot(moe_in, weights.w_router, preferred_element_type=jnp.float32)
    pick_table, kept_pair, flat_index, source, filled, matches = route_tables(
        chosen, rank_rows, experts, capacity
    )
    selected = jnp.sum(pick_table * logits[:, None, :], axis=-1)
    gate_probs = jax.nn.softmax(selected, axis=-1)
    sent_rows = jnp.take(moe_in, source, axis=0) * filled[:, None].astype(jnp.bfloat16)
    received = lax.all_to_all(
        sent_rows.reshape(owners, exp_dev, capacity, model_width),
        "expert",
        split_axis=0,
        concat_axis=0,
        tiled=True,
    )
    gate_lin = jnp.einsum(
        "sjcd,jdf->sjcf", received, weights.w_gate, preferred_element_type=jnp.float32
    )
    up_lin = jnp.einsum(
        "sjcd,jdf->sjcf", received, weights.w_up, preferred_element_type=jnp.float32
    )
    hidden_act = (jax.nn.silu(gate_lin) * up_lin).astype(jnp.bfloat16)
    expert_out = jnp.einsum(
        "sjcf,jfd->sjcd", hidden_act, weights.w_down, preferred_element_type=jnp.float32
    ).astype(jnp.bfloat16)
    returned = lax.all_to_all(
        expert_out, "expert", split_axis=0, concat_axis=0, tiled=True
    ).reshape(experts * capacity, model_width)
    taken_rows = jnp.take(returned, flat_index.reshape(-1), axis=0).reshape(
        tok_count, top_count, model_width
    )
    weighting = gate_probs * kept_pair.astype(jnp.float32)
    mixture = jnp.sum(weighting[:, :, None] * taken_rows.astype(jnp.float32), axis=1)
    output = middle + mixture
    saved_state = SimpleNamespace(
        current=current,
        normed=normed,
        query_lin=query_lin,
        key_lin=key_lin,
        queries=queries,
        all_keys=all_keys,
        all_values=all_values,
        log_total=log_total,
        joined=joined,
        middle=middle,
        moe_in=moe_in,
        pick_table=pick_table,
        kept_pair=kept_pair,
        flat_index=flat_index,
        source=source,
        matches=matches,
        gate_probs=gate_probs,
        received=received,
        gate_lin=gate_lin,
        up_lin=up_lin,
        hidden_act=hidden_act,
        returned=returned,
    )
    return (output, saved_state)


def expert_backward(grad_after, weights, saved_state, owners):
    tok_count, model_width = grad_after.shape
    exp_dev = weights.w_gate.shape[0]
    experts = exp_dev * owners
    pick_table = saved_state.pick_table
    top_count = pick_table.shape[1]
    capacity = (tok_count * top_count * 9 + 8 * experts - 1) // (8 * experts)
    flat_index = saved_state.flat_index
    kept_float = saved_state.kept_pair.astype(jnp.float32)
    gate_probs = saved_state.gate_probs
    weighting = gate_probs * kept_float
    slot_gate = jnp.sum(
        jnp.where(saved_state.matches, weighting.reshape(-1)[:, None], 0.0), axis=0
    )
    slot_grad = (jnp.take(grad_after, saved_state.source, axis=0) * slot_gate[:, None]).astype(
        jnp.bfloat16
    )
    out_grad = lax.all_to_all(
        slot_grad.reshape(owners, exp_dev, capacity, model_width),
        "expert",
        split_axis=0,
        concat_axis=0,
        tiled=True,
    )
    taken_rows = jnp.take(saved_state.returned, flat_index.reshape(-1), axis=0).reshape(
        tok_count, top_count, model_width
    )
    weight_grad = (
        jnp.sum(taken_rows.astype(jnp.float32) * grad_after[:, None, :], axis=-1) * kept_float
    )
    select_grad = gate_probs * (
        weight_grad - jnp.sum(gate_probs * weight_grad, axis=-1, keepdims=True)
    )
    logit_grad = jnp.sum(pick_table * select_grad[:, :, None], axis=1).astype(jnp.bfloat16)
    gate_lin = saved_state.gate_lin
    up_lin = saved_state.up_lin
    received = saved_state.received
    hidden_grad = jnp.einsum(
        "sjcd,jfd->sjcf", out_grad, weights.w_down, preferred_element_type=jnp.float32
    )
    grad_down = jnp.einsum(
        "sjcf,sjcd->jdf", saved_state.hidden_act, out_grad, preferred_element_type=jnp.float32
    )
    sigmoid_gate = jax.nn.sigmoid(gate_lin)
    gate_grad = (
        hidden_grad * up_lin * sigmoid_gate * (1.0 + gate_lin * (1.0 - sigmoid_gate))
    ).astype(jnp.bfloat16)
    up_grad = (hidden_grad * gate_lin * sigmoid_gate).astype(jnp.bfloat16)
    grad_gate = jnp.einsum(
        "sjcd,sjcf->jdf", received, gate_grad, preferred_element_type=jnp.float32
    )
    grad_up = jnp.einsum("sjcd,sjcf->jdf", received, up_grad, preferred_element_type=jnp.float32)
    row_grad = jnp.einsum(
        "sjcf,jdf->sjcd", gate_grad, weights.w_gate, preferred_element_type=jnp.float32
    )
    row_grad = (
        row_grad
        + jnp.einsum("sjcf,jdf->sjcd", up_grad, weights.w_up, preferred_element_type=jnp.float32)
    ).astype(jnp.bfloat16)
    back_rows = lax.all_to_all(row_grad, "expert", split_axis=0, concat_axis=0, tiled=True).reshape(
        experts * capacity, model_width
    )
    token_grad = jnp.take(back_rows, flat_index.reshape(-1), axis=0).reshape(
        tok_count, top_count, model_width
    )
    moe_grad = jnp.sum(token_grad.astype(jnp.float32) * kept_float[:, :, None], axis=1)
    moe_grad = moe_grad + jnp.einsum(
        "te,de->td", logit_grad, weights.w_router, preferred_element_type=jnp.float32
    )
    grad_router = jnp.einsum(
        "td,te->de", saved_state.moe_in, logit_grad, preferred_element_type=jnp.float32
    )
    unused_out, ffn_pull = jax.vjp(rms_scale, saved_state.middle, weights.ffn_gain)
    middle_part, grad_ffn_gain = ffn_pull(moe_grad)
    grad_middle = grad_after + middle_part
    grads = SimpleNamespace(
        ffn_gain=grad_ffn_gain,
        w_router=grad_router,
        w_gate=grad_gate,
        w_up=grad_up,
        w_down=grad_down,
    )
    return (grad_middle, grads)


def attention_backward(grad_middle, weights, saved_state, places, visible):
    tok_count = grad_middle.shape[0]
    head_count = weights.w_query.shape[1] // HEAD
    kv_heads = weights.w_key.shape[1] // HEAD
    attn_grad = grad_middle.astype(jnp.bfloat16)
    grad_out = jnp.einsum(
        "tq,td->dq", saved_state.joined, attn_grad, preferred_element_type=jnp.float32
    )
    head_grad = jnp.einsum(
        "td,qd->tq", attn_grad, weights.w_out, preferred_element_type=jnp.float32
    ).astype(jnp.bfloat16)
    queries = saved_state.queries
    all_keys = saved_state.all_keys
    all_values = saved_state.all_values
    key_span = all_keys.shape[0]
    scores = attention_scores(queries, all_keys, visible, kv_heads)
    soft_probs = jnp.exp(scores - saved_state.log_total)
    probs_low = soft_probs.astype(jnp.bfloat16)
    grouped_grad = head_grad.reshape(tok_count, kv_heads, -1, HEAD)
    value_three = all_values.reshape(key_span, kv_heads, HEAD)
    key_three = all_keys.reshape(key_span, kv_heads, HEAD)
    prob_grad = jnp.einsum(
        "ikgd,jkd->kgij", grouped_grad, value_three, preferred_element_type=jnp.float32
    )
    value_part = jnp.einsum(
        "kgij,ikgd->jkd", probs_low, grouped_grad, preferred_element_type=jnp.float32
    )
    row_delta = jnp.sum(soft_probs * prob_grad, axis=-1, keepdims=True)
    score_grad = (soft_probs * (prob_grad - row_delta) * HEAD ** (-0.5)).astype(jnp.bfloat16)
    query_grad = jnp.einsum(
        "kgij,jkd->ikgd", score_grad, key_three, preferred_element_type=jnp.float32
    )
    key_part = jnp.einsum(
        "kgij,ikgd->jkd",
        score_grad,
        queries.reshape(tok_count, kv_heads, -1, HEAD),
        preferred_element_type=jnp.float32,
    )
    key_sum, value_sum = (
        lax.psum_scatter(
            key_part.reshape(key_span, kv_heads * HEAD).astype(jnp.bfloat16),
            "expert",
            scatter_dimension=0,
            tiled=True,
        ).astype(jnp.float32),
        lax.psum_scatter(
            value_part.reshape(key_span, kv_heads * HEAD).astype(jnp.bfloat16),
            "expert",
            scatter_dimension=0,
            tiled=True,
        ).astype(jnp.float32),
    )
    unused_query, turn_query = jax.vjp(partial(rotate, places=places), saved_state.query_lin)
    (query_back,) = turn_query(query_grad.reshape(tok_count, head_count, HEAD))
    query_low = query_back.reshape(tok_count, head_count * HEAD).astype(jnp.bfloat16)
    unused_key, turn_key = jax.vjp(partial(rotate, places=places), saved_state.key_lin)
    (key_back,) = turn_key(key_sum.reshape(tok_count, kv_heads, HEAD))
    key_low = key_back.reshape(tok_count, kv_heads * HEAD).astype(jnp.bfloat16)
    value_low = value_sum.astype(jnp.bfloat16)
    normed = saved_state.normed
    grad_query = jnp.einsum("td,tq->dq", normed, query_low, preferred_element_type=jnp.float32)
    grad_key = jnp.einsum("td,tq->dq", normed, key_low, preferred_element_type=jnp.float32)
    grad_value = jnp.einsum("td,tq->dq", normed, value_low, preferred_element_type=jnp.float32)
    normed_grad = jnp.einsum(
        "tq,dq->td", query_low, weights.w_query, preferred_element_type=jnp.float32
    )
    normed_grad = normed_grad + jnp.einsum(
        "tq,dq->td", key_low, weights.w_key, preferred_element_type=jnp.float32
    )
    normed_grad = normed_grad + jnp.einsum(
        "tq,dq->td", value_low, weights.w_value, preferred_element_type=jnp.float32
    )
    unused_attn, attn_pull = jax.vjp(rms_scale, saved_state.current, weights.attn_gain)
    current_part, grad_attn_gain = attn_pull(normed_grad)
    grad_before = grad_middle + current_part
    grads = SimpleNamespace(
        attn_gain=grad_attn_gain,
        w_query=grad_query,
        w_key=grad_key,
        w_value=grad_value,
        w_out=grad_out,
    )
    return (grad_before, grads)


def per_device(
    tokens,
    routes,
    slot_order,
    prefix,
    attn_gain,
    w_query,
    w_key,
    w_value,
    w_out,
    ffn_gain,
    w_router,
    w_gate,
    w_up,
    w_down,
    cotangent,
):
    owners = lax.axis_size("expert")
    tok_count = tokens.shape[0]
    layers = w_query.shape[0]
    key_span = tok_count * owners
    places = lax.axis_index("expert") * tok_count + jnp.arange(tok_count, dtype=jnp.int32)
    key_places = jnp.arange(key_span, dtype=jnp.int32)
    visible = (key_places[None, :] < prefix[0]) | (key_places[None, :] <= places[:, None])
    current = tokens.astype(jnp.float32)
    layer_index = 0
    weights = SimpleNamespace(
        attn_gain=attn_gain[0],
        w_query=w_query[0],
        w_key=w_key[0],
        w_value=w_value[0],
        w_out=w_out[0],
        ffn_gain=ffn_gain[0],
        w_router=w_router[0],
        w_gate=w_gate[0],
        w_up=w_up[0],
        w_down=w_down[0],
    )
    current, saved_state = layer_forward(
        current, weights, routes[layer_index], slot_order[layer_index, 0], places, visible, owners
    )
    kept_states = [saved_state]
    grad_now = cotangent
    layer_grads = [None] * layers
    for layer_index in reversed(range(layers)):
        weights = SimpleNamespace(
        attn_gain=attn_gain[0],
        w_query=w_query[0],
        w_key=w_key[0],
        w_value=w_value[0],
        w_out=w_out[0],
        ffn_gain=ffn_gain[0],
        w_router=w_router[0],
        w_gate=w_gate[0],
        w_up=w_up[0],
        w_down=w_down[0],
    )
        grad_middle, moe_grads = expert_backward(
            grad_now, weights, kept_states[layer_index], owners
        )
        expert_part = (moe_grads.w_gate, moe_grads.w_up, moe_grads.w_down)
        grad_now, attn_grads = attention_backward(
            grad_middle, weights, kept_states[layer_index], places, visible
        )
        layer_grads[layer_index] = (
            attn_grads.attn_gain,
            attn_grads.w_query,
            attn_grads.w_key,
            attn_grads.w_value,
            attn_grads.w_out,
            moe_grads.ffn_gain,
            moe_grads.w_router,
        ) + tuple(expert_part)
    gain_attn, g_query, g_key, g_value, g_out, gain_ffn, g_router, g_gate, g_up, g_down = layer_grads[0]
    low = jnp.bfloat16
    misc = jnp.concatenate([g_router, gain_attn[:, None], gain_ffn[:, None]], axis=1)
    misc = jnp.pad(misc, ((0, 0), (0, WIDE - misc.shape[1])))
    units = [g_gate.astype(low), g_up.astype(low), g_down.astype(low)]
    units += [part.astype(low)[None] for part in (
        g_query[:, :WIDE], g_query[:, WIDE:], g_key, g_value, g_out[:, :WIDE], g_out[:, WIDE:], misc
    )]
    grads = jnp.concatenate(units, axis=0).reshape(UNITS, 4, 4, 2, 32, WIDE)
    done_expert, done_shared = reduce_grads(grads)
    query_done = jnp.concatenate([done_shared[0], done_shared[1]], axis=1)[None]
    out_done = jnp.concatenate([done_shared[4], done_shared[5]], axis=1).T[None]
    rest = done_shared[6]
    experts = g_router.shape[1]
    return (
        current,
        grad_now,
        rest[:, experts][None],
        query_done,
        done_shared[2][None],
        done_shared[3][None],
        out_done,
        rest[:, experts + 1][None],
        rest[:, :experts][None],
        done_expert[0:3][None],
        done_expert[3:6][None],
        done_expert[6:9].transpose(0, 2, 1)[None],
    )


def solution(mesh):
    in_specs = (
        P(("group", "expert"), None),
        P(None, ("group", "expert"), None),
        P(None, ("group", "expert"), None),
        P("group"),
        P(),
        P(),
        P(),
        P(),
        P(),
        P(),
        P(),
        P(None, "expert", None, None),
        P(None, "expert", None, None),
        P(None, "expert", None, None),
        P(("group", "expert"), None),
    )
    out_specs = (
        P(("group", "expert"), None),
        P(("group", "expert"), None),
        P(None, ("group", "expert")),
        P(None, ("group", "expert"), None),
        P(None, ("group", "expert"), None),
        P(None, ("group", "expert"), None),
        P(None, None, ("group", "expert")),
        P(None, ("group", "expert")),
        P(None, ("group", "expert"), None),
        P(None, "expert", "group", None),
        P(None, "expert", "group", None),
        P(None, "expert", None, "group"),
    )
    return jax.shard_map(
        per_device, mesh=mesh, in_specs=in_specs, out_specs=out_specs, check_vma=False
    )
```

```python
import jax
import jax.numpy as jnp
import numpy as np
from jax import lax
from jax.experimental import pallas as pl
from jax.experimental.pallas import tpu as pltpu
from jax.sharding import PartitionSpec as P

MESH = pl.DeviceIdType.MESH
LOW = jnp.bfloat16
F32 = jnp.float32
EPS = 1e-06
CAP = 96
EXPERTS = 12
OWN_EXPERTS = 3
EXPERT_UNITS = 9
UNITS = 15
WIDE = 512
KEY_UNIT, VALUE_UNIT, QUERY_UNIT, OUT_UNIT, SPARE = 9, 10, 11, 13, 15
BIG = (4, 4, 2, 32, WIDE)
KV, COT, CODE, ROWS, BACK, DOTS, MIX, KVG = range(8)


def group_of(x_at, z_at, core):
    return x_at * 8 + z_at * 2 + core


def dot(first, second):
    return jnp.dot(first, second, preferred_element_type=F32)


def dot_nt(first, second):
    return lax.dot_general(first, second, (((1,), (1,)), ((), ())), preferred_element_type=F32)


def dot_tn(first, second):
    return lax.dot_general(first, second, (((0,), (0,)), ((), ())), preferred_element_type=F32)


def sum32(first, second):
    return (first.astype(F32) + second.astype(F32)).astype(LOW)


def lanes_of(shape):
    return lax.broadcasted_iota(jnp.int32, shape, len(shape) - 1)


def turn(values, cosine, sine, sign):
    first = lanes_of((128, 128)) % 64 < 32
    parts = []
    for at in range(values.shape[1] // 128):
        part = values[:, at * 128 : at * 128 + 128]
        swapped = jnp.where(first, pltpu.roll(part, 96, 1), pltpu.roll(part, 32, 1))
        parts.append(part * cosine + sign * (swapped * sine))
    return parts[0] if len(parts) == 1 else jnp.concatenate(parts, axis=1)


def four_heads(first, second):
    low_half = lanes_of((128, 128)) < 64
    zero = jnp.zeros((128, 128), F32)
    return jnp.concatenate(
        [
            jnp.where(low_half, first, zero),
            jnp.where(low_half, pltpu.roll(first, 64, 1), zero),
            jnp.where(low_half, zero, pltpu.roll(second, 64, 1)),
            jnp.where(low_half, zero, second),
        ],
        axis=0,
    ).astype(LOW)


def unfold_heads(stood):
    first = jnp.concatenate([stood[0:64, 0:128], stood[0:64, 128:256]], axis=0)
    second = jnp.concatenate([stood[64:128, 256:384], stood[64:128, 384:512]], axis=0)
    return first.T, second.T


def loop(count, body):
    def step(index, carry):
        body(index)
        return carry

    lax.fori_loop(0, count, step, 0)


def lane_block(index, width=128):
    return pl.ds(pl.multiple_of(index * width, width), width)


def layer_kernel(
    tokens, routes, order, prefix, attn_gain, ffn_gain, w_router,
    wq_far, wk_far, wv_far, wo_far, wg_far, wu_far, wd_far, cot_far, cos_far, sin_far,
    hidden_out, input_grad, expert_out, shared_out, misc_out,
    grads, weights, wd, router, cot, cosine, sine,
    normed, normed_t, q_low, joined, q_four, kv_all, x_all, g_all, code_all,
    x_t, g_t, probs, gates, own_dots, dots_send, dots_in, row_send, row_in, mix_in, kvg_in,
    pair_in, lo_in, hi_in, minus_in, plus_in, lo_in_b, hi_in_b, minus_in_b, plus_in_b, last, last_in,
    misc, misc_pair, misc_lo, misc_hi, misc_minus, misc_plus, misc_lo_b, misc_hi_b, misc_minus_b, misc_plus_b,
    misc_last, misc_last_in,
    y_send, y_recv, send_sem, recv_sem, local_sem,
):
    middle, own_row = hidden_out, input_grad
    group = lax.axis_index("group")
    y_at = lax.axis_index("expert")
    x_at, z_at, core = group // 8, (group // 2) % 4, group % 2
    spots = (x_at, z_at)

    def device(axis, offset):
        if axis == 0:
            return (group_of((x_at + offset) % 4, z_at, core), y_at)
        return (group_of(x_at, (z_at + offset) % 4, core), y_at)

    def across(offset):
        return (group, (y_at + offset) % 4)

    partner = (group_of(x_at, z_at, 1 - core), y_at)
    barrier = pltpu.get_barrier_semaphore()
    peers = [partner] + [device(axis, off) for axis in (0, 1) for off in (1, 3)]
    peers += [across(off) for off in (1, 2, 3)]
    for peer in peers:
        pl.semaphore_signal(barrier, inc=1, device_id=peer, device_id_type=MESH)

    half = pl.ds(0, WIDE), pl.ds(WIDE, WIDE)
    loads = {}

    def load(name, src, dst):
        copy = pltpu.make_async_copy(src, dst, local_sem.at[len(loads)])
        loads[name] = copy
        copy.start()

    def attn_loads(tag, ref, order_of):
        wk_to, wv_to, wq_to, wo_to = order_of
        load((tag, 0), wk_far, ref.at[wk_to])
        load((tag, 1), wv_far, ref.at[wv_to])
        for part in (0, 1):
            load((tag, 2 + part), wq_far.at[:, :, :, :, half[part]], ref.at[wq_to + part])
        for part in (0, 1):
            load((tag, 4 + part), wo_far.at[:, :, :, :, half[part]], ref.at[wo_to + part])

    load("cos", cos_far.at[pl.ds(y_at * 128, 128)], cosine)
    load("sin", sin_far.at[pl.ds(y_at * 128, 128)], sine)
    attn_loads("fwd", grads, (0, 1, 2, 4))
    load("cot", cot_far, cot)
    load("wg", wg_far, weights.at[pl.ds(0, 3)])
    load("wu", wu_far, weights.at[pl.ds(3, 3)])
    load("wd", wd_far, wd)

    def square(ref, unit):
        return ref[unit].reshape(1024, WIDE)

    def slab(index, rows=None):
        unit, top = QUERY_UNIT + index // 2, (index % 2) * 2
        if rows is None:
            return grads.at[unit, pl.ds(top, 2)]
        kind, at = rows
        if kind == 256:
            return grads.at[unit, top + at]
        return grads.at[unit, top + at // 2, pl.ds((at % 2) * 2, 2)]

    hidden = tokens[...].astype(F32)
    attn_r = lax.rsqrt(jnp.mean(hidden * hidden, axis=1, keepdims=True) + EPS)
    normed[...] = (hidden * attn_r * attn_gain[...]).astype(LOW)
    for name in ("cos", "sin", ("fwd", 0), ("fwd", 1)):
        loads[name].wait()
    kv_all[y_at, :, 0:WIDE] = turn(dot(normed[...], square(grads, 0)), cosine[...], sine[...], 1.0).astype(LOW)
    kv_all[y_at, :, WIDE:] = dot(normed[...], square(grads, 1)).astype(LOW)
    pl.semaphore_wait(barrier, len(peers))

    def y_copy(kind, off, src, dst):
        return pltpu.make_async_remote_copy(
            src_ref=src, dst_ref=dst, send_sem=y_send.at[kind, off - 1], recv_sem=y_recv.at[kind, off - 1],
            device_id=across(off), device_id_type=MESH,
        )

    def share(kind, ref):
        return [y_copy(kind, off, ref.at[y_at], ref.at[y_at]) for off in (2, 1, 3)]

    def start(copies):
        for copy in copies:
            copy.start()

    def wait(copies):
        for copy in copies:
            copy.wait()

    kv_share = share(KV, kv_all)
    start(kv_share)

    for part in (0, 1):
        loads[("fwd", 2 + part)].wait()
        turned = turn(dot(normed[...], square(grads, 2 + part)), cosine[...], sine[...], 1.0)
        turned = turned.astype(LOW).astype(F32)
        for c in (0, 1):
            q_four[part * 2 + c] = four_heads(
                turned[:, c * 256 : c * 256 + 128], turned[:, c * 256 + 128 : c * 256 + 256]
            )

    lane = lanes_of((128, 128))
    member = jnp.zeros((128, 128), F32)
    for pick in range(routes.shape[1]):
        member = member + jnp.where(routes[:, pick : pick + 1] == lane, 1.0, 0.0)
    ranks = jnp.broadcast_to(order[...].astype(F32), (128, 128))
    earlier = jnp.where(ranks < ranks.T, 1.0, 0.0).astype(LOW)
    before = dot(earlier, member.astype(LOW))
    code_all[y_at] = jnp.where((member > 0.5) & (before < CAP - 0.5), 2.0, member).astype(LOW)
    loads["cot"].wait()
    g_all[y_at] = cot[...].astype(LOW)
    router[...] = jnp.zeros_like(router)
    router[:, 0:EXPERTS] = w_router[...]
    normed_t[...] = normed[...].T

    wait(kv_share)
    code_share = share(CODE, code_all)
    g_share = share(COT, g_all)
    start(code_share)
    start(g_share)

    def visible():
        shape = (512, 512)
        key_at = lax.broadcasted_iota(jnp.int32, shape, 0)
        query_at = y_at * 128 + lanes_of(shape) % 128
        return (key_at < prefix[0]) | (key_at <= query_at)

    def key_block(c):
        return kv_all[:, :, lane_block(c)].reshape(512, 128)

    def value_block(c):
        return kv_all[:, :, lane_block(c + 4)].reshape(512, 128)

    def prob_ref(c):
        return grads.at[KEY_UNIT + c // 2, pl.ds((c % 2) * 2, 2)]

    def attend(c):
        scores = jnp.where(visible(), dot_nt(key_block(c), q_four[c]) * 0.125, -1e30)
        raised = jnp.exp(scores - jnp.max(scores, axis=0, keepdims=True))
        soft = (raised * (1.0 / jnp.sum(raised, axis=0, keepdims=True))).astype(LOW)
        prob_ref(c)[...] = soft.reshape(2, 4, 2, 32, WIDE)
        first, second = unfold_heads(dot_tn(value_block(c), soft))
        joined[:, lane_block(2 * c)] = first.astype(LOW)
        joined[:, lane_block(2 * c + 1)] = second.astype(LOW)

    loop(4, attend)
    loads[("fwd", 4)].wait()
    loads[("fwd", 5)].wait()
    for part in (0, 1):
        middle[:, half[part]] = tokens[:, half[part]].astype(F32) + dot(joined[...], square(grads, 4 + part))
    ffn_r = lax.rsqrt(jnp.mean(middle[...] * middle[...], axis=1, keepdims=True) + EPS)
    x_all[y_at] = (middle[...] * ffn_r * ffn_gain[...]).astype(LOW)
    x_share = share(ROWS, x_all)
    start(x_share)

    wait(code_share)
    wait(g_share)

    def stand(ref, out):
        def body(block):
            out[:, lane_block(block)] = ref[block].T

        loop(4, body)

    stand(g_all, g_t)
    wait(x_share)
    stand(x_all, x_t)

    code = code_all[...].reshape(512, 128).astype(F32)
    in_use = code > 0.5
    logits = jnp.where(in_use, dot(x_all[...].reshape(512, 1024), router[...]), -1e30)
    raised = jnp.where(in_use, jnp.exp(logits - jnp.max(logits, axis=1, keepdims=True)), 0.0)
    soft = raised / jnp.sum(raised, axis=1, keepdims=True)
    probs[...] = soft.reshape(4, 128, 128)
    gates[...] = jnp.where(code > 1.5, soft, 0.0)
    own_dots[...] = jnp.zeros_like(own_dots)
    for name in ("wg", "wu", "wd"):
        loads[name].wait()

    def expert_step(step):
        j, part = step // 2, step % 2
        rows = pl.ds(pl.multiple_of(part * 256, 256), 256)
        blocks = pl.ds(part * 2, 2)
        here = lanes_of((256, 128)) == y_at * OWN_EXPERTS + j
        gate_of = jnp.sum(jnp.where(here, gates[rows, :], 0.0), axis=1, keepdims=True)
        inputs = x_all[blocks].reshape(256, 1024)
        gate_lin = dot(inputs, square(weights, j))
        up_lin = dot(inputs, square(weights, 3 + j))
        outer = dot_nt(g_all[blocks].reshape(256, 1024), wd[j])
        sig = 1.0 / (1.0 + jnp.exp(-gate_lin))
        silu = gate_lin * sig
        act = (silu * up_lin).astype(LOW).astype(F32)
        taken = jnp.where(gate_of > 0.0, jnp.sum(act * outer, axis=1, keepdims=True), 0.0)
        own_dots[rows, :] = jnp.where(here, taken, own_dots[rows, :])
        outer = outer * gate_of
        shape = (4, 2, 32, WIDE)
        slab(6 + j, (256, part))[...] = (act * gate_of).astype(LOW).reshape(shape)
        slab(j, (256, part))[...] = (outer * up_lin * sig * (1.0 + gate_lin * (1.0 - sig))).astype(LOW).reshape(shape)
        slab(3 + j, (256, part))[...] = (outer * silu).astype(LOW).reshape(shape)

    loop(6, expert_step)

    def dots_copy(off):
        return y_copy(DOTS, off, dots_send.at[(y_at + off) % 4], dots_in.at[off - 1])

    def back_copy(off):
        return y_copy(BACK, off, row_send.at[(y_at + off) % 4], row_in.at[off - 1])

    for block in range(4):
        dots_send[block] = own_dots[block * 128 : block * 128 + 128, :].T[0:16, :]
    for off in (2, 1, 3):
        dots_copy(off).start()

    def row_part(block):
        total = None
        for j in range(OWN_EXPERTS):
            for kind in (0, 3):
                lin = slab(kind + j, (128, block))[...].reshape(128, WIDE)
                part = dot_nt(lin, square(weights, kind + j))
                total = part if total is None else total + part
        return total

    for off in (2, 1, 3):
        row_send[(y_at + off) % 4] = row_part((y_at + off) % 4).astype(LOW)
        back_copy(off).start()
    own_row[...] = row_part(y_at)
    attn_loads("bwd", weights, (2, 5, 0, 3))

    class Wide:
        src, pair, lo, hi, minus, plus = grads, pair_in, lo_in, hi_in, minus_in, plus_in
        lo_b, hi_b, minus_b, plus_b = lo_in_b, hi_in_b, minus_in_b, plus_in_b

    class Narrow:
        src, pair, lo, hi, minus, plus = misc, misc_pair, misc_lo, misc_hi, misc_minus, misc_plus
        lo_b, hi_b, minus_b, plus_b = misc_lo_b, misc_hi_b, misc_minus_b, misc_plus_b

    def remote(unit, kind, src, dst, target):
        return pltpu.make_async_remote_copy(
            src_ref=src, dst_ref=dst, send_sem=send_sem.at[kind, unit], recv_sem=recv_sem.at[kind, unit],
            device_id=target, device_id_type=MESH,
        )

    class Unit:
        def __init__(self, unit):
            self.unit = unit
            self.set = Wide if unit < UNITS else Narrow
            self.at = unit if unit < UNITS else 0
            self.axis = unit % 2

        def block(self, axis, index):
            ref = self.set.src.at[self.at]
            return ref.at[index, :, core] if axis == 0 else ref.at[:, index, core]

        def cell(self, index):
            ref = self.set.src.at[self.at]
            return ref.at[x_at, index, core] if self.axis == 0 else ref.at[index, z_at, core]

        def pair_copy(self):
            s = self.set
            return remote(self.unit, 0, s.src.at[self.at, :, :, 1 - core], s.pair.at[self.at], partner)

        def far_copy(self, way):
            s = self.set
            src = self.block(self.axis, (spots[self.axis] + 2) % 4).at[pl.ds(2 * way, 2)]
            dst = (s.lo, s.hi)[way].at[self.at]
            return remote(self.unit, 1 + way, src, dst, device(self.axis, (1, 3)[way]))

        def near_copy(self, way):
            s = self.set
            src = self.block(self.axis, (spots[self.axis] + (1, 3)[way]) % 4)
            dst = (s.minus, s.plus)[way].at[self.at]
            return remote(self.unit, 3 + way, src, dst, device(self.axis, (1, 3)[way]))

        def far_copy_b(self, way):
            s = self.set
            src = self.cell((spots[1 - self.axis] + 2) % 4).at[pl.ds(16 * way, 16)]
            dst = (s.lo_b, s.hi_b)[way].at[self.at]
            return remote(self.unit, 5 + way, src, dst, device(1 - self.axis, (1, 3)[way]))

        def near_copy_b(self, way):
            s = self.set
            src = self.cell((spots[1 - self.axis] + (1, 3)[way]) % 4)
            dst = (s.minus_b, s.plus_b)[way].at[self.at]
            return remote(self.unit, 7 + way, src, dst, device(1 - self.axis, (1, 3)[way]))

        def across_copy(self, off):
            to = (y_at + off) % 4
            src, dst, at = (last, last_in, self.at - EXPERT_UNITS) if self.set is Wide else (misc_last, misc_last_in, 0)
            return remote(self.unit, 8 + off, src.at[at, pl.ds(to * 8, 8)], dst.at[off - 1, at], across(off))

        def begin(self):
            self.pair_copy().start()

        def after_pair(self):
            s = self.set
            self.pair_copy().wait()
            for slab_at in range(4):
                ref = s.src.at[self.at, slab_at, :, core]
                ref[...] = sum32(ref[...], s.pair[self.at, slab_at])
            self.far_copy(0).start()
            self.far_copy(1).start()

        def after_far(self):
            s = self.set
            for way in (0, 1):
                self.far_copy(way).wait()
                ref = self.block(self.axis, (spots[self.axis] + (1, 3)[way]) % 4).at[pl.ds(2 * way, 2)]
                ref[...] = sum32(ref[...], (s.lo, s.hi)[way][self.at])
                self.near_copy(way).start()

        def after_near(self):
            s = self.set
            for way in (0, 1):
                self.near_copy(way).wait()
            ref = self.block(self.axis, spots[self.axis])
            total = ref[...].astype(F32) + s.minus[self.at].astype(F32)
            ref[...] = (total + s.plus[self.at].astype(F32)).astype(LOW)
            for way in (0, 1):
                self.far_copy_b(way).start()

        def after_far_b(self):
            s = self.set
            for way in (0, 1):
                self.far_copy_b(way).wait()
                ref = self.cell((spots[1 - self.axis] + (1, 3)[way]) % 4).at[pl.ds(16 * way, 16)]
                ref[...] = sum32(ref[...], (s.lo_b, s.hi_b)[way][self.at])
                self.near_copy_b(way).start()

        def after_near_b(self):
            s = self.set
            for way in (0, 1):
                self.near_copy_b(way).wait()
            total = self.cell(spots[1 - self.axis])[...].astype(F32) + s.minus_b[self.at].astype(F32)
            total = total + s.plus_b[self.at].astype(F32)
            if self.unit < EXPERT_UNITS:
                expert_out[self.unit] = total
                return
            if self.set is Wide:
                last[self.at - EXPERT_UNITS] = total
            else:
                misc_last[0] = total
            for off in (1, 2, 3):
                self.across_copy(off).start()

        def finish(self):
            for off in (1, 2, 3):
                self.across_copy(off).wait()
            src, dst, at = (last, last_in, self.at - EXPERT_UNITS) if self.set is Wide else (misc_last, misc_last_in, 0)
            total = src[at, pl.ds(pl.multiple_of(y_at * 8, 8), 8), :]
            for off in (1, 2, 3):
                total = total + dst[off - 1, at]
            if self.set is Wide:
                shared_out[at] = total
            else:
                misc_out[...] = total

    STAGES = ("after_pair", "after_far", "after_near", "after_far_b", "after_near_b", "finish")
    units = [Unit(unit) for unit in range(UNITS + 1)]

    def run(stage, *which):
        for unit in which:
            getattr(units[unit], STAGES[stage])()

    def weight_grad(unit, left, right):
        value = right()

        def body(tile):
            rows = pl.ds(pl.multiple_of(tile * 256, 256), 256)
            grads[unit, tile] = dot(left[rows, :], value).astype(LOW).reshape(4, 2, 32, WIDE)

        loop(4, body)
        units[unit].begin()

    def slab_value(index):
        return lambda: slab(index)[...].reshape(512, WIDE)

    before_unit = None
    for j in range(OWN_EXPERTS):
        for kind, left in ((0, x_t), (3, x_t), (6, g_t)):
            weight_grad(kind + j, left, slab_value(kind + j))
            if before_unit is not None:
                run(0, before_unit)
            before_unit = kind + j
    run(0, before_unit)
    run(1, 0, 3, 6, 1)

    def mix_part(block):
        total = None
        for j in range(OWN_EXPERTS):
            part = dot(slab(6 + j, (128, block))[...].reshape(128, WIDE), wd[j])
            total = part if total is None else total + part
        x_all[block] = total.astype(LOW)

    loop(4, mix_part)
    run(1, 4, 7)

    for off in (1, 2, 3):
        dots_copy(off).wait()
        back_copy(off).wait()

    def mix_copy(off):
        return y_copy(MIX, off, x_all.at[(y_at + off) % 4], mix_in.at[off - 1])

    for off in (2, 1, 3):
        mix_copy(off).start()
    taken = dots_send[y_at]
    moe_grad = own_row[...]
    for off in (1, 2, 3):
        taken = taken + dots_in[off - 1]
        moe_grad = moe_grad + row_in[off - 1].astype(F32)
    taken = jnp.concatenate([taken, jnp.zeros((112, 128), F32)], axis=0).T
    own_probs = probs[y_at]
    select = own_probs * (taken - jnp.sum(own_probs * taken, axis=1, keepdims=True))
    select = select.astype(LOW)
    moe_grad = moe_grad + dot_nt(select, router[...])
    router_grad = dot(x_t[:, lane_block(y_at)], select)
    normal = middle[...]
    ffn_r = lax.rsqrt(jnp.mean(normal * normal, axis=1, keepdims=True) + EPS)
    scaled = moe_grad * ffn_gain[...]
    ffn_gain_grad = jnp.sum(moe_grad * normal * ffn_r, axis=0, keepdims=True)
    shrink = ffn_r * ffn_r * ffn_r * jnp.mean(scaled * normal, axis=1, keepdims=True)
    cot[...] = cot[...] + ffn_r * scaled - normal * shrink
    attn_grad = cot[...].astype(LOW)
    for part in (0, 1):
        loads[("bwd", 4 + part)].wait()
    head_grad = dot_nt(attn_grad[:, 0:WIDE], square(weights, 3)) + dot_nt(attn_grad[:, WIDE:], square(weights, 4))
    head_low = head_grad.astype(LOW).astype(F32)
    for c in range(4):
        q_four[4 + c] = four_heads(head_low[:, c * 256 : c * 256 + 128], head_low[:, c * 256 + 128 : c * 256 + 256])
    x_t[:, 0:128] = attn_grad.T

    key_sums, value_sums = pair_in.at[0], pair_in.at[3]

    def attend_back(c):
        heads = q_four[4 + c]
        low = prob_ref(c)[...].reshape(512, 512)
        soft = low.astype(F32)
        weighted = soft * dot_nt(value_block(c), heads)
        sums = jnp.sum(weighted, axis=0, keepdims=True)
        score_grad = ((weighted - soft * sums) * 0.125).astype(LOW)
        value_sums[:, :, :, lane_block(c)] = dot(low, heads).astype(LOW).reshape(4, 4, 32, 128)
        key_sums[:, :, :, lane_block(c)] = dot(score_grad, q_four[c]).astype(LOW).reshape(4, 4, 32, 128)
        first, second = unfold_heads(dot_tn(key_block(c), score_grad))
        q_low[:, lane_block(2 * c)] = turn(first, cosine[...], sine[...], -1.0).astype(LOW)
        q_low[:, lane_block(2 * c + 1)] = turn(second, cosine[...], sine[...], -1.0).astype(LOW)

    loop(4, attend_back)

    def kvg_copies(off):
        to = (y_at + off) % 4
        return [
            pltpu.make_async_remote_copy(
                src_ref=src.at[to], dst_ref=kvg_in.at[off - 1, kind], send_sem=y_send.at[KVG + kind, off - 1],
                recv_sem=y_recv.at[KVG + kind, off - 1], device_id=across(off), device_id_type=MESH,
            )
            for kind, src in ((0, key_sums), (1, value_sums))
        ]

    for off in (2, 1, 3):
        start(kvg_copies(off))

    run(1, 2, 5, 8)
    run(2, 0, 3, 6)
    for part in (0, 1):
        weight_grad(OUT_UNIT + part, x_t.at[:, pl.ds(0, 128)], lambda: joined[:, half[part]])
    run(2, 1, 4)
    for part in (0, 1):
        weight_grad(QUERY_UNIT + part, normed_t, lambda: q_low[:, half[part]])
    run(0, OUT_UNIT, OUT_UNIT + 1, QUERY_UNIT, QUERY_UNIT + 1)
    run(2, 7, 2, 5, 8)
    for part in (0, 1, 2, 3):
        loads[("bwd", part)].wait()
    normed_grad = dot_nt(q_low[:, 0:WIDE], square(weights, 0)) + dot_nt(q_low[:, WIDE:], square(weights, 1))
    input_grad[...] = normed_grad
    for off in (1, 2, 3):
        mix_copy(off).wait()
    total = middle[...] + x_all[y_at].astype(F32)
    for off in (1, 2, 3):
        total = total + mix_in[off - 1].astype(F32)
    hidden_out[...] = total
    run(1, OUT_UNIT, OUT_UNIT + 1)
    run(3, 0, 3, 6, 1, 4)

    for off in (1, 2, 3):
        wait(kvg_copies(off))
    key_back, value_back = key_sums[y_at].reshape(128, WIDE).astype(F32), value_sums[y_at].reshape(128, WIDE).astype(F32)
    for off in (1, 2, 3):
        key_back = key_back + kvg_in[off - 1, 0].reshape(128, WIDE).astype(F32)
        value_back = value_back + kvg_in[off - 1, 1].reshape(128, WIDE).astype(F32)
    q_low[:, half[0]] = turn(key_back, cosine[...], sine[...], -1.0).astype(LOW)
    q_low[:, half[1]] = value_back.astype(LOW)
    weight_grad(KEY_UNIT, normed_t, lambda: q_low[:, half[0]])
    weight_grad(VALUE_UNIT, normed_t, lambda: q_low[:, half[1]])
    normed_grad = input_grad[...] + dot_nt(q_low[:, 0:WIDE], square(weights, 2))
    normed_grad = normed_grad + dot_nt(q_low[:, WIDE:], square(weights, 5))
    hidden = tokens[...].astype(F32)
    attn_r = lax.rsqrt(jnp.mean(hidden * hidden, axis=1, keepdims=True) + EPS)
    scaled = normed_grad * attn_gain[...]
    attn_gain_grad = jnp.sum(normed_grad * hidden * attn_r, axis=0, keepdims=True)
    shrink = attn_r * attn_r * attn_r * jnp.mean(scaled * hidden, axis=1, keepdims=True)
    input_grad[...] = cot[...] + attn_r * scaled - hidden * shrink
    wide_lane = lanes_of((1024, 128))
    gains = jnp.where(
        wide_lane == EXPERTS,
        jnp.broadcast_to(attn_gain_grad, (128, 1024)).T,
        jnp.broadcast_to(ffn_gain_grad, (128, 1024)).T,
    )
    misc[0] = jnp.where(wide_lane < EXPERTS, router_grad, gains).astype(LOW).reshape(4, 4, 2, 32, 128)
    units[UNITS].begin()

    rest = (OUT_UNIT, OUT_UNIT + 1, QUERY_UNIT, QUERY_UNIT + 1, KEY_UNIT, VALUE_UNIT, UNITS)
    run(0, KEY_UNIT, VALUE_UNIT, UNITS)
    run(1, QUERY_UNIT, QUERY_UNIT + 1)
    run(2, OUT_UNIT, OUT_UNIT + 1)
    run(1, KEY_UNIT, VALUE_UNIT, UNITS)
    run(3, 7, 2, 5, 8)
    run(4, 0, 3, 6, 1, 4, 7, 2, 5, 8)
    run(3, OUT_UNIT, OUT_UNIT + 1)
    run(2, QUERY_UNIT, QUERY_UNIT + 1, KEY_UNIT, VALUE_UNIT, UNITS)
    run(4, OUT_UNIT, OUT_UNIT + 1)
    run(3, QUERY_UNIT, QUERY_UNIT + 1, KEY_UNIT, VALUE_UNIT, UNITS)
    run(4, QUERY_UNIT, QUERY_UNIT + 1, KEY_UNIT, VALUE_UNIT, UNITS)
    run(5, *rest)


def layer(*args):
    vmem = pl.BlockSpec(memory_space=pltpu.VMEM)
    smem = pl.BlockSpec(memory_space=pltpu.SMEM)
    far = pl.BlockSpec(memory_space=pl.ANY)
    low = lambda *shape: pltpu.VMEM(shape, LOW)
    wide = lambda *shape: pltpu.VMEM(shape, F32)
    sems = pltpu.SemaphoreType.DMA
    scratch = [
        low(UNITS + 1, *BIG), low(6, *BIG), low(3, 512, 1024), low(1024, 128), wide(128, 1024), wide(128, 128), wide(128, 128),
        low(128, 1024), low(1024, 128), low(128, 1024), low(128, 1024), low(8, 512, 128),
        low(4, 128, 1024), low(4, 128, 1024), low(4, 128, 1024), low(4, 128, 128),
        low(1024, 512), low(1024, 512), wide(4, 128, 128), wide(512, 128), wide(512, 128),
        wide(4, 16, 128), wide(3, 16, 128), low(4, 128, 1024), low(3, 128, 1024),
        low(3, 128, 1024), low(3, 2, 4, 32, WIDE),
    ]
    for count, width in ((UNITS, WIDE), (1, 128)):
        if count == 1:
            scratch += [low(1, 4, 4, 2, 32, width)]
        scratch += [low(count, 4, 4, 32, width), low(count, 2, 32, width), low(count, 2, 32, width)]
        scratch += [low(count, 4, 32, width), low(count, 4, 32, width)]
        scratch += [low(count, 16, width), low(count, 16, width), low(count, 32, width), low(count, 32, width)]
        shared = count - EXPERT_UNITS if count == UNITS else 1
        scratch += [wide(shared, 32, width), wide(3, shared, 8, width)]
    scratch += [sems((9, 3)), sems((9, 3)), sems((12, UNITS + 1)), sems((12, UNITS + 1)), sems((20,))]
    shape = jax.ShapeDtypeStruct
    return pl.pallas_call(
        layer_kernel,
        out_shape=(
            shape((128, 1024), F32),
            shape((128, 1024), F32),
            shape((EXPERT_UNITS, 32, WIDE), F32),
            shape((UNITS - EXPERT_UNITS, 8, WIDE), F32),
            shape((8, 128), F32),
        ),
        in_specs=[vmem, vmem, vmem, smem, vmem, vmem, vmem] + [far] * 10,
        out_specs=(vmem,) * 5,
        scratch_shapes=scratch,
        compiler_params=pltpu.CompilerParams(
            collective_id=0, has_side_effects=True, vmem_limit_bytes=60 * 2**20
        ),
        name="layer",
    )(*args)


def rope_tables(length):
    inverse = np.float32(10000.0) ** (-np.arange(32, dtype=np.float32) / np.float32(32))
    angles = np.arange(length, dtype=np.float32)[:, None] * inverse[None, :]
    cosine, sine = np.cos(angles), np.sin(angles)
    return np.tile(cosine, (1, 4)), np.concatenate([-sine, sine, -sine, sine], axis=1)


def per_device(
    tokens, routes, slot_order, prefix, attn_gain, w_query, w_key, w_value, w_out, ffn_gain, w_router,
    w_gate, w_up, w_down, cotangent,
):
    cosine, sine = rope_tables(512)
    hidden_out, input_grad, expert_done, shared, misc = layer(
        tokens, routes[0], slot_order[0], prefix, attn_gain, ffn_gain, w_router[0],
        w_query.reshape(4, 4, 2, 32, 1024), w_key.reshape(BIG), w_value.reshape(BIG), w_out.reshape(4, 4, 2, 32, 1024),
        w_gate.reshape(3, *BIG), w_up.reshape(3, *BIG), w_down[0], cotangent, jnp.asarray(cosine), jnp.asarray(sine),
    )
    at = lambda unit: unit - EXPERT_UNITS
    return (
        hidden_out,
        input_grad,
        misc[:, EXPERTS][None],
        jnp.concatenate([shared[at(QUERY_UNIT)], shared[at(QUERY_UNIT + 1)]], axis=1)[None],
        shared[at(KEY_UNIT)][None],
        shared[at(VALUE_UNIT)][None],
        jnp.concatenate([shared[at(OUT_UNIT)], shared[at(OUT_UNIT + 1)]], axis=1).T[None],
        misc[:, EXPERTS + 1][None],
        misc[:, :EXPERTS][None],
        expert_done[0:3][None],
        expert_done[3:6][None],
        expert_done[6:9].transpose(0, 2, 1)[None],
    )


def solution(mesh):
    both = ("group", "expert")
    in_specs = (
        P(both, None), P(None, both, None), P(None, both, None), P("group"), P(), P(), P(), P(), P(), P(), P(),
        P(None, "expert", None, None), P(None, "expert", None, None), P(None, "expert", None, None), P(both, None),
    )
    out_specs = (
        P(both, None), P(both, None), P(None, both), P(None, both, None), P(None, both, None), P(None, both, None),
        P(None, None, both), P(None, both), P(None, both, None), P(None, "expert", "group", None),
        P(None, "expert", "group", None), P(None, "expert", None, "group"),
    )
    return jax.shard_map(per_device, mesh=mesh, in_specs=in_specs, out_specs=out_specs, check_vma=False)
```

```python
import jax
import jax.numpy as jnp
import numpy as np
from jax import lax
from jax.experimental import pallas as pl
from jax.experimental.pallas import tpu as pltpu
from jax.sharding import PartitionSpec as P

MESH = pl.DeviceIdType.MESH
LOW = jnp.bfloat16
F32 = jnp.float32
EPS = 1e-06
CAP = 96
EXPERTS = 12
OWN_EXPERTS = 3
EXPERT_UNITS = 9
UNITS = 15
WIDE = 512
KEY_UNIT, VALUE_UNIT, QUERY_UNIT, OUT_UNIT, SPARE = 9, 10, 11, 13, 15
BIG = (4, 4, 2, 32, WIDE)


def group_of(x_at, z_at, core):
    return x_at * 8 + z_at * 2 + core


def dot(first, second):
    return jnp.dot(first, second, preferred_element_type=F32)


def dot_nt(first, second):
    return lax.dot_general(first, second, (((1,), (1,)), ((), ())), preferred_element_type=F32)


def dot_tn(first, second):
    return lax.dot_general(first, second, (((0,), (0,)), ((), ())), preferred_element_type=F32)


def sum32(first, second):
    return (first.astype(F32) + second.astype(F32)).astype(LOW)


def lanes_of(shape):
    return lax.broadcasted_iota(jnp.int32, shape, len(shape) - 1)


def turn(values, cosine, sine, sign):
    first = lanes_of((values.shape[0], 128)) % 64 < 32
    parts = []
    for at in range(values.shape[1] // 128):
        part = values[:, at * 128 : at * 128 + 128]
        swapped = jnp.where(first, pltpu.roll(part, 96, 1), pltpu.roll(part, 32, 1))
        parts.append(part * cosine + sign * (swapped * sine))
    return parts[0] if len(parts) == 1 else jnp.concatenate(parts, axis=1)


def four_heads(first, second):
    low_half = lanes_of((128, 128)) < 64
    zero = jnp.zeros((128, 128), F32)
    return jnp.concatenate(
        [
            jnp.where(low_half, first, zero),
            jnp.where(low_half, pltpu.roll(first, 64, 1), zero),
            jnp.where(low_half, zero, pltpu.roll(second, 64, 1)),
            jnp.where(low_half, zero, second),
        ],
        axis=0,
    ).astype(LOW)


def unfold_heads(stood):
    first = jnp.concatenate([stood[0:64, 0:128], stood[0:64, 128:256]], axis=0)
    second = jnp.concatenate([stood[64:128, 256:384], stood[64:128, 384:512]], axis=0)
    return first.T, second.T


def loop(count, body):
    def step(index, carry):
        body(index)
        return carry

    lax.fori_loop(0, count, step, 0)


def lane_block(index, width=128):
    return pl.ds(pl.multiple_of(index * width, width), width)


def layer_kernel(
    tokens, routes, order, prefix, attn_gain, ffn_gain, w_router,
    wq_far, wk_far, wv_far, wo_far, wg_far, wu_far, wd_far, cot_far, cos_far, sin_far,
    hidden_out, input_grad, expert_out, shared_out, misc_out,
    grads, weights, wd, router, cot, cosine, sine,
    normed_all, joined, q_four, kv_all, x_all, g_all, code_all,
    x_t, g_t, probs, gates, own_dots, dots_send, dots_in, row_send, row_in, mix_in, kvg_in,
    pair_in, lo_in, hi_in, minus_in, plus_in, lo_in_b, hi_in_b, minus_in_b, plus_in_b, last, last_in,
    misc, misc_pair, misc_lo, misc_hi, misc_minus, misc_plus, misc_lo_b, misc_hi_b, misc_minus_b, misc_plus_b,
    misc_last, misc_last_in,
    y_send, y_recv, send_sem, recv_sem, local_sem,
):
    group = lax.axis_index("group")
    y_at = lax.axis_index("expert")
    x_at, z_at, core = group // 8, (group // 2) % 4, group % 2
    spots = (x_at, z_at)
    own_rows = pl.ds(pl.multiple_of(y_at * 128, 128), 128)
    middle, own_row, q_low, normed_t = hidden_out, input_grad, normed_all.at[y_at], g_t

    def device(axis, offset):
        if axis == 0:
            return (group_of((x_at + offset) % 4, z_at, core), y_at)
        return (group_of(x_at, (z_at + offset) % 4, core), y_at)

    def across(offset):
        return (group, (y_at + offset) % 4)

    partner = (group_of(x_at, z_at, 1 - core), y_at)
    barrier = pltpu.get_barrier_semaphore()
    peers = [partner] + [device(axis, off) for axis in (0, 1) for off in (1, 3)]
    peers += [across(off) for off in (1, 2, 3)]
    for peer in peers:
        pl.semaphore_signal(barrier, inc=1, device_id=peer, device_id_type=MESH)

    half = pl.ds(0, WIDE), pl.ds(WIDE, WIDE)
    loads = {}

    def load(name, src, dst):
        copy = pltpu.make_async_copy(src, dst, local_sem.at[len(loads)])
        loads[name] = copy
        copy.start()

    def load_keys(tag, ref, wk_to, wv_to):
        load((tag, 0), wk_far, ref.at[wk_to])
        load((tag, 1), wv_far, ref.at[wv_to])

    def load_pair(tag, at, src, ref, to):
        for part in (0, 1):
            load((tag, at + part), src.at[:, :, :, :, half[part]], ref.at[to + part])

    load_pair("fwd", 2, wq_far, grads, 2)
    load("cos", cos_far, cosine)
    load("sin", sin_far, sine)
    load_keys("fwd", grads, 0, 1)

    def square(ref, unit):
        return ref[unit].reshape(1024, WIDE)

    def slab(index, rows=None):
        unit, top = QUERY_UNIT + index // 2, (index % 2) * 2
        if rows is None:
            return grads.at[unit, pl.ds(top, 2)]
        kind, at = rows
        if kind == 256:
            return grads.at[unit, top + at]
        return grads.at[unit, top + at // 2, pl.ds((at % 2) * 2, 2)]

    hidden = tokens[...].astype(F32)
    attn_r = lax.rsqrt(jnp.mean(hidden * hidden, axis=1, keepdims=True) + EPS)
    normed_all[y_at] = (hidden * attn_r * attn_gain[...]).astype(LOW)
    pl.semaphore_wait(barrier, len(peers))

    y_used = []

    def y_copy(off, src, dst):
        at = len(y_used)
        y_used.append(off)
        return pltpu.make_async_remote_copy(
            src_ref=src, dst_ref=dst, send_sem=y_send.at[at], recv_sem=y_recv.at[at],
            device_id=across(off), device_id_type=MESH,
        )

    def start(copies):
        for copy in copies:
            copy.start()

    def wait(copies):
        for copy in copies:
            copy.wait()

    left, right = (y_at + 3) % 4, (y_at + 1) % 4
    low_rows, high_rows = pl.ds(0, 64), pl.ds(64, 64)

    class Gather:
        def __init__(self, ref):
            def pass_on(block, rows, off):
                return y_copy(off, ref.at[block, rows], ref.at[block, rows])

            self.first = [pass_on(y_at, low_rows, 1), pass_on(y_at, high_rows, 3)]
            self.first += [pass_on(y_at, high_rows, 1), pass_on(y_at, low_rows, 3)]
            self.second = [pass_on(left, low_rows, 1), pass_on(right, high_rows, 3)]

        def start(self):
            start(self.first)

        def forward(self):
            for came, on in zip(self.first, self.second):
                came.wait_recv()
                on.start()

        def finish(self):
            for copy in self.first[2:]:
                copy.wait_recv()
            for copy in self.first:
                copy.wait_send()
            wait(self.second)

    class Scatter:
        def __init__(self, block, land):
            self.block, self.land = block, land
            far = (y_at + 2) % 4
            self.far = [y_copy(1, block(far, 0), land(0, 0)), y_copy(3, block(far, 1), land(0, 1))]
            self.near = [y_copy(1, block(right, 1), land(1, 1)), y_copy(3, block(left, 0), land(2, 0))]
            self.last = [y_copy(1, block(right, 0), land(1, 0)), y_copy(3, block(left, 1), land(2, 1))]

        def start(self):
            start(self.far)
            start(self.near)

        def turn(self):
            for part, to in ((0, right), (1, left)):
                self.far[part].wait()
                ref = self.block(to, part)
                ref[...] = sum32(ref[...], self.land(0, part)[...])
                self.last[part].start()

        def finish(self):
            wait(self.near)
            wait(self.last)

    normed_share = Gather(normed_all)
    normed_share.start()
    load_pair("fwd", 4, wo_far, grads, 4)
    load("cot", cot_far, cot)
    load("wg", wg_far, weights.at[pl.ds(0, 3)])
    load("wu", wu_far, weights.at[pl.ds(3, 3)])
    load("wd", wd_far, wd)

    for name in ("cos", "sin"):
        loads[name].wait()
    for part in (0, 1):
        loads[("fwd", 2 + part)].wait()
        turned = turn(dot(normed_all[y_at], square(grads, 2 + part)), cosine[own_rows, :], sine[own_rows, :], 1.0)
        turned = turned.astype(LOW).astype(F32)
        for c in (0, 1):
            q_four[part * 2 + c] = four_heads(
                turned[:, c * 256 : c * 256 + 128], turned[:, c * 256 + 128 : c * 256 + 256]
            )

    expert_at = lax.broadcasted_iota(jnp.int32, (128, 128), 0)
    member = jnp.zeros((128, 128), F32)
    for pick in range(routes.shape[0]):
        member = member + jnp.where(routes[pick : pick + 1, :] == expert_at, 1.0, 0.0)
    member = member.T
    ranks = jnp.broadcast_to(order[...].astype(F32), (128, 128))
    earlier = jnp.where(ranks < ranks.T, 1.0, 0.0).astype(LOW)
    before = dot(earlier, member.astype(LOW))
    code_all[y_at] = jnp.where((member > 0.5) & (before < CAP - 0.5), 2.0, member).astype(LOW)
    loads["cot"].wait()
    g_all[y_at] = cot[...].astype(LOW)
    router[...] = jnp.zeros_like(router)
    router[0:EXPERTS, :] = w_router[...]
    for part in (0, 1):
        loads[("fwd", part)].wait()
    normed_share.forward()
    normed_share.finish()

    def keys_values(part):
        lanes = lane_block(part, 256)
        inputs = normed_all[...].reshape(512, 1024)
        keys = turn(dot(inputs, grads[0, :, :, :, :, lanes].reshape(1024, 256)), cosine[...], sine[...], 1.0)
        kv_all[:, :, lanes] = keys.astype(LOW).reshape(4, 128, 256)
        values = dot(inputs, grads[1, :, :, :, :, lanes].reshape(1024, 256))
        kv_all[:, :, lane_block(2 + part, 256)] = values.astype(LOW).reshape(4, 128, 256)

    loop(2, keys_values)
    g_share = Gather(g_all)
    g_share.start()
    code_share = [y_copy(off, code_all.at[y_at], code_all.at[y_at]) for off in (1, 3, 2)]
    start(code_share)

    def visible():
        shape = (512, 512)
        key_at = lax.broadcasted_iota(jnp.int32, shape, 0)
        query_at = y_at * 128 + lanes_of(shape) % 128
        return (key_at < prefix[0]) | (key_at <= query_at)

    def key_block(c):
        return kv_all[:, :, lane_block(c)].reshape(512, 128)

    def value_block(c):
        return kv_all[:, :, lane_block(c + 4)].reshape(512, 128)

    def prob_ref(c):
        return grads.at[KEY_UNIT + c // 2, pl.ds((c % 2) * 2, 2)]

    def attend(c):
        scores = jnp.where(visible(), dot_nt(key_block(c), q_four[c]) * 0.125, -1e30)
        raised = jnp.exp(scores - jnp.max(scores, axis=0, keepdims=True))
        soft = (raised * (1.0 / jnp.sum(raised, axis=0, keepdims=True))).astype(LOW)
        prob_ref(c)[...] = soft.reshape(2, 4, 2, 32, WIDE)
        first, second = unfold_heads(dot_tn(value_block(c), soft))
        joined[:, lane_block(2 * c)] = first.astype(LOW)
        joined[:, lane_block(2 * c + 1)] = second.astype(LOW)

    loop(4, attend)
    loads[("fwd", 4)].wait()
    loads[("fwd", 5)].wait()
    for part in (0, 1):
        middle[:, half[part]] = tokens[:, half[part]].astype(F32) + dot(joined[...], square(grads, 4 + part))
    ffn_r = lax.rsqrt(jnp.mean(middle[...] * middle[...], axis=1, keepdims=True) + EPS)
    x_all[y_at] = (middle[...] * ffn_r * ffn_gain[...]).astype(LOW)
    x_share = Gather(x_all)
    x_share.start()

    wait(code_share)

    def stand(ref, out):
        def body(block):
            out[:, lane_block(block)] = ref[block].T

        loop(4, body)

    x_share.forward()
    x_share.finish()
    g_share.forward()

    code = code_all[...].reshape(512, 128).astype(F32)
    in_use = code > 0.5
    logits = jnp.where(in_use, dot_nt(x_all[...].reshape(512, 1024), router[...]), -1e30)
    raised = jnp.where(in_use, jnp.exp(logits - jnp.max(logits, axis=1, keepdims=True)), 0.0)
    soft = raised / jnp.sum(raised, axis=1, keepdims=True)
    probs[...] = soft.reshape(4, 128, 128)
    gates[...] = jnp.where(code > 1.5, soft, 0.0)
    own_dots[...] = jnp.zeros_like(own_dots)
    for name in ("wg", "wu", "wd"):
        loads[name].wait()
    slab_shape = (2, 4, 2, 32, 256)

    def gate_of(j):
        here = lanes_of((512, 128)) == y_at * OWN_EXPERTS + j
        return here, jnp.sum(jnp.where(here, gates[...], 0.0), axis=1, keepdims=True)

    def expert_forward(step):
        j, lanes = step // 2, lane_block(step % 2, 256)
        inputs = x_all[...].reshape(512, 1024)
        gate_lin = dot(inputs, weights[j, :, :, :, :, lanes].reshape(1024, 256))
        up_lin = dot(inputs, weights[3 + j, :, :, :, :, lanes].reshape(1024, 256))
        sig = 1.0 / (1.0 + jnp.exp(-gate_lin))
        silu = gate_lin * sig
        act = (silu * up_lin).astype(LOW).astype(F32) * gate_of(j)[1]
        slab(6 + j)[:, :, :, :, lanes] = act.astype(LOW).reshape(slab_shape)
        slab(j)[:, :, :, :, lanes] = (up_lin * sig * (1.0 + gate_lin * (1.0 - sig))).astype(LOW).reshape(slab_shape)
        slab(3 + j)[:, :, :, :, lanes] = silu.astype(LOW).reshape(slab_shape)

    def expert_back(step):
        j, lanes = step // 2, lane_block(step % 2, 256)
        here, gate = gate_of(j)
        outer = dot_nt(g_all[...].reshape(512, 1024), wd[j, lanes, :])
        act = slab(6 + j)[:, :, :, :, lanes].reshape(512, 256).astype(F32)
        own_dots[...] += jnp.where(here, jnp.sum(act * outer, axis=1, keepdims=True), 0.0)
        outer = outer * gate
        for index in (j, 3 + j):
            slope = slab(index)[:, :, :, :, lanes].reshape(512, 256).astype(F32)
            slab(index)[:, :, :, :, lanes] = (outer * slope).astype(LOW).reshape(slab_shape)

    loop(2 * OWN_EXPERTS, expert_forward)
    g_share.finish()
    loop(2 * OWN_EXPERTS, expert_back)

    dots_copies = [y_copy(off, dots_send.at[(y_at + off) % 4], dots_in.at[off - 1]) for off in (1, 3, 2)]
    for block in range(4):
        dots_send[block] = own_dots[block * 128 : block * 128 + 128, :].T[0:16, :]
    start(dots_copies)

    def row_part(first, second):
        total = None
        for j in range(OWN_EXPERTS):
            for kind in (0, 3):
                pair = [slab(kind + j, (128, block))[...].reshape(128, WIDE) for block in (first, second)]
                part = dot_nt(jnp.concatenate(pair, axis=0), square(weights, kind + j))
                total = part if total is None else total + part
        return total

    def across_block(off):
        return (y_at + off) % 4

    rows = row_part(across_block(2), across_block(1))
    for off in (2, 1):
        row_send[across_block(off)] = rows[128 * (2 - off) : 128 * (3 - off)].astype(LOW)
    rows_back = Scatter(
        lambda block, part: row_send.at[block, pl.ds(64 * part, 64)], lambda at, part: row_in.at[at, pl.ds(64 * part, 64)]
    )
    start(rows_back.far)
    rows_back.near[0].start()
    rows = row_part(across_block(3), y_at)
    row_send[across_block(3)] = rows[0:128].astype(LOW)
    rows_back.near[1].start()
    own_row[...] = rows[128:256]
    stand(x_all, x_t)
    stand(g_all, g_t)
    rows_back.turn()
    load_pair("bwd", 4, wo_far, weights, 3)
    load_pair("bwd", 2, wq_far, weights, 0)
    load_keys("bwd", weights, 2, 5)

    class Wide:
        src, pair, lo, hi, minus, plus = grads, pair_in, lo_in, hi_in, minus_in, plus_in
        lo_b, hi_b, minus_b, plus_b = lo_in_b, hi_in_b, minus_in_b, plus_in_b

    class Narrow:
        src, pair, lo, hi, minus, plus = misc, misc_pair, misc_lo, misc_hi, misc_minus, misc_plus
        lo_b, hi_b, minus_b, plus_b = misc_lo_b, misc_hi_b, misc_minus_b, misc_plus_b

    def remote(unit, kind, src, dst, target):
        return pltpu.make_async_remote_copy(
            src_ref=src, dst_ref=dst, send_sem=send_sem.at[kind, unit], recv_sem=recv_sem.at[kind, unit],
            device_id=target, device_id_type=MESH,
        )

    class Unit:
        def __init__(self, unit):
            self.unit = unit
            self.set = Wide if unit < UNITS else Narrow
            self.at = unit if unit < UNITS else 0
            self.axis = unit % 2

        def block(self, axis, index):
            ref = self.set.src.at[self.at]
            return ref.at[index, :, core] if axis == 0 else ref.at[:, index, core]

        def cell(self, index):
            ref = self.set.src.at[self.at]
            return ref.at[x_at, index, core] if self.axis == 0 else ref.at[index, z_at, core]

        def pair_copy(self):
            s = self.set
            return remote(self.unit, 0, s.src.at[self.at, :, :, 1 - core], s.pair.at[self.at], partner)

        def far_copy(self, way):
            s = self.set
            src = self.block(self.axis, (spots[self.axis] + 2) % 4).at[pl.ds(2 * way, 2)]
            dst = (s.lo, s.hi)[way].at[self.at]
            return remote(self.unit, 1 + way, src, dst, device(self.axis, (1, 3)[way]))

        def near_copy(self, way):
            s = self.set
            src = self.block(self.axis, (spots[self.axis] + (1, 3)[way]) % 4)
            dst = (s.minus, s.plus)[way].at[self.at]
            return remote(self.unit, 3 + way, src, dst, device(self.axis, (1, 3)[way]))

        def far_copy_b(self, way):
            s = self.set
            src = self.cell((spots[1 - self.axis] + 2) % 4).at[pl.ds(16 * way, 16)]
            dst = (s.lo_b, s.hi_b)[way].at[self.at]
            return remote(self.unit, 5 + way, src, dst, device(1 - self.axis, (1, 3)[way]))

        def near_copy_b(self, way):
            s = self.set
            src = self.cell((spots[1 - self.axis] + (1, 3)[way]) % 4)
            dst = (s.minus_b, s.plus_b)[way].at[self.at]
            return remote(self.unit, 7 + way, src, dst, device(1 - self.axis, (1, 3)[way]))

        def across_copy(self, off):
            to = (y_at + off) % 4
            src, dst, at = (last, last_in, self.at - EXPERT_UNITS) if self.set is Wide else (misc_last, misc_last_in, 0)
            return remote(self.unit, 8 + off, src.at[at, pl.ds(to * 8, 8)], dst.at[off - 1, at], across(off))

        def begin(self):
            self.pair_copy().start()

        def after_pair(self):
            s = self.set
            self.pair_copy().wait()
            for slab_at in range(4):
                ref = s.src.at[self.at, slab_at, :, core]
                ref[...] = sum32(ref[...], s.pair[self.at, slab_at])
            self.far_copy(0).start()
            self.far_copy(1).start()

        def after_far(self):
            s = self.set
            for way in (0, 1):
                self.far_copy(way).wait()
                ref = self.block(self.axis, (spots[self.axis] + (1, 3)[way]) % 4).at[pl.ds(2 * way, 2)]
                ref[...] = sum32(ref[...], (s.lo, s.hi)[way][self.at])
                self.near_copy(way).start()

        def after_near(self):
            s = self.set
            for way in (0, 1):
                self.near_copy(way).wait()
            ref = self.block(self.axis, spots[self.axis])
            total = ref[...].astype(F32) + s.minus[self.at].astype(F32)
            ref[...] = (total + s.plus[self.at].astype(F32)).astype(LOW)
            for way in (0, 1):
                self.far_copy_b(way).start()

        def after_far_b(self):
            s = self.set
            for way in (0, 1):
                self.far_copy_b(way).wait()
                ref = self.cell((spots[1 - self.axis] + (1, 3)[way]) % 4).at[pl.ds(16 * way, 16)]
                ref[...] = sum32(ref[...], (s.lo_b, s.hi_b)[way][self.at])
                self.near_copy_b(way).start()

        def after_near_b(self):
            s = self.set
            for way in (0, 1):
                self.near_copy_b(way).wait()
            total = self.cell(spots[1 - self.axis])[...].astype(F32) + s.minus_b[self.at].astype(F32)
            total = total + s.plus_b[self.at].astype(F32)
            if self.unit < EXPERT_UNITS:
                expert_out[self.unit] = total
                return
            if self.set is Wide:
                last[self.at - EXPERT_UNITS] = total
            else:
                misc_last[0] = total
            for off in (1, 2, 3):
                self.across_copy(off).start()

        def finish(self):
            for off in (1, 2, 3):
                self.across_copy(off).wait()
            src, dst, at = (last, last_in, self.at - EXPERT_UNITS) if self.set is Wide else (misc_last, misc_last_in, 0)
            total = src[at, pl.ds(pl.multiple_of(y_at * 8, 8), 8), :]
            for off in (1, 2, 3):
                total = total + dst[off - 1, at]
            if self.set is Wide:
                shared_out[at] = total
            else:
                misc_out[...] = total

    STAGES = ("after_pair", "after_far", "after_near", "after_far_b", "after_near_b", "finish")
    units = [Unit(unit) for unit in range(UNITS + 1)]

    def run(stage, *which):
        for unit in which:
            getattr(units[unit], STAGES[stage])()

    def weight_grad(unit, left, right):
        grads[unit] = dot(left[...], right()).astype(LOW).reshape(BIG)
        units[unit].begin()

    def slab_value(index):
        return lambda: slab(index)[...].reshape(512, WIDE)

    before_unit = None
    for j in range(OWN_EXPERTS):
        for kind, turned_rows in ((0, x_t), (3, x_t), (6, g_t)):
            weight_grad(kind + j, turned_rows, slab_value(kind + j))
            if before_unit is not None:
                run(0, before_unit)
            before_unit = kind + j
    run(0, before_unit)
    run(1, 0, 3, 6, 1)

    def mix_part(part):
        total = None
        for j in range(OWN_EXPERTS):
            piece = dot(slab(6 + j, (256, part))[...].reshape(256, WIDE), wd[j])
            total = piece if total is None else total + piece
        x_all[pl.ds(part * 2, 2)] = total.astype(LOW).reshape(2, 128, 1024)

    loop(2, mix_part)
    run(1, 4, 7)

    def normed_stand(block):
        normed_t[:, lane_block(block)] = normed_all[block].T

    loop(4, normed_stand)

    wait(dots_copies)
    rows_back.finish()
    mix_back = Scatter(
        lambda block, part: x_all.at[block, pl.ds(64 * part, 64)], lambda at, part: mix_in.at[at, pl.ds(64 * part, 64)]
    )
    mix_back.start()
    taken = dots_send[y_at]
    moe_grad = own_row[...]
    for off in (1, 2, 3):
        taken = taken + dots_in[off - 1]
    for at in (1, 2):
        moe_grad = moe_grad + row_in[at].astype(F32)
    taken = jnp.concatenate([taken, jnp.zeros((112, 128), F32)], axis=0).T
    own_probs = probs[y_at]
    select = taken - own_probs * jnp.sum(taken, axis=1, keepdims=True)
    select = select.astype(LOW)
    moe_grad = moe_grad + dot(select, router[...])
    router_grad = dot(x_t[:, lane_block(y_at)], select)
    normal = middle[...]
    ffn_r = lax.rsqrt(jnp.mean(normal * normal, axis=1, keepdims=True) + EPS)
    scaled = moe_grad * ffn_gain[...]
    ffn_gain_grad = jnp.sum(moe_grad * normal * ffn_r, axis=0, keepdims=True)
    shrink = ffn_r * ffn_r * ffn_r * jnp.mean(scaled * normal, axis=1, keepdims=True)
    cot[...] = cot[...] + ffn_r * scaled - normal * shrink
    attn_grad = cot[...].astype(LOW)
    for part in (0, 1):
        loads[("bwd", 4 + part)].wait()
    head_grad = dot_nt(attn_grad[:, 0:WIDE], square(weights, 3)) + dot_nt(attn_grad[:, WIDE:], square(weights, 4))
    head_low = head_grad.astype(LOW).astype(F32)

    def head_ref(c):
        return x_t.at[lane_block(c % 2, 512), lane_block(1 + c // 2)]

    for c in range(4):
        head_ref(c)[...] = four_heads(head_low[:, c * 256 : c * 256 + 128], head_low[:, c * 256 + 128 : c * 256 + 256])
    x_t[:, 0:128] = attn_grad.T

    key_sums, value_sums = pair_in.at[0], pair_in.at[3]

    def attend_back(c):
        heads = head_ref(c)[...]
        low = prob_ref(c)[...].reshape(512, 512)
        soft = low.astype(F32)
        weighted = soft * dot_nt(value_block(c), heads)
        sums = jnp.sum(weighted, axis=0, keepdims=True)
        score_grad = ((weighted - soft * sums) * 0.125).astype(LOW)
        value_sums[:, :, :, lane_block(c)] = dot(low, heads).astype(LOW).reshape(4, 4, 32, 128)
        key_part = turn(dot(score_grad, q_four[c]), cosine[...], sine[...], -1.0)
        key_sums[:, :, :, lane_block(c)] = key_part.astype(LOW).reshape(4, 4, 32, 128)
        first, second = unfold_heads(dot_tn(key_block(c), score_grad))
        own_cosine, own_sine = cosine[own_rows, :], sine[own_rows, :]
        q_low[:, lane_block(2 * c)] = turn(first, own_cosine, own_sine, -1.0).astype(LOW)
        q_low[:, lane_block(2 * c + 1)] = turn(second, own_cosine, own_sine, -1.0).astype(LOW)

    loop(4, attend_back)
    mix_back.turn()
    kv_back = Scatter(lambda block, part: (key_sums, value_sums)[part].at[block], lambda at, part: kvg_in.at[at, part])
    kv_back.start()

    run(1, 2, 5, 8)
    run(2, 0, 3, 6)
    for part in (0, 1):
        weight_grad(OUT_UNIT + part, x_t.at[:, pl.ds(0, 128)], lambda: joined[:, half[part]])
    weight_grad(KEY_UNIT, normed_t, lambda: key_sums[...].reshape(512, WIDE))
    weight_grad(VALUE_UNIT, normed_t, lambda: value_sums[...].reshape(512, WIDE))
    run(0, OUT_UNIT, OUT_UNIT + 1)
    run(2, 1, 4)
    for part in (0, 1):
        weight_grad(QUERY_UNIT + part, normed_t.at[:, lane_block(y_at)], lambda: q_low[:, half[part]])
    run(0, KEY_UNIT, VALUE_UNIT)
    run(2, 7, 2, 5, 8)
    run(1, OUT_UNIT, OUT_UNIT + 1)
    run(0, QUERY_UNIT, QUERY_UNIT + 1)
    for part in (0, 1, 2, 3):
        loads[("bwd", part)].wait()
    normed_grad = dot_nt(q_low[:, 0:WIDE], square(weights, 0)) + dot_nt(q_low[:, WIDE:], square(weights, 1))
    input_grad[...] = normed_grad
    kv_back.turn()
    mix_back.finish()
    total = middle[...] + x_all[y_at].astype(F32)
    for at in (1, 2):
        total = total + mix_in[at].astype(F32)
    hidden_out[...] = total
    run(3, 0, 3, 6, 1, 4)
    run(1, KEY_UNIT, VALUE_UNIT)
    run(2, OUT_UNIT, OUT_UNIT + 1)
    run(1, QUERY_UNIT, QUERY_UNIT + 1)
    run(4, 0, 3, 6, 1, 4)

    kv_back.finish()
    key_back, value_back = key_sums[y_at].reshape(128, WIDE).astype(F32), value_sums[y_at].reshape(128, WIDE).astype(F32)
    for at in (1, 2):
        key_back = key_back + kvg_in[at, 0].reshape(128, WIDE).astype(F32)
        value_back = value_back + kvg_in[at, 1].reshape(128, WIDE).astype(F32)
    q_low[:, half[0]] = key_back.astype(LOW)
    q_low[:, half[1]] = value_back.astype(LOW)
    normed_grad = input_grad[...] + dot_nt(q_low[:, 0:WIDE], square(weights, 2))
    normed_grad = normed_grad + dot_nt(q_low[:, WIDE:], square(weights, 5))
    hidden = tokens[...].astype(F32)
    attn_r = lax.rsqrt(jnp.mean(hidden * hidden, axis=1, keepdims=True) + EPS)
    scaled = normed_grad * attn_gain[...]
    attn_gain_grad = jnp.sum(normed_grad * hidden * attn_r, axis=0, keepdims=True)
    shrink = attn_r * attn_r * attn_r * jnp.mean(scaled * hidden, axis=1, keepdims=True)
    input_grad[...] = cot[...] + attn_r * scaled - hidden * shrink
    wide_lane = lanes_of((1024, 128))
    gains = jnp.where(
        wide_lane == EXPERTS,
        jnp.broadcast_to(attn_gain_grad, (128, 1024)).T,
        jnp.broadcast_to(ffn_gain_grad, (128, 1024)).T,
    )
    misc[0] = jnp.where(wide_lane < EXPERTS, router_grad, gains).astype(LOW).reshape(4, 4, 2, 32, 128)
    units[UNITS].begin()

    rest = (OUT_UNIT, OUT_UNIT + 1, QUERY_UNIT, QUERY_UNIT + 1, KEY_UNIT, VALUE_UNIT, UNITS)
    run(3, 7, 2, 5, 8)
    run(2, KEY_UNIT, VALUE_UNIT)
    run(0, UNITS)
    run(3, OUT_UNIT, OUT_UNIT + 1)
    run(4, 7, 2, 5, 8)
    run(2, QUERY_UNIT, QUERY_UNIT + 1)
    run(1, UNITS)
    run(3, KEY_UNIT, VALUE_UNIT)
    run(4, OUT_UNIT, OUT_UNIT + 1)
    run(2, UNITS)
    run(3, QUERY_UNIT, QUERY_UNIT + 1, UNITS)
    run(4, KEY_UNIT, VALUE_UNIT, QUERY_UNIT, QUERY_UNIT + 1, UNITS)
    run(5, *rest)


def layer(*args):
    vmem = pl.BlockSpec(memory_space=pltpu.VMEM)
    smem = pl.BlockSpec(memory_space=pltpu.SMEM)
    far = pl.BlockSpec(memory_space=pl.ANY)
    low = lambda *shape: pltpu.VMEM(shape, LOW)
    wide = lambda *shape: pltpu.VMEM(shape, F32)
    sems = pltpu.SemaphoreType.DMA
    scratch = [
        low(UNITS + 1, *BIG), low(6, *BIG), low(3, 512, 1024), low(128, 1024), wide(128, 1024), wide(512, 128), wide(512, 128),
        low(4, 128, 1024), low(128, 1024), low(4, 512, 128),
        low(4, 128, 1024), low(4, 128, 1024), low(4, 128, 1024), low(4, 128, 128),
        low(1024, 512), low(1024, 512), wide(4, 128, 128), wide(512, 128), wide(512, 128),
        wide(4, 16, 128), wide(3, 16, 128), low(4, 128, 1024), low(3, 128, 1024),
        low(3, 128, 1024), low(3, 2, 4, 32, WIDE),
    ]
    for count, width in ((UNITS, WIDE), (1, 128)):
        if count == 1:
            scratch += [low(1, 4, 4, 2, 32, width)]
        scratch += [low(count, 4, 4, 32, width), low(count, 2, 32, width), low(count, 2, 32, width)]
        scratch += [low(count, 4, 32, width), low(count, 4, 32, width)]
        scratch += [low(count, 16, width), low(count, 16, width), low(count, 32, width), low(count, 32, width)]
        shared = count - EXPERT_UNITS if count == UNITS else 1
        scratch += [wide(shared, 32, width), wide(3, shared, 8, width)]
    scratch += [sems((48,)), sems((48,)), sems((12, UNITS + 1)), sems((12, UNITS + 1)), sems((20,))]
    shape = jax.ShapeDtypeStruct
    return pl.pallas_call(
        layer_kernel,
        out_shape=(
            shape((128, 1024), F32),
            shape((128, 1024), F32),
            shape((EXPERT_UNITS, 32, WIDE), F32),
            shape((UNITS - EXPERT_UNITS, 8, WIDE), F32),
            shape((8, 128), F32),
        ),
        in_specs=[vmem, vmem, vmem, smem, vmem, vmem, vmem] + [far] * 10,
        out_specs=(vmem,) * 5,
        scratch_shapes=scratch,
        compiler_params=pltpu.CompilerParams(
            collective_id=0, has_side_effects=True, vmem_limit_bytes=60 * 2**20
        ),
        name="layer",
    )(*args)


def place_kernel(
    hidden_in, input_in, experts_in, shared_in, misc_in,
    hidden_out, input_grad, attn_gain, query, key, value, out, ffn_gain, router, gate, up, down,
):
    hidden_out[...] = hidden_in[...]
    input_grad[...] = input_in[...]
    for kind, to in enumerate((gate, up, down)):
        to[...] = experts_in[3 * kind : 3 * kind + 3]
    key[...] = shared_in[KEY_UNIT - EXPERT_UNITS]
    value[...] = shared_in[VALUE_UNIT - EXPERT_UNITS]
    for part, lanes in ((0, slice(0, WIDE)), (1, slice(WIDE, 2 * WIDE))):
        query[:, lanes] = shared_in[QUERY_UNIT - EXPERT_UNITS + part]
        out[:, lanes] = shared_in[OUT_UNIT - EXPERT_UNITS + part]
    router[...] = misc_in[:, 0:EXPERTS]
    flipped = jnp.concatenate([misc_in[...], jnp.zeros((120, 128), F32)], axis=0).T
    attn_gain[...] = flipped[EXPERTS : EXPERTS + 1, 0:8]
    ffn_gain[...] = flipped[EXPERTS + 1 : EXPERTS + 2, 0:8]


def place(*results):
    vmem = pl.BlockSpec(memory_space=pltpu.VMEM)
    shape = lambda *dims: jax.ShapeDtypeStruct(dims, F32)
    return pl.pallas_call(
        place_kernel,
        out_shape=(
            shape(128, 1024), shape(128, 1024), shape(1, 8), shape(8, 1024), shape(8, WIDE), shape(8, WIDE), shape(8, 1024),
            shape(1, 8), shape(8, EXPERTS), shape(3, 32, WIDE), shape(3, 32, WIDE), shape(3, 32, WIDE),
        ),
        in_specs=[vmem] * 5,
        out_specs=(vmem,) * 12,
        name="place",
    )(*results)


def rope_tables(length):
    inverse = np.float32(10000.0) ** (-np.arange(32, dtype=np.float32) / np.float32(32))
    angles = np.arange(length, dtype=np.float32)[:, None] * inverse[None, :]
    cosine, sine = np.cos(angles), np.sin(angles)
    return np.tile(cosine, (1, 4)), np.concatenate([-sine, sine, -sine, sine], axis=1)


def per_device(
    tokens, routes, slot_order, prefix, attn_gain, w_query, w_key, w_value, w_out, ffn_gain, w_router,
    w_gate, w_up, w_down, cotangent,
):
    cosine, sine = rope_tables(512)
    results = layer(
        tokens, routes[0].T, slot_order[0], prefix, attn_gain, ffn_gain, w_router[0].T,
        w_query.reshape(4, 4, 2, 32, 1024), w_key.reshape(BIG), w_value.reshape(BIG), w_out.reshape(4, 4, 2, 32, 1024),
        w_gate.reshape(3, *BIG), w_up.reshape(3, *BIG), w_down[0], cotangent, jnp.asarray(cosine), jnp.asarray(sine),
    )
    hidden_out, input_grad, gain_attn, query, key, value, out, gain_ffn, router, gate, up, down = place(*results)
    return (
        hidden_out, input_grad, gain_attn, query[None], key[None], value[None], out.T[None], gain_ffn, router[None],
        gate[None], up[None], down.transpose(0, 2, 1)[None],
    )


def solution(mesh):
    both = ("group", "expert")
    in_specs = (
        P(both, None), P(None, both, None), P(None, both, None), P("group"), P(), P(), P(), P(), P(), P(), P(),
        P(None, "expert", None, None), P(None, "expert", None, None), P(None, "expert", None, None), P(both, None),
    )
    out_specs = (
        P(both, None), P(both, None), P(None, both), P(None, both, None), P(None, both, None), P(None, both, None),
        P(None, None, both), P(None, both), P(None, both, None), P(None, "expert", "group", None),
        P(None, "expert", "group", None), P(None, "expert", None, "group"),
    )
    return jax.shard_map(per_device, mesh=mesh, in_specs=in_specs, out_specs=out_specs, check_vma=False)
```

```python
import jax
import jax.numpy as jnp
import numpy as np
from jax import lax
from jax.experimental import pallas as pl
from jax.experimental.pallas import tpu as pltpu
from jax.sharding import PartitionSpec as P

MESH = pl.DeviceIdType.MESH
LOW = jnp.bfloat16
F32 = jnp.float32
EPS = 1e-06
CAP = 96
EXPERTS = 12
OWN_EXPERTS = 3
EXPERT_UNITS = 9
UNITS = 13
WIDE, NARROW = 512, 384
KEY_UNIT, VALUE_UNIT, OUT_UNIT = 9, 10, 11
SLOTS = (0, 1, 2, 3, 4, 5, 6, 7, 8, 9, 10, 13, 14)
PROBS, SLABS, SLOT_COUNT = 9, 11, 16
BIG = (4, 4, 2, 32, WIDE)


PLAN = (
    (),
    (),
    (),
    ((0, 0), (0, 3)),
    ((0, 6),),
    ((1, 0), (1, 3)),
    (),
    (),
    ((1, 6), (0, 1)),
    ((2, 3), (0, 4)),
    ((0, 7), (2, 0)),
    ((1, 1), (0, 2)),
    (),
    ((2, 6), (3, 3)),
    ((0, 5), (0, 8)),
    ((1, 4), (1, 7)),
    ((3, 0), (1, 2)),
    ((2, 1), (3, 6)),
    ((4, 3), (0, 11)),
    ((1, 5), (0, 12)),
    ((1, 8), (2, 7)),
    (),
    (
        (2, 4), (4, 0), (4, 6), (2, 2), (3, 1), (1, 11), (0, 9), (1, 12), (0, 10), (2, 5), (2, 8), (3, 7), (3, 4),
        (4, 1), (0, 13), (3, 2), (2, 12), (2, 11),
    ),
    ((1, 10), (1, 9), (3, 5), (3, 8), (4, 7), (3, 11), (4, 4), (1, 13)),
    ((2, 10), (4, 5), (4, 11), (4, 2), (3, 12), (2, 9), (4, 8)),
    (
        (6, 0), (2, 13), (5, 11), (3, 10), (3, 9), (4, 12), (3, 13), (4, 10), (4, 9), (6, 1), (4, 13), (5, 12),
        (5, 10), (5, 9), (5, 13),
    ),
)


def group_of(x_at, z_at, core):
    return x_at * 8 + z_at * 2 + core


def dot(first, second):
    return jnp.dot(first, second, preferred_element_type=F32)


def dot_nt(first, second):
    return lax.dot_general(first, second, (((1,), (1,)), ((), ())), preferred_element_type=F32)


def dot_tn(first, second):
    return lax.dot_general(first, second, (((0,), (0,)), ((), ())), preferred_element_type=F32)


def sum32(first, second):
    return (first.astype(F32) + second.astype(F32)).astype(LOW)


def lanes_of(shape):
    return lax.broadcasted_iota(jnp.int32, shape, len(shape) - 1)


def turn(values, cosine, sine, sign):
    first = lanes_of((values.shape[0], 128)) % 64 < 32
    parts = []
    for at in range(values.shape[1] // 128):
        part = values[:, at * 128 : at * 128 + 128]
        swapped = jnp.where(first, pltpu.roll(part, 96, 1), pltpu.roll(part, 32, 1))
        parts.append(part * cosine + sign * (swapped * sine))
    return parts[0] if len(parts) == 1 else jnp.concatenate(parts, axis=1)


def four_heads(first, second):
    low_half = lanes_of((128, 128)) < 64
    zero = jnp.zeros((128, 128), F32)
    return jnp.concatenate(
        [
            jnp.where(low_half, first, zero),
            jnp.where(low_half, pltpu.roll(first, 64, 1), zero),
            jnp.where(low_half, zero, pltpu.roll(second, 64, 1)),
            jnp.where(low_half, zero, second),
        ],
        axis=0,
    ).astype(LOW)


def unfold_heads(stood):
    first = jnp.concatenate([stood[0:64, 0:128], stood[0:64, 128:256]], axis=0)
    second = jnp.concatenate([stood[64:128, 256:384], stood[64:128, 384:512]], axis=0)
    return first.T, second.T


def loop(count, body):
    def step(index, carry):
        body(index)
        return carry

    lax.fori_loop(0, count, step, 0)


def lane_block(index, width=128):
    return pl.ds(pl.multiple_of(index * width, width), width)


def layer_kernel(
    prefix, tokens_far, routes_far, order_far, attn_gain_far, ffn_gain_far, w_router_far,
    wq_far, wk_far, wv_far, wo_far, wg_far, wu_far, wd_far, cot_far, cos_far, sin_far,
    hidden_to, input_to, expert_to, query_to, key_to, value_to, out_to, misc_to,
    hidden_out, input_grad, expert_out, query_out, key_out, value_out, out_out, misc_out,
    tokens, routes, order, attn_gain, ffn_gain, w_router,
    grads, weights, wd, router, cot, cosine, sine,
    normed_all, joined, q_four, kv_all, x_all, g_all, code_all,
    x_t, g_t, probs, gates, own_dots, dots_send, dots_in, row_send, row_in, mix_in, q_low, q_all, grad_in,
    pair_in, lo_in, hi_in, minus_in, plus_in, lo_in_b, hi_in_b, minus_in_b, plus_in_b, last, last_in,
    misc, misc_pair, misc_lo, misc_hi, misc_minus, misc_plus, misc_lo_b, misc_hi_b, misc_minus_b, misc_plus_b,
    misc_last, misc_last_in,
    y_send, y_recv, send_sem, recv_sem, local_sem,
):
    group = lax.axis_index("group")
    y_at = lax.axis_index("expert")
    x_at, z_at, core = group // 8, (group // 2) % 4, group % 2
    spots = (x_at, z_at)
    own_rows = pl.ds(pl.multiple_of(y_at * 128, 128), 128)
    middle, own_row, normed_t = hidden_out, input_grad, g_t

    def device(axis, offset):
        if axis == 0:
            return (group_of((x_at + offset) % 4, z_at, core), y_at)
        return (group_of(x_at, (z_at + offset) % 4, core), y_at)

    def across(offset):
        return (group, (y_at + offset) % 4)

    partner = (group_of(x_at, z_at, 1 - core), y_at)
    barrier = pltpu.get_barrier_semaphore()
    peers = [partner] + [device(axis, off) for axis in (0, 1) for off in (1, 3)]
    peers += [across(off) for off in (1, 2, 3)]
    for peer in peers:
        pl.semaphore_signal(barrier, inc=1, device_id=peer, device_id_type=MESH)

    half = pl.ds(0, WIDE), pl.ds(WIDE, WIDE)
    loads = {}

    def load(name, src, dst):
        copy = pltpu.make_async_copy(src, dst, local_sem.at[len(loads)])
        loads[name] = copy
        copy.start()

    def load_keys(tag, ref, wk_to, wv_to):
        load((tag, 0), wk_far, ref.at[wk_to])
        load((tag, 1), wv_far, ref.at[wv_to])

    def load_pair(tag, at, src, ref, to):
        for part in (0, 1):
            load((tag, at + part), src.at[:, :, :, :, half[part]], ref.at[to + part])

    small = (
        (tokens_far, tokens), (attn_gain_far, attn_gain), (routes_far, routes), (order_far, order),
        (ffn_gain_far, ffn_gain), (w_router_far, w_router),
    )
    for at, (src, dst) in enumerate(small):
        load(("small", at), src, dst)
    load_pair("fwd", 2, wq_far, grads, 2)
    load("cos", cos_far, cosine)
    load("sin", sin_far, sine)
    load_keys("fwd", grads, 0, 1)

    def square(ref, unit):
        return ref[unit].reshape(1024, WIDE)

    def slab(index, rows=None):
        unit, top = SLABS + index // 2, (index % 2) * 2
        if rows is None:
            return grads.at[unit, pl.ds(top, 2)]
        kind, at = rows
        if kind == 256:
            return grads.at[unit, top + at]
        return grads.at[unit, top + at // 2, pl.ds((at % 2) * 2, 2)]

    for at in (0, 1):
        loads[("small", at)].wait()
    hidden = tokens[...].astype(F32)
    attn_r = lax.rsqrt(jnp.mean(hidden * hidden, axis=1, keepdims=True) + EPS)
    normed_all[y_at] = (hidden * attn_r * attn_gain[...]).astype(LOW)
    pl.semaphore_wait(barrier, len(peers))

    y_used = []

    def y_copy(off, src, dst):
        at = len(y_used)
        y_used.append(off)
        return pltpu.make_async_remote_copy(
            src_ref=src, dst_ref=dst, send_sem=y_send.at[at], recv_sem=y_recv.at[at],
            device_id=across(off), device_id_type=MESH,
        )

    def start(copies):
        for copy in copies:
            copy.start()

    def wait(copies):
        for copy in copies:
            copy.wait()

    left, right = (y_at + 3) % 4, (y_at + 1) % 4
    low_rows, high_rows = pl.ds(0, 64), pl.ds(64, 64)

    class Gather:
        def __init__(self, ref):
            def pass_on(block, rows, off):
                return y_copy(off, ref.at[block, rows], ref.at[block, rows])

            self.first = [pass_on(y_at, low_rows, 1), pass_on(y_at, high_rows, 3)]
            self.first += [pass_on(y_at, high_rows, 1), pass_on(y_at, low_rows, 3)]
            self.second = [pass_on(left, low_rows, 1), pass_on(right, high_rows, 3)]

        def start(self):
            start(self.first)

        def forward(self):
            for came, on in zip(self.first, self.second):
                came.wait_recv()
                on.start()

        def finish(self):
            for copy in self.first[2:]:
                copy.wait_recv()
            for copy in self.first:
                copy.wait_send()
            wait(self.second)

    class Scatter:
        def __init__(self, spot, send, block, land):
            self.block, self.land = block, land
            far, self.right, self.left = (spot + 2) % 4, (spot + 1) % 4, (spot + 3) % 4
            self.far = [send(1, block(far, 0), land(0, 0)), send(3, block(far, 1), land(0, 1))]
            self.near = [send(1, block(self.right, 1), land(1, 1)), send(3, block(self.left, 0), land(2, 0))]
            self.last = [send(1, block(self.right, 0), land(1, 0)), send(3, block(self.left, 1), land(2, 1))]

        def start(self):
            start(self.far)
            start(self.near)

        def turn(self):
            for part, to in ((0, self.right), (1, self.left)):
                self.far[part].wait()
                ref = self.block(to, part)
                ref[...] = sum32(ref[...], self.land(0, part)[...])
                self.last[part].start()

        def finish(self):
            wait(self.near)
            wait(self.last)

    normed_share = Gather(normed_all)
    normed_share.start()
    load_pair("fwd", 4, wo_far, grads, 4)
    load("cot", cot_far, cot)
    load("wg", wg_far, weights.at[pl.ds(0, 3)])
    load("wu", wu_far, weights.at[pl.ds(3, 3)])
    load("wd", wd_far, wd)

    for name in ("cos", "sin", ("small", 2), ("small", 3), ("small", 4), ("small", 5)):
        loads[name].wait()
    for part in (0, 1):
        loads[("fwd", 2 + part)].wait()
        turned = turn(dot(normed_all[y_at], square(grads, 2 + part)), cosine[own_rows, :], sine[own_rows, :], 1.0)
        turned = turned.astype(LOW).astype(F32)
        for c in (0, 1):
            q_four[part * 2 + c] = four_heads(
                turned[:, c * 256 : c * 256 + 128], turned[:, c * 256 + 128 : c * 256 + 256]
            )

    expert_at = lax.broadcasted_iota(jnp.int32, (128, 128), 0)
    member = jnp.zeros((128, 128), F32)
    for pick in range(routes.shape[0]):
        member = member + jnp.where(routes[pick : pick + 1, :] == expert_at, 1.0, 0.0)
    member = member.T
    ranks = jnp.broadcast_to(order[...].astype(F32), (128, 128))
    earlier = jnp.where(ranks < ranks.T, 1.0, 0.0).astype(LOW)
    before = dot(earlier, member.astype(LOW))
    code_all[y_at] = jnp.where((member > 0.5) & (before < CAP - 0.5), 2.0, member).astype(LOW)
    loads["cot"].wait()
    g_all[y_at] = cot[...].astype(LOW)
    router[...] = jnp.zeros_like(router)
    router[0:EXPERTS, :] = w_router[...]
    for part in (0, 1):
        loads[("fwd", part)].wait()
    normed_share.forward()
    normed_share.finish()

    def keys_values(part):
        lanes = lane_block(part, 256)
        inputs = normed_all[...].reshape(512, 1024)
        keys = turn(dot(inputs, grads[0, :, :, :, :, lanes].reshape(1024, 256)), cosine[...], sine[...], 1.0)
        kv_all[:, :, lanes] = keys.astype(LOW).reshape(4, 128, 256)
        values = dot(inputs, grads[1, :, :, :, :, lanes].reshape(1024, 256))
        kv_all[:, :, lane_block(2 + part, 256)] = values.astype(LOW).reshape(4, 128, 256)

    loop(2, keys_values)
    g_share = Gather(g_all)
    g_share.start()
    code_share = [y_copy(off, code_all.at[y_at], code_all.at[y_at]) for off in (1, 3, 2)]
    start(code_share)

    def visible():
        shape = (512, 512)
        key_at = lax.broadcasted_iota(jnp.int32, shape, 0)
        query_at = y_at * 128 + lanes_of(shape) % 128
        return (key_at < prefix[0]) | (key_at <= query_at)

    def key_block(c):
        return kv_all[:, :, lane_block(c)].reshape(512, 128)

    def value_block(c):
        return kv_all[:, :, lane_block(c + 4)].reshape(512, 128)

    def prob_ref(c):
        return grads.at[PROBS + c // 2, pl.ds((c % 2) * 2, 2)]

    def attend(c):
        scores = jnp.where(visible(), dot_nt(key_block(c), q_four[c]) * 0.125, -1e30)
        raised = jnp.exp(scores - jnp.max(scores, axis=0, keepdims=True))
        soft = (raised * (1.0 / jnp.sum(raised, axis=0, keepdims=True))).astype(LOW)
        prob_ref(c)[...] = soft.reshape(2, 4, 2, 32, WIDE)
        first, second = unfold_heads(dot_tn(value_block(c), soft))
        joined[:, lane_block(2 * c)] = first.astype(LOW)
        joined[:, lane_block(2 * c + 1)] = second.astype(LOW)

    loop(4, attend)
    loads[("fwd", 4)].wait()
    loads[("fwd", 5)].wait()
    for part in (0, 1):
        middle[:, half[part]] = tokens[:, half[part]].astype(F32) + dot(joined[...], square(grads, 4 + part))
    ffn_r = lax.rsqrt(jnp.mean(middle[...] * middle[...], axis=1, keepdims=True) + EPS)
    x_all[y_at] = (middle[...] * ffn_r * ffn_gain[...]).astype(LOW)
    x_share = Gather(x_all)
    x_share.start()

    wait(code_share)

    def stand(ref, out):
        def body(block):
            out[:, lane_block(block)] = ref[block].T

        loop(4, body)

    x_share.forward()
    x_share.finish()
    g_share.forward()

    code = code_all[...].reshape(512, 128).astype(F32)
    in_use = code > 0.5
    logits = jnp.where(in_use, dot_nt(x_all[...].reshape(512, 1024), router[...]), -1e30)
    raised = jnp.where(in_use, jnp.exp(logits - jnp.max(logits, axis=1, keepdims=True)), 0.0)
    soft = raised / jnp.sum(raised, axis=1, keepdims=True)
    probs[...] = soft.reshape(4, 128, 128)
    gates[...] = jnp.where(code > 1.5, soft, 0.0)
    own_dots[...] = jnp.zeros_like(own_dots)
    for name in ("wg", "wu", "wd"):
        loads[name].wait()
    slab_shape = (2, 4, 2, 32, 256)

    def gate_of(j):
        here = lanes_of((512, 128)) == y_at * OWN_EXPERTS + j
        return here, jnp.sum(jnp.where(here, gates[...], 0.0), axis=1, keepdims=True)

    def expert_forward(step):
        j, lanes = step // 2, lane_block(step % 2, 256)
        inputs = x_all[...].reshape(512, 1024)
        gate_lin = dot(inputs, weights[j, :, :, :, :, lanes].reshape(1024, 256))
        up_lin = dot(inputs, weights[3 + j, :, :, :, :, lanes].reshape(1024, 256))
        sig = 1.0 / (1.0 + jnp.exp(-gate_lin))
        silu = gate_lin * sig
        act = (silu * up_lin).astype(LOW).astype(F32) * gate_of(j)[1]
        slab(6 + j)[:, :, :, :, lanes] = act.astype(LOW).reshape(slab_shape)
        slab(j)[:, :, :, :, lanes] = (up_lin * sig * (1.0 + gate_lin * (1.0 - sig))).astype(LOW).reshape(slab_shape)
        slab(3 + j)[:, :, :, :, lanes] = silu.astype(LOW).reshape(slab_shape)

    def expert_back(step):
        j, lanes = step // 2, lane_block(step % 2, 256)
        here, gate = gate_of(j)
        outer = dot_nt(g_all[...].reshape(512, 1024), wd[j, lanes, :])
        act = slab(6 + j)[:, :, :, :, lanes].reshape(512, 256).astype(F32)
        own_dots[...] += jnp.where(here, jnp.sum(act * outer, axis=1, keepdims=True), 0.0)
        outer = outer * gate
        for index in (j, 3 + j):
            slope = slab(index)[:, :, :, :, lanes].reshape(512, 256).astype(F32)
            slab(index)[:, :, :, :, lanes] = (outer * slope).astype(LOW).reshape(slab_shape)

    loop(2 * OWN_EXPERTS, expert_forward)
    stand(x_all, x_t)
    g_share.finish()
    stand(g_all, g_t)
    loop(2, expert_back)

    class Wide:
        src, pair, lo, hi, minus, plus = grads, pair_in, lo_in, hi_in, minus_in, plus_in
        lo_b, hi_b, minus_b, plus_b = lo_in_b, hi_in_b, minus_in_b, plus_in_b

    class Narrow:
        src, pair, lo, hi, minus, plus = misc, misc_pair, misc_lo, misc_hi, misc_minus, misc_plus
        lo_b, hi_b, minus_b, plus_b = misc_lo_b, misc_hi_b, misc_minus_b, misc_plus_b

    class Unit:
        def __init__(self, unit):
            self.unit, self.axis, self.used = unit, unit % 2, 0
            self.set, self.at = (Wide, unit) if unit < UNITS else (Narrow, 0)
            s = self.set
            ref = s.src.at[SLOTS[unit] if s is Wide else 0]
            self.ref = ref
            self.pair = self.remote(partner, ref.at[:, :, 1 - core], s.pair.at[self.at])

            def block(index, part):
                halves = pl.ds(2 * part, 2)
                return ref.at[index, halves, core] if self.axis == 0 else ref.at[halves, index, core]

            def land(at, part):
                if at == 0:
                    return (s.lo, s.hi)[part].at[self.at]
                return (s.minus, s.plus)[at - 1].at[self.at, pl.ds(2 * part, 2)]

            def cell(index, part=None):
                place = ref.at[x_at, index, core] if self.axis == 0 else ref.at[index, z_at, core]
                return place if part is None else place.at[pl.ds(16 * part, 16)]

            def land_b(at, part):
                if at == 0:
                    return (s.lo_b, s.hi_b)[part].at[self.at]
                return (s.minus_b, s.plus_b)[at - 1].at[self.at, pl.ds(16 * part, 16)]

            axis = self.axis
            self.ring = Scatter(spots[axis], lambda off, src, dst: self.remote(device(axis, off), src, dst), block, land)
            self.ring_b = Scatter(spots[1 - axis], lambda off, src, dst: self.remote(device(1 - axis, off), src, dst), cell, land_b)
            self.own = ref.at[spots[0], :, core] if axis == 0 else ref.at[:, spots[1], core]
            self.own_b = cell(spots[1 - axis])
            if unit >= EXPERT_UNITS:
                src, dst, at = (last, last_in, unit - EXPERT_UNITS) if s is Wide else (misc_last, misc_last_in, 0)
                self.last, self.last_in = src.at[at], [dst.at[off, at] for off in range(3)]
                self.across = [
                    self.remote(across(off), self.last.at[pl.ds((y_at + off) % 4 * 8, 8)], self.last_in[off - 1])
                    for off in (1, 2, 3)
                ]

        def remote(self, to, src, dst):
            self.used += 1
            return pltpu.make_async_remote_copy(
                src_ref=src, dst_ref=dst, send_sem=send_sem.at[self.unit, self.used - 1],
                recv_sem=recv_sem.at[self.unit, self.used - 1], device_id=to, device_id_type=MESH,
            )

        def begin(self):
            self.pair.start()

        def after_pair(self):
            s = self.set
            self.pair.wait()
            for slab_at in range(4):
                ref = self.ref.at[slab_at, :, core]
                ref[...] = sum32(ref[...], s.pair[self.at, slab_at])
            self.ring.start()

        def turn(self):
            self.ring.turn()

        def after_ring(self):
            s = self.set
            self.ring.finish()
            total = self.own[...].astype(F32) + s.minus[self.at].astype(F32)
            self.own[...] = (total + s.plus[self.at].astype(F32)).astype(LOW)
            self.ring_b.start()

        def turn_b(self):
            self.ring_b.turn()

        def after_ring_b(self):
            s = self.set
            self.ring_b.finish()
            total = self.own_b[...].astype(F32) + s.minus_b[self.at].astype(F32)
            total = total + s.plus_b[self.at].astype(F32)
            if self.unit < EXPERT_UNITS:
                expert_out[self.unit] = total
            else:
                self.last[...] = total
                start(self.across)

        def finish(self):
            wait(self.across)
            total = self.last[pl.ds(pl.multiple_of(y_at * 8, 8), 8), :]
            if self.set is Narrow:
                for off in range(4):
                    rows = self.last_in[off - 1][:, 0:256] if off else total[:, 0:256]
                    query_out[:, lane_block((y_at + 4 - off) % 4, 256)] = rows
            for came in self.last_in:
                total = total + came[...]
            if self.unit == KEY_UNIT:
                key_out[...] = total
            elif self.unit == VALUE_UNIT:
                value_out[...] = total
            elif self.set is Wide:
                out_out[:, half[self.unit - OUT_UNIT]] = total
            else:
                misc_out[...] = total[:, 256:]

    extras = {}
    stages = (Unit.after_pair, Unit.turn, Unit.after_ring, Unit.turn_b, Unit.after_ring_b, Unit.finish)
    units = [Unit(unit) for unit in range(UNITS + 1)]

    def run(point):
        for stage, unit in PLAN[point]:
            if stage < len(stages):
                stages[stage](units[unit])
            else:
                extras[unit]()

    def weight_grad(unit, left, right):
        grads[SLOTS[unit]] = dot(left[...], right()).astype(LOW).reshape(BIG)
        units[unit].begin()

    def slab_value(index):
        return lambda: slab(index)[...].reshape(512, WIDE)

    def expert_units(j, point):
        for at, (kind, turned_rows) in enumerate(((0, x_t), (3, x_t), (6, g_t))):
            weight_grad(kind + j, turned_rows, slab_value(kind + j))
            run(point + at)

    expert_units(0, 0)
    loop(2 * OWN_EXPERTS - 2, lambda step: expert_back(step + 2))

    dots_copies = [y_copy(off, dots_send.at[(y_at + off) % 4], dots_in.at[off - 1]) for off in (1, 3, 2)]
    for block in range(4):
        dots_send[block] = own_dots[block * 128 : block * 128 + 128, :].T[0:16, :]
    start(dots_copies)

    def row_part(first, second):
        total = None
        for j in range(OWN_EXPERTS):
            for kind in (0, 3):
                pair = [slab(kind + j, (128, block))[...].reshape(128, WIDE) for block in (first, second)]
                part = dot_nt(jnp.concatenate(pair, axis=0), square(weights, kind + j))
                total = part if total is None else total + part
        return total

    def across_block(off):
        return (y_at + off) % 4

    rows = row_part(across_block(2), across_block(1))
    for off in (2, 1):
        row_send[across_block(off)] = rows[128 * (2 - off) : 128 * (3 - off)].astype(LOW)
    rows_back = Scatter(
        y_at, y_copy, lambda block, part: row_send.at[block, pl.ds(64 * part, 64)], lambda at, part: row_in.at[at, pl.ds(64 * part, 64)]
    )
    start(rows_back.far)
    rows_back.near[0].start()
    run(3)
    rows = row_part(across_block(3), y_at)
    row_send[across_block(3)] = rows[0:128].astype(LOW)
    rows_back.near[1].start()
    own_row[...] = rows[128:256]
    run(4)
    rows_back.turn()
    load_pair("bwd", 4, wo_far, weights, 3)
    load_pair("bwd", 2, wq_far, weights, 0)
    load_keys("bwd", weights, 2, 5)

    expert_units(1, 5)
    expert_units(2, 8)

    def mix_part(part):
        total = None
        for j in range(OWN_EXPERTS):
            piece = dot(slab(6 + j, (256, part))[...].reshape(256, WIDE), wd[j])
            total = piece if total is None else total + piece
        x_all[pl.ds(part * 2, 2)] = total.astype(LOW).reshape(2, 128, 1024)

    loop(2, mix_part)
    run(11)

    def normed_stand(block):
        normed_t[:, lane_block(block)] = normed_all[block].T

    loop(4, normed_stand)
    run(12)

    wait(dots_copies)
    rows_back.finish()
    mix_back = Scatter(
        y_at, y_copy, lambda block, part: x_all.at[block, pl.ds(64 * part, 64)], lambda at, part: mix_in.at[at, pl.ds(64 * part, 64)]
    )
    taken = dots_send[y_at]
    moe_grad = own_row[...]
    for off in (1, 2, 3):
        taken = taken + dots_in[off - 1]
    for at in (1, 2):
        moe_grad = moe_grad + row_in[at].astype(F32)
    taken = jnp.concatenate([taken, jnp.zeros((112, 128), F32)], axis=0).T
    own_probs = probs[y_at]
    select = taken - own_probs * jnp.sum(taken, axis=1, keepdims=True)
    select = select.astype(LOW)
    moe_grad = moe_grad + dot(select, router[...])
    router_grad = dot(x_t[:, lane_block(y_at)], select)
    normal = middle[...]
    ffn_r = lax.rsqrt(jnp.mean(normal * normal, axis=1, keepdims=True) + EPS)
    scaled = moe_grad * ffn_gain[...]
    ffn_gain_grad = jnp.sum(moe_grad * normal * ffn_r, axis=0, keepdims=True)
    shrink = ffn_r * ffn_r * ffn_r * jnp.mean(scaled * normal, axis=1, keepdims=True)
    cot[...] = cot[...] + ffn_r * scaled - normal * shrink
    attn_grad = cot[...].astype(LOW)
    for part in (0, 1):
        loads[("bwd", 4 + part)].wait()
    head_grad = dot_nt(attn_grad[:, 0:WIDE], square(weights, 3)) + dot_nt(attn_grad[:, WIDE:], square(weights, 4))
    head_low = head_grad.astype(LOW).astype(F32)
    run(13)

    def head_ref(c):
        return x_t.at[lane_block(c % 2, 512), lane_block(1 + c // 2)]

    for c in range(4):
        head_ref(c)[...] = four_heads(head_low[:, c * 256 : c * 256 + 128], head_low[:, c * 256 + 128 : c * 256 + 256])
    x_t[:, 0:128] = attn_grad.T
    for part in (0, 1):
        weight_grad(OUT_UNIT + part, x_t.at[:, pl.ds(0, 128)], lambda: joined[:, half[part]])
    run(14)

    key_sums, value_sums = pair_in.at[0], pair_in.at[3]
    def attend_back(c):
        heads = head_ref(c)[...]
        low = prob_ref(c)[...].reshape(512, 512)
        soft = low.astype(F32)
        weighted = soft * dot_nt(value_block(c), heads)
        sums = jnp.sum(weighted, axis=0, keepdims=True)
        score_grad = ((weighted - soft * sums) * 0.125).astype(LOW)
        value_sums[:, :, :, lane_block(c)] = dot(low, heads).astype(LOW).reshape(4, 4, 32, 128)
        key_part = turn(dot(score_grad, q_four[c]), cosine[...], sine[...], -1.0)
        key_sums[:, :, :, lane_block(c)] = key_part.astype(LOW).reshape(4, 4, 32, 128)
        first, second = unfold_heads(dot_tn(key_block(c), score_grad))
        own_cosine, own_sine = cosine[own_rows, :], sine[own_rows, :]
        q_low[:, lane_block(2 * c)] = turn(first, own_cosine, own_sine, -1.0).astype(LOW)
        q_low[:, lane_block(2 * c + 1)] = turn(second, own_cosine, own_sine, -1.0).astype(LOW)

    for c in range(4):
        attend_back(c)
        run(15 + c)
    q_copies = [y_copy(off, q_low.at[:, lane_block(across_block(off), 256)], q_all.at[y_at]) for off in (1, 3, 2)]
    start(q_copies)
    q_all[y_at] = q_low[:, lane_block(y_at, 256)]
    weight_grad(KEY_UNIT, normed_t, lambda: key_sums[...].reshape(512, WIDE))
    run(19)
    weight_grad(VALUE_UNIT, normed_t, lambda: value_sums[...].reshape(512, WIDE))
    run(20)

    for part in (0, 1, 2, 3):
        loads[("bwd", part)].wait()
    gain_rows = jnp.zeros((1, 1024), F32)
    for part in (0, 1):
        blocks = pl.ds(2 * part, 2)
        rows = dot_nt(key_sums[blocks].reshape(256, WIDE), square(weights, 2))
        rows = rows + dot_nt(value_sums[blocks].reshape(256, WIDE), square(weights, 5))
        row_send[blocks] = rows.astype(LOW).reshape(2, 128, 1024)
        scaled = rows * normed_all[blocks].reshape(256, 1024).astype(F32)
        gain_rows = gain_rows + jnp.sum(scaled, axis=0, keepdims=True)
    grad_back = Scatter(
        y_at, y_copy, lambda block, part: row_send.at[block, pl.ds(64 * part, 64)], lambda at, part: grad_in.at[at, pl.ds(64 * part, 64)]
    )
    grad_back.start()
    rows = dot_nt(q_low[:, 0:WIDE], square(weights, 0)) + dot_nt(q_low[:, WIDE:], square(weights, 1))
    input_grad[...] = rows
    gain_rows = gain_rows + jnp.sum(rows * normed_all[y_at].astype(F32), axis=0, keepdims=True)
    wide_lane = lanes_of((1024, 128))
    gains = jnp.where(
        wide_lane == EXPERTS,
        jnp.broadcast_to(gain_rows / attn_gain[...], (128, 1024)).T,
        jnp.broadcast_to(ffn_gain_grad, (128, 1024)).T,
    )
    gains = jnp.where(wide_lane < EXPERTS, router_grad, gains).astype(LOW)
    misc[0, :, :, :, :, 256:] = gains.reshape(4, 4, 2, 32, 128)
    run(21)
    wait(q_copies)
    misc[0, :, :, :, :, 0:256] = dot(normed_t[...], q_all[...].reshape(512, 256)).astype(LOW).reshape(4, 4, 2, 32, 256)
    units[UNITS].begin()
    run(22)
    grad_back.turn()
    mix_back.start()
    run(23)

    grad_back.finish()
    normed_grad = input_grad[...] + row_send[y_at].astype(F32) + grad_in[1].astype(F32) + grad_in[2].astype(F32)
    hidden = tokens[...].astype(F32)
    attn_r = lax.rsqrt(jnp.mean(hidden * hidden, axis=1, keepdims=True) + EPS)
    scaled = normed_grad * attn_gain[...]
    shrink = attn_r * attn_r * attn_r * jnp.mean(scaled * hidden, axis=1, keepdims=True)
    input_grad[...] = cot[...] + attn_r * scaled - hidden * shrink
    results = {}

    def result(src, dst):
        copy = pltpu.make_async_copy(src, dst, local_sem.at[len(loads) + len(results)])
        results[len(results)] = copy
        copy.start()

    result(input_grad, input_to)

    def finish_mix():
        mix_back.finish()
        total = middle[...] + x_all[y_at].astype(F32)
        for at in (1, 2):
            total = total + mix_in[at].astype(F32)
        hidden_out[...] = total
        result(hidden_out, hidden_to)

    extras[0] = mix_back.turn
    extras[1] = finish_mix
    run(24)
    result(expert_out, expert_to)
    run(25)
    for src, dst in ((query_out, query_to), (key_out, key_to), (value_out, value_to), (out_out, out_to), (misc_out, misc_to)):
        result(src, dst)
    wait(results.values())


def layer(*args):
    smem = pl.BlockSpec(memory_space=pltpu.SMEM)
    far = pl.BlockSpec(memory_space=pl.ANY)
    low = lambda *shape: pltpu.VMEM(shape, LOW)
    wide = lambda *shape: pltpu.VMEM(shape, F32)
    sems = pltpu.SemaphoreType.DMA
    scratch = [
        wide(128, 1024), wide(128, 1024), wide(EXPERT_UNITS, 32, WIDE),
        wide(8, 1024), wide(8, WIDE), wide(8, WIDE), wide(8, 1024), wide(8, 128),
        low(128, 1024), pltpu.VMEM((8, 128), jnp.int32), pltpu.VMEM((1, 128), jnp.int32),
        wide(1, 1024), wide(1, 1024), low(EXPERTS, 1024),
        low(SLOT_COUNT, *BIG), low(6, *BIG), low(3, 512, 1024), low(128, 1024), wide(128, 1024), wide(512, 128), wide(512, 128),
        low(4, 128, 1024), low(128, 1024), low(4, 512, 128),
        low(4, 128, 1024), low(4, 128, 1024), low(4, 128, 1024), low(4, 128, 128),
        low(1024, 512), low(1024, 512), wide(4, 128, 128), wide(512, 128), wide(512, 128),
        wide(4, 16, 128), wide(3, 16, 128), low(4, 128, 1024), low(3, 128, 1024), low(3, 128, 1024),
        low(128, 1024), low(4, 128, 256), low(3, 128, 1024),
    ]
    for count, width in ((UNITS, WIDE), (1, NARROW)):
        if count == 1:
            scratch += [low(1, 4, 4, 2, 32, width)]
        scratch += [low(count, 4, 4, 32, width), low(count, 2, 32, width), low(count, 2, 32, width)]
        scratch += [low(count, 4, 32, width), low(count, 4, 32, width)]
        scratch += [low(count, 16, width), low(count, 16, width), low(count, 32, width), low(count, 32, width)]
        shared = count - EXPERT_UNITS if count == UNITS else 1
        scratch += [wide(shared, 32, width), wide(3, shared, 8, width)]
    scratch += [sems((48,)), sems((48,)), sems((UNITS + 1, 16)), sems((UNITS + 1, 16)), sems((32,))]
    shape = jax.ShapeDtypeStruct
    return pl.pallas_call(
        layer_kernel,
        out_shape=(
            shape((128, 1024), F32),
            shape((128, 1024), F32),
            shape((EXPERT_UNITS, 32, WIDE), F32),
            shape((8, 1024), F32),
            shape((8, WIDE), F32),
            shape((8, WIDE), F32),
            shape((8, 1024), F32),
            shape((8, 128), F32),
        ),
        in_specs=[smem] + [far] * 16,
        out_specs=(far,) * 8,
        scratch_shapes=scratch,
        compiler_params=pltpu.CompilerParams(
            collective_id=0, has_side_effects=True, vmem_limit_bytes=60 * 2**20
        ),
        name="layer",
    )(*args)


def place_kernel(
    hidden_in, input_in, experts_in, query_in, key_in, value_in, out_in, misc_in,
    hidden_out, input_grad, attn_gain, query, key, value, out, ffn_gain, router, gate, up, down,
):
    hidden_out[...] = hidden_in[...]
    input_grad[...] = input_in[...]
    for kind, to in enumerate((gate, up, down)):
        to[...] = experts_in[3 * kind : 3 * kind + 3]
    for src, to in ((query_in, query), (key_in, key), (value_in, value), (out_in, out)):
        to[...] = src[...]
    router[...] = misc_in[:, 0:EXPERTS]
    flipped = jnp.concatenate([misc_in[...], jnp.zeros((120, 128), F32)], axis=0).T
    attn_gain[...] = flipped[EXPERTS : EXPERTS + 1, 0:8]
    ffn_gain[...] = flipped[EXPERTS + 1 : EXPERTS + 2, 0:8]


def place(*results):
    vmem = pl.BlockSpec(memory_space=pltpu.VMEM)
    shape = lambda *dims: jax.ShapeDtypeStruct(dims, F32)
    return pl.pallas_call(
        place_kernel,
        out_shape=(
            shape(128, 1024), shape(128, 1024), shape(1, 8), shape(8, 1024), shape(8, WIDE), shape(8, WIDE), shape(8, 1024),
            shape(1, 8), shape(8, EXPERTS), shape(3, 32, WIDE), shape(3, 32, WIDE), shape(3, 32, WIDE),
        ),
        in_specs=[vmem] * 8,
        out_specs=(vmem,) * 12,
        name="place",
    )(*results)


def rope_tables(length):
    inverse = np.float32(10000.0) ** (-np.arange(32, dtype=np.float32) / np.float32(32))
    angles = np.arange(length, dtype=np.float32)[:, None] * inverse[None, :]
    cosine, sine = np.cos(angles), np.sin(angles)
    return np.tile(cosine, (1, 4)), np.concatenate([-sine, sine, -sine, sine], axis=1)


def per_device(
    tokens, routes, slot_order, prefix, attn_gain, w_query, w_key, w_value, w_out, ffn_gain, w_router,
    w_gate, w_up, w_down, cotangent,
):
    cosine, sine = rope_tables(512)
    results = layer(
        prefix, tokens, routes[0].T, slot_order[0], attn_gain, ffn_gain, w_router[0].T,
        w_query.reshape(4, 4, 2, 32, 1024), w_key.reshape(BIG), w_value.reshape(BIG), w_out.reshape(4, 4, 2, 32, 1024),
        w_gate.reshape(3, *BIG), w_up.reshape(3, *BIG), w_down[0], cotangent, jnp.asarray(cosine), jnp.asarray(sine),
    )
    hidden_out, input_grad, gain_attn, query, key, value, out, gain_ffn, router, gate, up, down = place(*results)
    return (
        hidden_out, input_grad, gain_attn, query[None], key[None], value[None], out.T[None], gain_ffn, router[None],
        gate[None], up[None], down.transpose(0, 2, 1)[None],
    )


def solution(mesh):
    both = ("group", "expert")
    in_specs = (
        P(both, None), P(None, both, None), P(None, both, None), P("group"), P(), P(), P(), P(), P(), P(), P(),
        P(None, "expert", None, None), P(None, "expert", None, None), P(None, "expert", None, None), P(both, None),
    )
    out_specs = (
        P(both, None), P(both, None), P(None, both), P(None, both, None), P(None, both, None), P(None, both, None),
        P(None, None, both), P(None, both), P(None, both, None), P(None, "expert", "group", None),
        P(None, "expert", "group", None), P(None, "expert", None, "group"),
    )
    return jax.shard_map(per_device, mesh=mesh, in_specs=in_specs, out_specs=out_specs, check_vma=False)
```

```python
import jax
import jax.numpy as jnp
import numpy as np
from jax import lax
from jax.experimental import pallas as pl
from jax.experimental.pallas import tpu as pltpu
from jax.sharding import PartitionSpec as P

MESH = pl.DeviceIdType.MESH
LOW = jnp.bfloat16
F32 = jnp.float32
EPS = 1e-06
CAP = 96
EXPERTS = 12
OWN_EXPERTS = 3
EXPERT_UNITS = 9
UNITS = 13
WIDE, NARROW = 512, 384
KV_UNIT, OUT_UNIT = 9, 11
SLOTS = (0, 1, 2, 3, 4, 5, 6, 7, 8, 9, 10, 13, 14)
PROBS, SLABS, SLOT_COUNT = 9, 11, 16
BIG = (4, 4, 2, 32, WIDE)


PLAN = (
    (),
    (),
    (),
    ((0, 0),),
    ((0, 3), (0, 6)),
    (),
    (),
    ((1, 0),),
    (),
    (),
    (),
    ((1, 3), (0, 1)),
    ((1, 6), (0, 4), (0, 7), (2, 0), (0, 2), (0, 5)),
    ((2, 3), (0, 8)),
    ((2, 6), (1, 1)),
    ((1, 4), (1, 7)),
    ((1, 2),),
    ((5, 0),),
    ((0, 11), (5, 3)),
    (),
    ((0, 12), (1, 5), (1, 8)),
    ((2, 1), (2, 4)),
    (
        (0, 10), (1, 11), (1, 12), (2, 7), (2, 2), (0, 13), (1, 9), (3, 0), (3, 3), (2, 5), (2, 8), (1, 10),
        (5, 1), (5, 4), (3, 6),
    ),
    ((2, 12), (2, 11), (1, 13), (5, 7), (5, 2), (2, 10), (5, 5), (2, 9), (3, 1)),
    ((3, 11), (5, 8), (3, 12), (2, 13), (3, 9), (3, 10), (3, 7), (3, 4), (3, 13), (3, 5), (3, 2), (3, 8)),
    ((6, 1), (4, 11), (4, 12), (4, 9), (4, 10), (4, 13)),
    (),
    (),
    ((6, 0), (5, 6)),
    ((0, 9),),
)


def group_of(x_at, z_at, core):
    return x_at * 8 + z_at * 2 + core


def dot(first, second):
    return jnp.dot(first, second, preferred_element_type=F32)


def dot_nt(first, second):
    return lax.dot_general(first, second, (((1,), (1,)), ((), ())), preferred_element_type=F32)


def dot_tn(first, second):
    return lax.dot_general(first, second, (((0,), (0,)), ((), ())), preferred_element_type=F32)


def add(first, second):
    return first + second


def lanes_of(shape):
    return lax.broadcasted_iota(jnp.int32, shape, len(shape) - 1)


def turn(values, cosine, sine, sign):
    first = lanes_of((values.shape[0], 128)) % 64 < 32
    parts = []
    for at in range(values.shape[1] // 128):
        part = values[:, at * 128 : at * 128 + 128]
        swapped = jnp.where(first, pltpu.roll(part, 96, 1), pltpu.roll(part, 32, 1))
        parts.append(part * cosine + sign * (swapped * sine))
    return parts[0] if len(parts) == 1 else jnp.concatenate(parts, axis=1)


def four_heads(first, second):
    low_half = lanes_of((128, 128)) < 64
    zero = jnp.zeros((128, 128), F32)
    return jnp.concatenate(
        [
            jnp.where(low_half, first, zero),
            jnp.where(low_half, pltpu.roll(first, 64, 1), zero),
            jnp.where(low_half, zero, pltpu.roll(second, 64, 1)),
            jnp.where(low_half, zero, second),
        ],
        axis=0,
    ).astype(LOW)


def unfold_heads(stood):
    first = jnp.concatenate([stood[0:64, 0:128], stood[0:64, 128:256]], axis=0)
    second = jnp.concatenate([stood[64:128, 256:384], stood[64:128, 384:512]], axis=0)
    return first.T, second.T


def loop(count, body):
    def step(index, carry):
        body(index)
        return carry

    lax.fori_loop(0, count, step, 0)


def lane_block(index, width=128):
    return pl.ds(pl.multiple_of(index * width, width), width)


def layer_kernel(
    prefix, tokens_far, routes_far, order_far, attn_gain_far, ffn_gain_far, w_router_far,
    wq_far, wk_far, wv_far, wo_far, wg_far, wu_far, wd_far, cot_far, cos_far, sin_far,
    hidden_to, input_to, expert_to, query_to, key_to, value_to, out_to, misc_to,
    hidden_out, input_grad, expert_out, query_out, key_out, value_out, out_out, misc_out,
    tokens, routes, order, attn_gain, ffn_gain, w_router,
    grads, weights, wd, router, cot, cosine, sine,
    normed_all, joined, q_four, kv_all, x_all, g_all, code_all, codes,
    x_t, g_t, probs, gates, own_dots, dots_send, dots_in, row_send, row_in, mix_in, q_low, q_all, grad_in,
    pair_in, lo_in, hi_in, minus_in, plus_in, cells_in, last, last_in,
    misc, misc_pair, misc_lo, misc_hi, misc_minus, misc_plus, misc_cells,
    misc_last, misc_last_in,
    y_send, y_recv, send_sem, recv_sem, local_sem,
):
    group = lax.axis_index("group")
    y_at = lax.axis_index("expert")
    x_at, z_at, core = group // 8, (group // 2) % 4, group % 2
    spots = (x_at, z_at)
    own_rows = pl.ds(pl.multiple_of(y_at * 128, 128), 128)
    middle, own_row, normed_t = hidden_out, input_grad, g_t

    def device(axis, offset):
        if axis == 0:
            return (group_of((x_at + offset) % 4, z_at, core), y_at)
        return (group_of(x_at, (z_at + offset) % 4, core), y_at)

    def across(offset):
        return (group, (y_at + offset) % 4)

    partner = (group_of(x_at, z_at, 1 - core), y_at)
    barrier = pltpu.get_barrier_semaphore()
    peers = [partner] + [device(axis, off) for axis in (0, 1) for off in (1, 3)]
    peers += [across(off) for off in (1, 2, 3)]
    for peer in peers:
        pl.semaphore_signal(barrier, inc=1, device_id=peer, device_id_type=MESH)

    half = pl.ds(0, WIDE), pl.ds(WIDE, WIDE)
    loads = {}

    def load(name, src, dst):
        copy = pltpu.make_async_copy(src, dst, local_sem.at[len(loads)])
        loads[name] = copy
        copy.start()

    def load_keys(tag, ref, wk_to, wv_to):
        load((tag, 0), wk_far, ref.at[wk_to])
        load((tag, 1), wv_far, ref.at[wv_to])

    def load_pair(tag, at, src, ref, to):
        for part in (0, 1):
            load((tag, at + part), src.at[:, :, :, :, half[part]], ref.at[to + part])

    small = (
        (tokens_far, tokens), (attn_gain_far, attn_gain), (routes_far, routes), (order_far, order),
        (ffn_gain_far, ffn_gain), (w_router_far, w_router),
    )
    for at, (src, dst) in enumerate(small):
        load(("small", at), src, dst)
    load_pair("fwd", 2, wq_far, grads, 2)
    load("cos", cos_far, cosine)
    load("sin", sin_far, sine)
    load_keys("fwd", grads, 0, 1)

    def square(ref, unit):
        return ref[unit].reshape(1024, WIDE)

    def slab(index, rows=None):
        unit, top = SLABS + index // 2, (index % 2) * 2
        if rows is None:
            return grads.at[unit, pl.ds(top, 2)]
        kind, at = rows
        if kind == 256:
            return grads.at[unit, top + at]
        return grads.at[unit, top + at // 2, pl.ds((at % 2) * 2, 2)]

    for at in (0, 1):
        loads[("small", at)].wait()
    hidden = tokens[...].astype(F32)
    attn_r = lax.rsqrt(jnp.mean(hidden * hidden, axis=1, keepdims=True) + EPS)
    normed_all[y_at] = (hidden * attn_r * attn_gain[...]).astype(LOW)
    for at in (2, 3):
        loads[("small", at)].wait()
    expert_at = lax.broadcasted_iota(jnp.int32, (128, 128), 0)
    member = jnp.zeros((128, 128), F32)
    for pick in range(routes.shape[0]):
        member = member + jnp.where(routes[pick : pick + 1, :] == expert_at, 1.0, 0.0)
    member = member.T
    ranks = jnp.broadcast_to(order[...].astype(F32), (128, 128))
    earlier = jnp.where(ranks < ranks.T, 1.0, 0.0).astype(LOW)
    before = dot(earlier, member.astype(LOW))
    code = jnp.where((member > 0.5) & (before < CAP - 0.5), 2.0, member)
    code_all[y_at] = code.T[0:16].astype(LOW)
    pl.semaphore_wait(barrier, len(peers))

    y_used = []

    def y_copy(off, src, dst):
        at = len(y_used)
        y_used.append(off)
        return pltpu.make_async_remote_copy(
            src_ref=src, dst_ref=dst, send_sem=y_send.at[at], recv_sem=y_recv.at[at],
            device_id=across(off), device_id_type=MESH,
        )

    def start(copies):
        for copy in copies:
            copy.start()

    def wait(copies):
        for copy in copies:
            copy.wait()

    left, right = (y_at + 3) % 4, (y_at + 1) % 4
    low_rows, high_rows = pl.ds(0, 64), pl.ds(64, 64)

    class Gather:
        def __init__(self, ref):
            def pass_on(block, rows, off):
                return y_copy(off, ref.at[block, rows], ref.at[block, rows])

            self.first = [pass_on(y_at, low_rows, 1), pass_on(y_at, high_rows, 3)]
            self.first += [pass_on(y_at, high_rows, 1), pass_on(y_at, low_rows, 3)]
            self.second = [pass_on(left, low_rows, 1), pass_on(right, high_rows, 3)]

        def start(self):
            start(self.first)

        def forward(self):
            for came, on in zip(self.first, self.second):
                came.wait_recv()
                on.start()

        def near(self):
            for copy in self.first[2:]:
                copy.wait_recv()

        def finish(self):
            for copy in self.first:
                copy.wait_send()
            wait(self.second)

    class Scatter:
        def __init__(self, spot, send, block, land):
            self.block, self.land = block, land
            far, self.right, self.left = (spot + 2) % 4, (spot + 1) % 4, (spot + 3) % 4
            self.far = [send(1, block(far, 0), land(0, 0)), send(3, block(far, 1), land(0, 1))]
            self.near = [send(1, block(self.right, 1), land(1, 1)), send(3, block(self.left, 0), land(2, 0))]
            self.last = [send(1, block(self.right, 0), land(1, 0)), send(3, block(self.left, 1), land(2, 1))]

        def start(self):
            start(self.far)
            start(self.near)

        def turn(self):
            for part, to in ((0, self.right), (1, self.left)):
                self.far[part].wait()
                ref = self.block(to, part)
                ref[...] = add(ref[...], self.land(0, part)[...])
                self.last[part].start()

        def finish(self):
            wait(self.near)
            wait(self.last)

    normed_share = Gather(normed_all)
    normed_share.start()
    code_share = [y_copy(off, code_all.at[y_at], code_all.at[y_at]) for off in (1, 3, 2)]
    start(code_share)
    load_pair("fwd", 4, wo_far, grads, 4)
    load("cot", cot_far, cot)
    load("wg", wg_far, weights.at[pl.ds(0, 3)])
    load("wu", wu_far, weights.at[pl.ds(3, 3)])
    load("wd", wd_far, wd)

    for name in ("cos", "sin", ("small", 4), ("small", 5)):
        loads[name].wait()
    for part in (0, 1):
        loads[("fwd", 2 + part)].wait()
        turned = turn(dot(normed_all[y_at], square(grads, 2 + part)), cosine[own_rows, :], sine[own_rows, :], 1.0)
        turned = turned.astype(LOW).astype(F32)
        for c in (0, 1):
            q_four[part * 2 + c] = four_heads(
                turned[:, c * 256 : c * 256 + 128], turned[:, c * 256 + 128 : c * 256 + 256]
            )

    loads["cot"].wait()
    g_all[y_at] = cot[...].astype(LOW)
    router[...] = jnp.zeros_like(router)
    router[0:EXPERTS, :] = w_router[...]
    for part in (0, 1):
        loads[("fwd", part)].wait()
    normed_share.forward()
    g_share = Gather(g_all)
    g_share.start()
    normed_share.near()
    normed_share.finish()

    def keys_values(part):
        lanes = lane_block(part, 256)
        inputs = normed_all[...].reshape(512, 1024)
        keys = turn(dot(inputs, grads[0, :, :, :, :, lanes].reshape(1024, 256)), cosine[...], sine[...], 1.0)
        kv_all[:, :, lanes] = keys.astype(LOW).reshape(4, 128, 256)
        values = dot(inputs, grads[1, :, :, :, :, lanes].reshape(1024, 256))
        kv_all[:, :, lane_block(2 + part, 256)] = values.astype(LOW).reshape(4, 128, 256)

    loop(2, keys_values)

    def visible():
        shape = (512, 512)
        key_at = lax.broadcasted_iota(jnp.int32, shape, 0)
        query_at = y_at * 128 + lanes_of(shape) % 128
        return (key_at < prefix[0]) | (key_at <= query_at)

    def key_block(c):
        return kv_all[:, :, lane_block(c)].reshape(512, 128)

    def value_block(c):
        return kv_all[:, :, lane_block(c + 4)].reshape(512, 128)

    def prob_ref(c):
        return grads.at[PROBS + c // 2, pl.ds((c % 2) * 2, 2)]

    def attend(c):
        scores = jnp.where(visible(), dot_nt(key_block(c), q_four[c]) * 0.125, -1e30)
        raised = jnp.exp(scores - jnp.max(scores, axis=0, keepdims=True))
        soft = (raised * (1.0 / jnp.sum(raised, axis=0, keepdims=True))).astype(LOW)
        prob_ref(c)[...] = soft.reshape(2, 4, 2, 32, WIDE)
        first, second = unfold_heads(dot_tn(value_block(c), soft))
        joined[:, lane_block(2 * c)] = first.astype(LOW)
        joined[:, lane_block(2 * c + 1)] = second.astype(LOW)

    loop(4, attend)
    loads[("fwd", 4)].wait()
    loads[("fwd", 5)].wait()
    for part in (0, 1):
        middle[:, half[part]] = tokens[:, half[part]].astype(F32) + dot(joined[...], square(grads, 4 + part))
    ffn_r = lax.rsqrt(jnp.mean(middle[...] * middle[...], axis=1, keepdims=True) + EPS)
    x_all[y_at] = (middle[...] * ffn_r * ffn_gain[...]).astype(LOW)
    x_share = Gather(x_all)
    x_share.start()

    wait(code_share)
    for block in range(4):
        short = code_all[block].astype(F32)
        codes[block] = jnp.concatenate([short, jnp.zeros((112, 128), F32)], axis=0).T

    def stand(ref, out):
        def body(block):
            out[:, lane_block(block)] = ref[block].T

        loop(4, body)

    x_share.forward()
    g_share.forward()
    for name in ("wg", "wu", "wd"):
        loads[name].wait()
    slab_shape = (2, 4, 2, 32, 256)

    def gate_of(j, rows=pl.ds(0, 512), count=512):
        here = lanes_of((count, 128)) == y_at * OWN_EXPERTS + j
        return here, jnp.sum(jnp.where(here, gates[rows, :], 0.0), axis=1, keepdims=True)

    def expert_forward(blocks):
        def rows_of(ref):
            return jnp.concatenate([ref[block] for block in blocks], axis=0)

        code = rows_of(codes)
        in_use = code > 0.5
        logits = jnp.where(in_use, dot_nt(rows_of(x_all), router[...]), -1e30)
        raised = jnp.where(in_use, jnp.exp(logits - jnp.max(logits, axis=1, keepdims=True)), 0.0)
        soft = raised / jnp.sum(raised, axis=1, keepdims=True)
        kept = jnp.where(code > 1.5, soft, 0.0)
        for at, block in enumerate(blocks):
            probs[block] = soft[128 * at : 128 * at + 128]
            gates[lane_block(block), :] = kept[128 * at : 128 * at + 128]

        def body(step):
            j, lanes = step // 2, lane_block(step % 2, 256)
            inputs = rows_of(x_all)
            gate_lin = dot(inputs, weights[j, :, :, :, :, lanes].reshape(1024, 256))
            up_lin = dot(inputs, weights[3 + j, :, :, :, :, lanes].reshape(1024, 256))
            sig = 1.0 / (1.0 + jnp.exp(-gate_lin))
            silu = gate_lin * sig
            gate = jnp.concatenate([gate_of(j, lane_block(block), 128)[1] for block in blocks], axis=0)
            act = (silu * up_lin).astype(LOW).astype(F32) * gate
            slope = up_lin * sig * (1.0 + gate_lin * (1.0 - sig))
            for index, value in ((6 + j, act), (j, slope), (3 + j, silu)):
                value = value.astype(LOW)
                for at, block in enumerate(blocks):
                    piece = value[128 * at : 128 * at + 128].reshape(2, 2, 32, 256)
                    slab(index, (128, block))[:, :, :, lanes] = piece

        loop(2 * OWN_EXPERTS, body)

    own_dots[...] = jnp.zeros_like(own_dots)
    x_share.near()
    expert_forward((y_at, left, right))
    x_share.finish()
    expert_forward(((y_at + 2) % 4,))

    def expert_back(step):
        j, lanes = step // 2, lane_block(step % 2, 256)
        here, gate = gate_of(j)
        outer = dot_nt(g_all[...].reshape(512, 1024), wd[j, lanes, :])
        act = slab(6 + j)[:, :, :, :, lanes].reshape(512, 256).astype(F32)
        own_dots[...] += jnp.where(here, jnp.sum(act * outer, axis=1, keepdims=True), 0.0)
        outer = outer * gate
        for index in (j, 3 + j):
            slope = slab(index)[:, :, :, :, lanes].reshape(512, 256).astype(F32)
            slab(index)[:, :, :, :, lanes] = (outer * slope).astype(LOW).reshape(slab_shape)

    stand(x_all, x_t)
    g_share.near()
    g_share.finish()
    stand(g_all, g_t)
    loop(2, expert_back)

    class Wide:
        src, pair, lo, hi, minus, plus = grads, pair_in, lo_in, hi_in, minus_in, plus_in
        cells = cells_in

    class Narrow:
        src, pair, lo, hi, minus, plus = misc, misc_pair, misc_lo, misc_hi, misc_minus, misc_plus
        cells = misc_cells

    class Unit:
        def __init__(self, unit):
            self.unit, self.axis, self.used = unit, unit % 2, 0
            self.set, self.at = (Wide, unit) if unit < UNITS else (Narrow, 0)
            s = self.set
            ref = s.src.at[SLOTS[unit] if s is Wide else 0]
            self.ref = ref
            self.pair = self.remote(partner, ref.at[:, :, 1 - core], s.pair.at[self.at])

            def block(index, part):
                halves = pl.ds(2 * part, 2)
                return ref.at[index, halves, core] if self.axis == 0 else ref.at[halves, index, core]

            def land(at, part):
                if at == 0:
                    return (s.lo, s.hi)[part].at[self.at]
                return (s.minus, s.plus)[at - 1].at[self.at, pl.ds(2 * part, 2)]

            def cell(index):
                return ref.at[x_at, index, core] if self.axis == 0 else ref.at[index, z_at, core]

            axis = self.axis
            self.ring = Scatter(spots[axis], lambda off, src, dst: self.remote(device(axis, off), src, dst), block, land)
            spot = spots[1 - axis]
            self.cell, self.cells_in = cell(spot), [s.cells.at[off, self.at] for off in range(3)]
            self.direct = unit >= EXPERT_UNITS
            if self.direct:
                self.cells = [
                    self.remote(device(1 - axis, off), cell((spot + off) % 4), self.cells_in[off - 1]) for off in (1, 3, 2)
                ]
            else:
                self.ring_b = Scatter(
                    spot,
                    lambda off, src, dst: self.remote(device(1 - axis, off), src, dst),
                    lambda index, part: cell(index).at[pl.ds(16 * part, 16)],
                    lambda at, part: self.cells_in[at].at[pl.ds(16 * part, 16)],
                )
            self.own = ref.at[spots[0], :, core] if axis == 0 else ref.at[:, spots[1], core]
            if unit >= EXPERT_UNITS:
                src, dst, at = (last, last_in, unit - EXPERT_UNITS) if s is Wide else (misc_last, misc_last_in, 0)
                self.last, self.last_in = src.at[at], [dst.at[off, at] for off in range(3)]
                self.across = [
                    self.remote(across(off), self.last.at[pl.ds((y_at + off) % 4 * 8, 8)], self.last_in[off - 1])
                    for off in (1, 2, 3)
                ]

        def remote(self, to, src, dst):
            self.used += 1
            return pltpu.make_async_remote_copy(
                src_ref=src, dst_ref=dst, send_sem=send_sem.at[self.unit, self.used - 1],
                recv_sem=recv_sem.at[self.unit, self.used - 1], device_id=to, device_id_type=MESH,
            )

        def begin(self):
            self.pair.start()

        def after_pair(self):
            s = self.set
            self.pair.wait()
            for slab_at in range(4):
                ref = self.ref.at[slab_at, :, core]
                ref[...] = add(ref[...], s.pair[self.at, slab_at])
            self.ring.start()

        def turn(self):
            self.ring.turn()

        def after_ring(self):
            s = self.set
            self.ring.finish()
            total = self.own[...].astype(F32) + s.minus[self.at].astype(F32)
            self.own[...] = (total + s.plus[self.at].astype(F32)).astype(LOW)
            (start(self.cells) if self.direct else self.ring_b.start())

        def turn_b(self):
            self.ring_b.turn()

        def after_cells(self):
            if self.direct:
                wait(self.cells)
            else:
                self.ring_b.finish()
            total = self.cell[...].astype(F32)
            for came in self.cells_in if self.direct else self.cells_in[1:]:
                total = total + came[...].astype(F32)
            if self.unit < EXPERT_UNITS:
                expert_out[self.unit] = total
            else:
                self.last[...] = total
                start(self.across)

        def finish(self):
            wait(self.across)
            total = self.last[pl.ds(pl.multiple_of(y_at * 8, 8), 8), :]
            if self.set is Narrow:
                for off in range(4):
                    rows = self.last_in[off - 1][:, 0:256] if off else total[:, 0:256]
                    query_out[:, lane_block((y_at + 4 - off) % 4, 256)] = rows
            for came in self.last_in:
                total = total + came[...]
            if self.unit in (KV_UNIT, KV_UNIT + 1):
                lanes = lane_block(self.unit - KV_UNIT, 256)
                key_out[:, lanes] = total[:, 0:256]
                value_out[:, lanes] = total[:, 256:]
            elif self.set is Wide:
                out_out[:, half[self.unit - OUT_UNIT]] = total
            else:
                misc_out[...] = total[:, 256:]

    extras = {}
    stages = (Unit.after_pair, Unit.turn, Unit.after_ring, Unit.after_cells, Unit.finish, Unit.turn_b)
    units = [Unit(unit) for unit in range(UNITS + 1)]

    def run(point):
        for stage, unit in PLAN[point]:
            if stage < len(stages):
                stages[stage](units[unit])
            else:
                extras[unit]()

    def weight_grad(unit, left, right):
        grads[SLOTS[unit]] = dot(left[...], right()).astype(LOW).reshape(BIG)
        units[unit].begin()

    def slab_value(index):
        return lambda: slab(index)[...].reshape(512, WIDE)

    def expert_units(j, point):
        for at, (kind, turned_rows) in enumerate(((0, x_t), (3, x_t), (6, g_t))):
            weight_grad(kind + j, turned_rows, slab_value(kind + j))
            run(point + at)

    expert_units(0, 0)
    loop(2, lambda step: expert_back(step + 2))
    run(26)
    loop(2, lambda step: expert_back(step + 4))
    run(27)

    dots_copies = [y_copy(off, dots_send.at[(y_at + off) % 4], dots_in.at[off - 1]) for off in (1, 3, 2)]
    for block in range(4):
        dots_send[block] = own_dots[block * 128 : block * 128 + 128, :].T[0:16, :]
    start(dots_copies)

    def row_part(first, second):
        total = None
        for j in range(OWN_EXPERTS):
            for kind in (0, 3):
                pair = [slab(kind + j, (128, block))[...].reshape(128, WIDE) for block in (first, second)]
                part = dot_nt(jnp.concatenate(pair, axis=0), square(weights, kind + j))
                total = part if total is None else total + part
        return total

    def across_block(off):
        return (y_at + off) % 4

    rows = row_part(across_block(2), across_block(1))
    for off in (2, 1):
        row_send[across_block(off)] = rows[128 * (2 - off) : 128 * (3 - off)].astype(LOW)
    rows_back = Scatter(
        y_at, y_copy, lambda block, part: row_send.at[block, pl.ds(64 * part, 64)], lambda at, part: row_in.at[at, pl.ds(64 * part, 64)]
    )
    start(rows_back.far)
    rows_back.near[0].start()
    run(3)
    rows = row_part(across_block(3), y_at)
    row_send[across_block(3)] = rows[0:128].astype(LOW)
    rows_back.near[1].start()
    own_row[...] = rows[128:256]
    run(4)
    rows_back.turn()
    load_pair("bwd", 4, wo_far, weights, 3)
    load_pair("bwd", 2, wq_far, weights, 0)
    load_keys("bwd", weights, 2, 5)

    expert_units(1, 5)
    expert_units(2, 8)

    def mix_part(part):
        total = None
        for j in range(OWN_EXPERTS):
            piece = dot(slab(6 + j, (256, part))[...].reshape(256, WIDE), wd[j])
            total = piece if total is None else total + piece
        x_all[pl.ds(part * 2, 2)] = total.astype(LOW).reshape(2, 128, 1024)

    loop(2, mix_part)
    run(11)

    def normed_stand(block):
        normed_t[:, lane_block(block)] = normed_all[block].T

    loop(4, normed_stand)
    run(12)

    wait(dots_copies)
    rows_back.finish()
    mix_back = Scatter(
        y_at, y_copy, lambda block, part: x_all.at[block, pl.ds(64 * part, 64)], lambda at, part: mix_in.at[at, pl.ds(64 * part, 64)]
    )
    mix_back.start()
    taken = dots_send[y_at]
    moe_grad = own_row[...]
    for off in (1, 2, 3):
        taken = taken + dots_in[off - 1]
    for at in (1, 2):
        moe_grad = moe_grad + row_in[at].astype(F32)
    taken = jnp.concatenate([taken, jnp.zeros((112, 128), F32)], axis=0).T
    own_probs = probs[y_at]
    select = taken - own_probs * jnp.sum(taken, axis=1, keepdims=True)
    select = select.astype(LOW)
    moe_grad = moe_grad + dot(select, router[...])
    router_grad = dot(x_t[:, lane_block(y_at)], select)
    normal = middle[...]
    ffn_r = lax.rsqrt(jnp.mean(normal * normal, axis=1, keepdims=True) + EPS)
    scaled = moe_grad * ffn_gain[...]
    ffn_gain_grad = jnp.sum(moe_grad * normal * ffn_r, axis=0, keepdims=True)
    shrink = ffn_r * ffn_r * ffn_r * jnp.mean(scaled * normal, axis=1, keepdims=True)
    cot[...] = cot[...] + ffn_r * scaled - normal * shrink
    attn_grad = cot[...].astype(LOW)
    for part in (0, 1):
        loads[("bwd", 4 + part)].wait()
    head_grad = dot_nt(attn_grad[:, 0:WIDE], square(weights, 3)) + dot_nt(attn_grad[:, WIDE:], square(weights, 4))
    head_low = head_grad.astype(LOW).astype(F32)
    run(13)

    def head_ref(c):
        return x_t.at[lane_block(c % 2, 512), lane_block(1 + c // 2)]

    for c in range(4):
        head_ref(c)[...] = four_heads(head_low[:, c * 256 : c * 256 + 128], head_low[:, c * 256 + 128 : c * 256 + 256])
    x_t[:, 0:128] = attn_grad.T
    for part in (0, 1):
        weight_grad(OUT_UNIT + part, x_t.at[:, pl.ds(0, 128)], lambda: joined[:, half[part]])
    run(14)

    extras[0] = mix_back.turn

    key_sums, value_sums = pair_in.at[0], pair_in.at[3]
    def attend_back(c):
        heads = head_ref(c)[...]
        low = prob_ref(c)[...].reshape(512, 512)
        soft = low.astype(F32)
        weighted = soft * dot_nt(value_block(c), heads)
        sums = jnp.sum(weighted, axis=0, keepdims=True)
        score_grad = ((weighted - soft * sums) * 0.125).astype(LOW)
        value_sums[:, :, :, lane_block(c)] = dot(low, heads).astype(LOW).reshape(4, 4, 32, 128)
        key_part = turn(dot(score_grad, q_four[c]), cosine[...], sine[...], -1.0)
        key_sums[:, :, :, lane_block(c)] = key_part.astype(LOW).reshape(4, 4, 32, 128)
        first, second = unfold_heads(dot_tn(key_block(c), score_grad))
        own_cosine, own_sine = cosine[own_rows, :], sine[own_rows, :]
        q_low[:, lane_block(2 * c)] = turn(first, own_cosine, own_sine, -1.0).astype(LOW)
        q_low[:, lane_block(2 * c + 1)] = turn(second, own_cosine, own_sine, -1.0).astype(LOW)

    def kv_columns(part):
        lanes = pl.ds(256 * part, 256)
        return jnp.concatenate([ref[:, :, :, lanes].reshape(512, 256) for ref in (key_sums, value_sums)], axis=1)

    for c in range(4):
        attend_back(c)
        run(15 + c)
        if c % 2 == 1:
            weight_grad(KV_UNIT + c // 2, normed_t, lambda: kv_columns(c // 2))
            run(19 + c // 2)
    q_copies = [y_copy(off, q_low.at[:, lane_block(across_block(off), 256)], q_all.at[y_at]) for off in (1, 3, 2)]
    start(q_copies)
    q_all[y_at] = q_low[:, lane_block(y_at, 256)]

    for part in (0, 1, 2, 3):
        loads[("bwd", part)].wait()
    gain_rows = jnp.zeros((1, 1024), F32)
    for part in (0, 1):
        blocks = pl.ds(2 * part, 2)
        rows = dot_nt(key_sums[blocks].reshape(256, WIDE), square(weights, 2))
        rows = rows + dot_nt(value_sums[blocks].reshape(256, WIDE), square(weights, 5))
        row_send[blocks] = rows.astype(LOW).reshape(2, 128, 1024)
        scaled = rows * normed_all[blocks].reshape(256, 1024).astype(F32)
        gain_rows = gain_rows + jnp.sum(scaled, axis=0, keepdims=True)
        if part == 0:
            run(28)
    grad_back = Scatter(
        y_at, y_copy, lambda block, part: row_send.at[block, pl.ds(64 * part, 64)], lambda at, part: grad_in.at[at, pl.ds(64 * part, 64)]
    )
    grad_back.start()
    run(29)
    rows = dot_nt(q_low[:, 0:WIDE], square(weights, 0)) + dot_nt(q_low[:, WIDE:], square(weights, 1))
    input_grad[...] = rows
    gain_rows = gain_rows + jnp.sum(rows * normed_all[y_at].astype(F32), axis=0, keepdims=True)
    wide_lane = lanes_of((1024, 128))
    gains = jnp.where(
        wide_lane == EXPERTS,
        jnp.broadcast_to(gain_rows / attn_gain[...], (128, 1024)).T,
        jnp.broadcast_to(ffn_gain_grad, (128, 1024)).T,
    )
    gains = jnp.where(wide_lane < EXPERTS, router_grad, gains).astype(LOW)
    misc[0, :, :, :, :, 256:] = gains.reshape(4, 4, 2, 32, 128)
    run(21)
    wait(q_copies)
    misc[0, :, :, :, :, 0:256] = dot(normed_t[...], q_all[...].reshape(512, 256)).astype(LOW).reshape(4, 4, 2, 32, 256)
    units[UNITS].begin()
    run(22)
    grad_back.turn()
    run(23)

    grad_back.finish()
    normed_grad = input_grad[...] + row_send[y_at].astype(F32) + grad_in[1].astype(F32) + grad_in[2].astype(F32)
    hidden = tokens[...].astype(F32)
    attn_r = lax.rsqrt(jnp.mean(hidden * hidden, axis=1, keepdims=True) + EPS)
    scaled = normed_grad * attn_gain[...]
    shrink = attn_r * attn_r * attn_r * jnp.mean(scaled * hidden, axis=1, keepdims=True)
    input_grad[...] = cot[...] + attn_r * scaled - hidden * shrink
    results = {}

    def result(src, dst):
        copy = pltpu.make_async_copy(src, dst, local_sem.at[len(loads) + len(results)])
        results[len(results)] = copy
        copy.start()

    result(input_grad, input_to)

    def finish_mix():
        mix_back.finish()
        total = middle[...] + x_all[y_at].astype(F32)
        for at in (1, 2):
            total = total + mix_in[at].astype(F32)
        hidden_out[...] = total
        result(hidden_out, hidden_to)

    extras[1] = finish_mix
    run(24)
    result(expert_out, expert_to)
    run(25)
    for src, dst in ((query_out, query_to), (key_out, key_to), (value_out, value_to), (out_out, out_to), (misc_out, misc_to)):
        result(src, dst)
    wait(results.values())


def layer(*args):
    smem = pl.BlockSpec(memory_space=pltpu.SMEM)
    far = pl.BlockSpec(memory_space=pl.ANY)
    low = lambda *shape: pltpu.VMEM(shape, LOW)
    wide = lambda *shape: pltpu.VMEM(shape, F32)
    sems = pltpu.SemaphoreType.DMA
    scratch = [
        wide(128, 1024), wide(128, 1024), wide(EXPERT_UNITS, 32, WIDE),
        wide(8, 1024), wide(8, WIDE), wide(8, WIDE), wide(8, 1024), wide(8, 128),
        low(128, 1024), pltpu.VMEM((8, 128), jnp.int32), pltpu.VMEM((1, 128), jnp.int32),
        wide(1, 1024), wide(1, 1024), low(EXPERTS, 1024),
        low(SLOT_COUNT, *BIG), low(6, *BIG), low(3, 512, 1024), low(128, 1024), wide(128, 1024), wide(512, 128), wide(512, 128),
        low(4, 128, 1024), low(128, 1024), low(4, 512, 128),
        low(4, 128, 1024), low(4, 128, 1024), low(4, 128, 1024), low(4, 16, 128), wide(4, 128, 128),
        low(1024, 512), low(1024, 512), wide(4, 128, 128), wide(512, 128), wide(512, 128),
        wide(4, 16, 128), wide(3, 16, 128), low(4, 128, 1024), low(3, 128, 1024), low(3, 128, 1024),
        low(128, 1024), low(4, 128, 256), low(3, 128, 1024),
    ]
    for count, width in ((UNITS, WIDE), (1, NARROW)):
        if count == 1:
            scratch += [low(1, 4, 4, 2, 32, width)]
        scratch += [low(count, 4, 4, 32, width), low(count, 2, 32, width), low(count, 2, 32, width)]
        scratch += [low(count, 4, 32, width), low(count, 4, 32, width)]
        scratch += [low(3, count, 32, width)]
        shared = count - EXPERT_UNITS if count == UNITS else 1
        scratch += [wide(shared, 32, width), wide(3, shared, 8, width)]
    scratch += [sems((48,)), sems((48,)), sems((UNITS + 1, 16)), sems((UNITS + 1, 16)), sems((32,))]
    shape = jax.ShapeDtypeStruct
    return pl.pallas_call(
        layer_kernel,
        out_shape=(
            shape((128, 1024), F32),
            shape((128, 1024), F32),
            shape((EXPERT_UNITS, 32, WIDE), F32),
            shape((8, 1024), F32),
            shape((8, WIDE), F32),
            shape((8, WIDE), F32),
            shape((8, 1024), F32),
            shape((8, 128), F32),
        ),
        in_specs=[smem] + [far] * 16,
        out_specs=(far,) * 8,
        scratch_shapes=scratch,
        compiler_params=pltpu.CompilerParams(
            collective_id=0, has_side_effects=True, vmem_limit_bytes=60 * 2**20
        ),
        name="layer",
    )(*args)


def place_kernel(
    hidden_in, input_in, experts_in, query_in, key_in, value_in, out_in, misc_in,
    hidden_out, input_grad, attn_gain, query, key, value, out, ffn_gain, router, gate, up, down,
):
    hidden_out[...] = hidden_in[...]
    input_grad[...] = input_in[...]
    for kind, to in enumerate((gate, up, down)):
        to[...] = experts_in[3 * kind : 3 * kind + 3]
    for src, to in ((query_in, query), (key_in, key), (value_in, value), (out_in, out)):
        to[...] = src[...]
    router[...] = misc_in[:, 0:EXPERTS]
    flipped = jnp.concatenate([misc_in[...], jnp.zeros((120, 128), F32)], axis=0).T
    attn_gain[...] = flipped[EXPERTS : EXPERTS + 1, 0:8]
    ffn_gain[...] = flipped[EXPERTS + 1 : EXPERTS + 2, 0:8]


def place(*results):
    vmem = pl.BlockSpec(memory_space=pltpu.VMEM)
    shape = lambda *dims: jax.ShapeDtypeStruct(dims, F32)
    return pl.pallas_call(
        place_kernel,
        out_shape=(
            shape(128, 1024), shape(128, 1024), shape(1, 8), shape(8, 1024), shape(8, WIDE), shape(8, WIDE), shape(8, 1024),
            shape(1, 8), shape(8, EXPERTS), shape(3, 32, WIDE), shape(3, 32, WIDE), shape(3, 32, WIDE),
        ),
        in_specs=[vmem] * 8,
        out_specs=(vmem,) * 12,
        name="place",
    )(*results)


def rope_tables(length):
    inverse = np.float32(10000.0) ** (-np.arange(32, dtype=np.float32) / np.float32(32))
    angles = np.arange(length, dtype=np.float32)[:, None] * inverse[None, :]
    cosine, sine = np.cos(angles), np.sin(angles)
    return np.tile(cosine, (1, 4)), np.concatenate([-sine, sine, -sine, sine], axis=1)


def per_device(
    tokens, routes, slot_order, prefix, attn_gain, w_query, w_key, w_value, w_out, ffn_gain, w_router,
    w_gate, w_up, w_down, cotangent,
):
    cosine, sine = rope_tables(512)
    results = layer(
        prefix, tokens, routes[0].T, slot_order[0], attn_gain, ffn_gain, w_router[0].T,
        w_query.reshape(4, 4, 2, 32, 1024), w_key.reshape(BIG), w_value.reshape(BIG), w_out.reshape(4, 4, 2, 32, 1024),
        w_gate.reshape(3, *BIG), w_up.reshape(3, *BIG), w_down[0], cotangent, jnp.asarray(cosine), jnp.asarray(sine),
    )
    hidden_out, input_grad, gain_attn, query, key, value, out, gain_ffn, router, gate, up, down = place(*results)
    return (
        hidden_out, input_grad, gain_attn, query[None], key[None], value[None], out.T[None], gain_ffn, router[None],
        gate[None], up[None], down.transpose(0, 2, 1)[None],
    )


def solution(mesh):
    both = ("group", "expert")
    in_specs = (
        P(both, None), P(None, both, None), P(None, both, None), P("group"), P(), P(), P(), P(), P(), P(), P(),
        P(None, "expert", None, None), P(None, "expert", None, None), P(None, "expert", None, None), P(both, None),
    )
    out_specs = (
        P(both, None), P(both, None), P(None, both), P(None, both, None), P(None, both, None), P(None, both, None),
        P(None, None, both), P(None, both), P(None, both, None), P(None, "expert", "group", None),
        P(None, "expert", "group", None), P(None, "expert", None, "group"),
    )
    return jax.shard_map(per_device, mesh=mesh, in_specs=in_specs, out_specs=out_specs, check_vma=False)
```

```python
import jax
import jax.numpy as jnp
import numpy as np
from jax import lax
from jax.experimental import pallas as pl
from jax.experimental.pallas import tpu as pltpu
from jax.sharding import PartitionSpec as P

MESH = pl.DeviceIdType.MESH
LOW = jnp.bfloat16
F32 = jnp.float32
EPS = 1e-06
CAP = 96
EXPERTS = 12
OWN_EXPERTS = 3
EXPERT_UNITS = 9
UNITS = 13
WIDE, NARROW = 512, 384
KV_UNIT, OUT_UNIT = 9, 11
SLOTS = (0, 1, 2, 3, 4, 5, 6, 7, 8, 9, 10, 13, 14)
PROBS, SLABS, SLOT_COUNT = 9, 11, 16
BIG = (4, 4, 2, 32, WIDE)


PLAN = (
    (),
    (),
    (),
    ((0, 0),),
    ((0, 3),),
    ((0, 6),),
    ((1, 0),),
    (),
    (),
    ((1, 3),),
    ((0, 1),),
    ((1, 6), (0, 4)),
    ((0, 7), (2, 0), (2, 3), (0, 2), (0, 5), (1, 1)),
    ((2, 6),),
    ((0, 8),),
    ((1, 7), (1, 4), (5, 0)),
    ((5, 3),),
    (),
    ((0, 11),),
    ((1, 5), (1, 2)),
    ((0, 12),),
    ((2, 1),),
    (
        (0, 10), (1, 12), (1, 11), (6, 0), (2, 7), (1, 9), (2, 4), (2, 5), (0, 13), (2, 2), (3, 0), (3, 3), (5, 1),
        (2, 8), (3, 6),
    ),
    ((1, 10), (2, 9), (2, 11), (1, 13), (2, 12), (5, 4), (5, 7), (5, 5)),
    (
        (2, 10), (3, 9), (2, 13), (3, 12), (3, 11), (3, 10), (5, 2), (5, 8), (3, 13), (3, 1), (3, 4), (3, 7),
        (3, 5), (3, 2), (3, 8),
    ),
    ((6, 1), (4, 9), (4, 12), (4, 11), (4, 10), (4, 13)),
    (),
    (),
    ((5, 6), (1, 8)),
    ((0, 9),),
)


def group_of(x_at, z_at, core):
    return x_at * 8 + z_at * 2 + core


def dot(first, second):
    return jnp.dot(first, second, preferred_element_type=F32)


def dot_nt(first, second):
    return lax.dot_general(first, second, (((1,), (1,)), ((), ())), preferred_element_type=F32)


def dot_tn(first, second):
    return lax.dot_general(first, second, (((0,), (0,)), ((), ())), preferred_element_type=F32)


def add(first, second):
    return first + second


def lanes_of(shape):
    return lax.broadcasted_iota(jnp.int32, shape, len(shape) - 1)


def turn(values, cosine, sine, sign):
    first = lanes_of((values.shape[0], 128)) % 64 < 32
    parts = []
    for at in range(values.shape[1] // 128):
        part = values[:, at * 128 : at * 128 + 128]
        swapped = jnp.where(first, pltpu.roll(part, 96, 1), pltpu.roll(part, 32, 1))
        parts.append(part * cosine + sign * (swapped * sine))
    return parts[0] if len(parts) == 1 else jnp.concatenate(parts, axis=1)


def four_heads(first, second):
    low_half = lanes_of((128, 128)) < 64
    zero = jnp.zeros((128, 128), F32)
    return jnp.concatenate(
        [
            jnp.where(low_half, first, zero),
            jnp.where(low_half, pltpu.roll(first, 64, 1), zero),
            jnp.where(low_half, zero, pltpu.roll(second, 64, 1)),
            jnp.where(low_half, zero, second),
        ],
        axis=0,
    ).astype(LOW)


def unfold_heads(stood):
    first = jnp.concatenate([stood[0:64, 0:128], stood[0:64, 128:256]], axis=0)
    second = jnp.concatenate([stood[64:128, 256:384], stood[64:128, 384:512]], axis=0)
    return first.T, second.T


def loop(count, body):
    def step(index, carry):
        body(index)
        return carry

    lax.fori_loop(0, count, step, 0)


def lane_block(index, width=128):
    return pl.ds(pl.multiple_of(index * width, width), width)


def layer_kernel(
    prefix, tokens_far, routes_far, order_far, attn_gain_far, ffn_gain_far, w_router_far,
    wq_far, wk_far, wv_far, wo_far, wg_far, wu_far, wd_far, cot_far, cos_far, sin_far,
    hidden_to, input_to, expert_to, query_to, key_to, value_to, out_to, misc_to,
    hidden_out, input_grad, expert_out, query_out, key_out, value_out, out_out, misc_out,
    tokens, routes, order, attn_gain, ffn_gain, w_router,
    grads, weights, wd, router, cot, cosine, sine,
    normed_all, joined, q_four, kv_all, x_all, g_all, code_all, codes,
    x_t, g_t, probs, gates, own_dots, dots_send, dots_in, row_send, row_in, mix_in, q_low, q_all, grad_in,
    pair_in, lo_in, hi_in, minus_in, plus_in, cells_in, last, last_in,
    misc, misc_pair, misc_lo, misc_hi, misc_minus, misc_plus, misc_cells,
    misc_last, misc_last_in,
    y_send, y_recv, send_sem, recv_sem, local_sem,
):
    group = lax.axis_index("group")
    y_at = lax.axis_index("expert")
    x_at, z_at, core = group // 8, (group // 2) % 4, group % 2
    spots = (x_at, z_at)
    own_rows = pl.ds(pl.multiple_of(y_at * 128, 128), 128)
    middle, own_row, normed_t = hidden_out, input_grad, g_t

    def device(axis, offset):
        if axis == 0:
            return (group_of((x_at + offset) % 4, z_at, core), y_at)
        return (group_of(x_at, (z_at + offset) % 4, core), y_at)

    def across(offset):
        return (group, (y_at + offset) % 4)

    partner = (group_of(x_at, z_at, 1 - core), y_at)
    barrier = pltpu.get_barrier_semaphore()
    peers = [partner] + [device(axis, off) for axis in (0, 1) for off in (1, 3)]
    peers += [across(off) for off in (1, 2, 3)]
    for peer in peers:
        pl.semaphore_signal(barrier, inc=1, device_id=peer, device_id_type=MESH)

    half = pl.ds(0, WIDE), pl.ds(WIDE, WIDE)
    loads = {}

    def load(name, src, dst):
        copy = pltpu.make_async_copy(src, dst, local_sem.at[len(loads)])
        loads[name] = copy
        copy.start()

    def load_keys(tag, ref, wk_to, wv_to):
        load((tag, 0), wk_far, ref.at[wk_to])
        load((tag, 1), wv_far, ref.at[wv_to])

    def load_pair(tag, at, src, ref, to):
        for part in (0, 1):
            load((tag, at + part), src.at[:, :, :, :, half[part]], ref.at[to + part])

    small = (
        (tokens_far, tokens), (attn_gain_far, attn_gain), (routes_far, routes), (order_far, order),
        (ffn_gain_far, ffn_gain), (w_router_far, w_router),
    )
    for at, (src, dst) in enumerate(small):
        load(("small", at), src, dst)
    load_pair("fwd", 2, wq_far, grads, 2)
    load("cos", cos_far, cosine)
    load("sin", sin_far, sine)
    load_keys("fwd", grads, 0, 1)

    def square(ref, unit):
        return ref[unit].reshape(1024, WIDE)

    def slab(index, rows=None):
        unit, top = SLABS + index // 2, (index % 2) * 2
        if rows is None:
            return grads.at[unit, pl.ds(top, 2)]
        kind, at = rows
        if kind == 256:
            return grads.at[unit, top + at]
        return grads.at[unit, top + at // 2, pl.ds((at % 2) * 2, 2)]

    for at in (0, 1):
        loads[("small", at)].wait()
    hidden = tokens[...].astype(F32)
    attn_r = lax.rsqrt(jnp.mean(hidden * hidden, axis=1, keepdims=True) + EPS)
    normed_all[y_at] = (hidden * attn_r * attn_gain[...]).astype(LOW)
    for at in (2, 3):
        loads[("small", at)].wait()
    expert_at = lax.broadcasted_iota(jnp.int32, (128, 128), 0)
    member = jnp.zeros((128, 128), F32)
    for pick in range(routes.shape[0]):
        member = member + jnp.where(routes[pick : pick + 1, :] == expert_at, 1.0, 0.0)
    member = member.T
    ranks = jnp.broadcast_to(order[...].astype(F32), (128, 128))
    earlier = jnp.where(ranks < ranks.T, 1.0, 0.0).astype(LOW)
    before = dot(earlier, member.astype(LOW))
    code = jnp.where((member > 0.5) & (before < CAP - 0.5), 2.0, member)
    code_all[y_at] = code.T[0:16].astype(LOW)
    pl.semaphore_wait(barrier, len(peers))

    y_used = []

    def y_copy(off, src, dst):
        at = len(y_used)
        y_used.append(off)
        return pltpu.make_async_remote_copy(
            src_ref=src, dst_ref=dst, send_sem=y_send.at[at], recv_sem=y_recv.at[at],
            device_id=across(off), device_id_type=MESH,
        )

    def start(copies):
        for copy in copies:
            copy.start()

    def wait(copies):
        for copy in copies:
            copy.wait()

    left, right = (y_at + 3) % 4, (y_at + 1) % 4
    low_rows, high_rows = pl.ds(0, 64), pl.ds(64, 64)

    class Gather:
        def __init__(self, ref):
            def pass_on(block, rows, off):
                return y_copy(off, ref.at[block, rows], ref.at[block, rows])

            self.first = [pass_on(y_at, low_rows, 1), pass_on(y_at, high_rows, 3)]
            self.first += [pass_on(y_at, high_rows, 1), pass_on(y_at, low_rows, 3)]
            self.second = [pass_on(left, low_rows, 1), pass_on(right, high_rows, 3)]

        def start(self):
            start(self.first)

        def forward(self):
            for came, on in zip(self.first, self.second):
                came.wait_recv()
                on.start()

        def near(self):
            for copy in self.first[2:]:
                copy.wait_recv()

        def finish(self):
            for copy in self.first:
                copy.wait_send()
            wait(self.second)

    class Scatter:
        def __init__(self, spot, send, block, land):
            self.block, self.land = block, land
            far, self.right, self.left = (spot + 2) % 4, (spot + 1) % 4, (spot + 3) % 4
            self.far = [send(1, block(far, 0), land(0, 0)), send(3, block(far, 1), land(0, 1))]
            self.near = [send(1, block(self.right, 1), land(1, 1)), send(3, block(self.left, 0), land(2, 0))]
            self.last = [send(1, block(self.right, 0), land(1, 0)), send(3, block(self.left, 1), land(2, 1))]

        def start(self):
            start(self.far)
            start(self.near)

        def turn(self):
            for part, to in ((0, self.right), (1, self.left)):
                self.far[part].wait()
                ref = self.block(to, part)
                ref[...] = add(ref[...], self.land(0, part)[...])
                self.last[part].start()

        def finish(self):
            wait(self.near)
            wait(self.last)

    normed_share = Gather(normed_all)
    normed_share.start()
    code_share = [y_copy(off, code_all.at[y_at], code_all.at[y_at]) for off in (1, 3, 2)]
    start(code_share)
    load_pair("fwd", 4, wo_far, grads, 4)
    load("cot", cot_far, cot)
    load("wg", wg_far, weights.at[pl.ds(0, 3)])
    load("wu", wu_far, weights.at[pl.ds(3, 3)])
    load("wd", wd_far, wd)

    for name in ("cos", "sin", ("small", 4), ("small", 5)):
        loads[name].wait()
    for part in (0, 1):
        loads[("fwd", 2 + part)].wait()
        turned = turn(dot(normed_all[y_at], square(grads, 2 + part)), cosine[own_rows, :], sine[own_rows, :], 1.0)
        turned = turned.astype(LOW).astype(F32)
        for c in (0, 1):
            q_four[part * 2 + c] = four_heads(
                turned[:, c * 256 : c * 256 + 128], turned[:, c * 256 + 128 : c * 256 + 256]
            )

    loads["cot"].wait()
    g_all[y_at] = cot[...].astype(LOW)
    router[...] = jnp.zeros_like(router)
    router[0:EXPERTS, :] = w_router[...]
    for part in (0, 1):
        loads[("fwd", part)].wait()
    normed_share.forward()
    g_share = Gather(g_all)
    g_share.start()
    normed_share.near()
    normed_share.finish()

    def keys_values(part):
        lanes = lane_block(part, 256)
        inputs = normed_all[...].reshape(512, 1024)
        keys = turn(dot(inputs, grads[0, :, :, :, :, lanes].reshape(1024, 256)), cosine[...], sine[...], 1.0)
        kv_all[:, :, lanes] = keys.astype(LOW).reshape(4, 128, 256)
        values = dot(inputs, grads[1, :, :, :, :, lanes].reshape(1024, 256))
        kv_all[:, :, lane_block(2 + part, 256)] = values.astype(LOW).reshape(4, 128, 256)

    loop(2, keys_values)

    def visible():
        shape = (512, 512)
        key_at = lax.broadcasted_iota(jnp.int32, shape, 0)
        query_at = y_at * 128 + lanes_of(shape) % 128
        return (key_at < prefix[0]) | (key_at <= query_at)

    def key_block(c):
        return kv_all[:, :, lane_block(c)].reshape(512, 128)

    def value_block(c):
        return kv_all[:, :, lane_block(c + 4)].reshape(512, 128)

    def prob_ref(c):
        return grads.at[PROBS + c // 2, pl.ds((c % 2) * 2, 2)]

    def attend(c):
        scores = jnp.where(visible(), dot_nt(key_block(c), q_four[c]) * 0.125, -1e30)
        raised = jnp.exp(scores - jnp.max(scores, axis=0, keepdims=True))
        soft = (raised * (1.0 / jnp.sum(raised, axis=0, keepdims=True))).astype(LOW)
        prob_ref(c)[...] = soft.reshape(2, 4, 2, 32, WIDE)
        first, second = unfold_heads(dot_tn(value_block(c), soft))
        joined[:, lane_block(2 * c)] = first.astype(LOW)
        joined[:, lane_block(2 * c + 1)] = second.astype(LOW)

    loop(4, attend)
    loads[("fwd", 4)].wait()
    loads[("fwd", 5)].wait()
    for part in (0, 1):
        middle[:, half[part]] = tokens[:, half[part]].astype(F32) + dot(joined[...], square(grads, 4 + part))
    ffn_r = lax.rsqrt(jnp.mean(middle[...] * middle[...], axis=1, keepdims=True) + EPS)
    x_all[y_at] = (middle[...] * ffn_r * ffn_gain[...]).astype(LOW)
    x_share = Gather(x_all)
    x_share.start()

    wait(code_share)
    for block in range(4):
        short = code_all[block].astype(F32)
        codes[block] = jnp.concatenate([short, jnp.zeros((112, 128), F32)], axis=0).T

    def stand(ref, out):
        def body(block):
            out[:, lane_block(block)] = ref[block].T

        loop(4, body)

    x_share.forward()
    g_share.forward()
    for name in ("wg", "wu", "wd"):
        loads[name].wait()
    slab_shape = (2, 4, 2, 32, 256)

    def gate_of(j, rows=pl.ds(0, 512), count=512):
        here = lanes_of((count, 128)) == y_at * OWN_EXPERTS + j
        return here, jnp.sum(jnp.where(here, gates[rows, :], 0.0), axis=1, keepdims=True)

    def expert_forward(blocks):
        def rows_of(ref):
            return jnp.concatenate([ref[block] for block in blocks], axis=0)

        code = rows_of(codes)
        in_use = code > 0.5
        logits = jnp.where(in_use, dot_nt(rows_of(x_all), router[...]), -1e30)
        raised = jnp.where(in_use, jnp.exp(logits - jnp.max(logits, axis=1, keepdims=True)), 0.0)
        soft = raised / jnp.sum(raised, axis=1, keepdims=True)
        kept = jnp.where(code > 1.5, soft, 0.0)
        for at, block in enumerate(blocks):
            probs[block] = soft[128 * at : 128 * at + 128]
            gates[lane_block(block), :] = kept[128 * at : 128 * at + 128]

        def body(step):
            j, lanes = step // 2, lane_block(step % 2, 256)
            inputs = rows_of(x_all)
            gate_lin = dot(inputs, weights[j, :, :, :, :, lanes].reshape(1024, 256))
            up_lin = dot(inputs, weights[3 + j, :, :, :, :, lanes].reshape(1024, 256))
            sig = 1.0 / (1.0 + jnp.exp(-gate_lin))
            silu = gate_lin * sig
            gate = jnp.concatenate([gate_of(j, lane_block(block), 128)[1] for block in blocks], axis=0)
            act = (silu * up_lin).astype(LOW).astype(F32) * gate
            slope = up_lin * sig * (1.0 + gate_lin * (1.0 - sig))
            for index, value in ((6 + j, act), (j, slope), (3 + j, silu)):
                value = value.astype(LOW)
                for at, block in enumerate(blocks):
                    piece = value[128 * at : 128 * at + 128].reshape(2, 2, 32, 256)
                    slab(index, (128, block))[:, :, :, lanes] = piece

        loop(2 * OWN_EXPERTS, body)

    own_dots[...] = jnp.zeros_like(own_dots)
    x_share.near()
    expert_forward((y_at, left, right))
    x_share.finish()
    expert_forward(((y_at + 2) % 4,))

    def expert_back(step):
        j, lanes = step // 2, lane_block(step % 2, 256)
        here, gate = gate_of(j)
        outer = dot_nt(g_all[...].reshape(512, 1024), wd[j, lanes, :])
        act = slab(6 + j)[:, :, :, :, lanes].reshape(512, 256).astype(F32)
        own_dots[...] += jnp.where(here, jnp.sum(act * outer, axis=1, keepdims=True), 0.0)
        outer = outer * gate
        for index in (j, 3 + j):
            slope = slab(index)[:, :, :, :, lanes].reshape(512, 256).astype(F32)
            slab(index)[:, :, :, :, lanes] = (outer * slope).astype(LOW).reshape(slab_shape)

    stand(x_all, x_t)
    g_share.near()
    g_share.finish()
    loop(2, expert_back)

    class Wide:
        src, pair, lo, hi, minus, plus = grads, pair_in, lo_in, hi_in, minus_in, plus_in
        cells = cells_in

    class Narrow:
        src, pair, lo, hi, minus, plus = misc, misc_pair, misc_lo, misc_hi, misc_minus, misc_plus
        cells = misc_cells

    class Unit:
        def __init__(self, unit):
            self.unit, self.axis, self.used = unit, unit % 2, 0
            self.set, self.at = (Wide, unit) if unit < UNITS else (Narrow, 0)
            s = self.set
            ref = s.src.at[SLOTS[unit] if s is Wide else 0]
            self.ref = ref
            self.pair = self.remote(partner, ref.at[:, :, 1 - core], s.pair.at[self.at])

            def block(index, part):
                halves = pl.ds(2 * part, 2)
                return ref.at[index, halves, core] if self.axis == 0 else ref.at[halves, index, core]

            def land(at, part):
                if at == 0:
                    return (s.lo, s.hi)[part].at[self.at]
                return (s.minus, s.plus)[at - 1].at[self.at, pl.ds(2 * part, 2)]

            def cell(index):
                return ref.at[x_at, index, core] if self.axis == 0 else ref.at[index, z_at, core]

            axis = self.axis
            self.ring = Scatter(spots[axis], lambda off, src, dst: self.remote(device(axis, off), src, dst), block, land)
            spot = spots[1 - axis]
            self.cell, self.cells_in = cell(spot), [s.cells.at[off, self.at] for off in range(3)]
            self.direct = unit >= EXPERT_UNITS
            if self.direct:
                self.cells = [
                    self.remote(device(1 - axis, off), cell((spot + off) % 4), self.cells_in[off - 1]) for off in (1, 3, 2)
                ]
            else:
                self.ring_b = Scatter(
                    spot,
                    lambda off, src, dst: self.remote(device(1 - axis, off), src, dst),
                    lambda index, part: cell(index).at[pl.ds(16 * part, 16)],
                    lambda at, part: self.cells_in[at].at[pl.ds(16 * part, 16)],
                )
            self.own = ref.at[spots[0], :, core] if axis == 0 else ref.at[:, spots[1], core]
            if unit >= EXPERT_UNITS:
                src, dst, at = (last, last_in, unit - EXPERT_UNITS) if s is Wide else (misc_last, misc_last_in, 0)
                self.last, self.last_in = src.at[at], [dst.at[off, at] for off in range(3)]
                self.across = [
                    self.remote(across(off), self.last.at[pl.ds((y_at + off) % 4 * 8, 8)], self.last_in[off - 1])
                    for off in (1, 2, 3)
                ]

        def remote(self, to, src, dst):
            self.used += 1
            return pltpu.make_async_remote_copy(
                src_ref=src, dst_ref=dst, send_sem=send_sem.at[self.unit, self.used - 1],
                recv_sem=recv_sem.at[self.unit, self.used - 1], device_id=to, device_id_type=MESH,
            )

        def begin(self):
            self.pair.start()

        def after_pair(self):
            s = self.set
            self.pair.wait()
            for slab_at in range(4):
                ref = self.ref.at[slab_at, :, core]
                ref[...] = add(ref[...], s.pair[self.at, slab_at])
            self.ring.start()

        def turn(self):
            self.ring.turn()

        def after_ring(self):
            s = self.set
            self.ring.finish()
            total = self.own[...].astype(F32) + s.minus[self.at].astype(F32)
            self.own[...] = (total + s.plus[self.at].astype(F32)).astype(LOW)
            (start(self.cells) if self.direct else self.ring_b.start())

        def turn_b(self):
            self.ring_b.turn()

        def after_cells(self):
            if self.direct:
                wait(self.cells)
            else:
                self.ring_b.finish()
            total = self.cell[...].astype(F32)
            for came in self.cells_in if self.direct else self.cells_in[1:]:
                total = total + came[...].astype(F32)
            if self.unit < EXPERT_UNITS:
                expert_out[self.unit] = total
            else:
                self.last[...] = total
                start(self.across)

        def finish(self):
            wait(self.across)
            total = self.last[pl.ds(pl.multiple_of(y_at * 8, 8), 8), :]
            if self.set is Narrow:
                for off in range(4):
                    rows = self.last_in[off - 1][:, 0:256] if off else total[:, 0:256]
                    query_out[:, lane_block((y_at + 4 - off) % 4, 256)] = rows
            for came in self.last_in:
                total = total + came[...]
            if self.unit in (KV_UNIT, KV_UNIT + 1):
                lanes = lane_block(self.unit - KV_UNIT, 256)
                key_out[:, lanes] = total[:, 0:256]
                value_out[:, lanes] = total[:, 256:]
            elif self.set is Wide:
                out_out[:, half[self.unit - OUT_UNIT]] = total
            else:
                misc_out[...] = total[:, 256:]

    extras = {}
    stages = (Unit.after_pair, Unit.turn, Unit.after_ring, Unit.after_cells, Unit.finish, Unit.turn_b)
    units = [Unit(unit) for unit in range(UNITS + 1)]

    def run(point):
        for stage, unit in PLAN[point]:
            if stage < len(stages):
                stages[stage](units[unit])
            else:
                extras[unit]()

    def weight_grad(unit, left, right):
        grads[SLOTS[unit]] = dot(left[...], right()).astype(LOW).reshape(BIG)
        units[unit].begin()

    def slab_value(index):
        return lambda: slab(index)[...].reshape(512, WIDE)

    def expert_units(j, point):
        for at, (kind, turned_rows) in enumerate(((0, x_t), (3, x_t), (6, g_t))):
            if kind + j == 6:
                stand(g_all, g_t)
            weight_grad(kind + j, turned_rows, slab_value(kind + j))
            run(point + at)

    expert_units(0, 0)
    loop(2, lambda step: expert_back(step + 2))
    run(26)
    loop(2, lambda step: expert_back(step + 4))
    run(27)

    dots_copies = [y_copy(off, dots_send.at[(y_at + off) % 4], dots_in.at[off - 1]) for off in (1, 3, 2)]
    for block in range(4):
        dots_send[block] = own_dots[block * 128 : block * 128 + 128, :].T[0:16, :]
    start(dots_copies)

    def row_part(first, second):
        total = None
        for j in range(OWN_EXPERTS):
            for kind in (0, 3):
                pair = [slab(kind + j, (128, block))[...].reshape(128, WIDE) for block in (first, second)]
                part = dot_nt(jnp.concatenate(pair, axis=0), square(weights, kind + j))
                total = part if total is None else total + part
        return total

    def across_block(off):
        return (y_at + off) % 4

    rows = row_part(across_block(2), across_block(1))
    for off in (2, 1):
        row_send[across_block(off)] = rows[128 * (2 - off) : 128 * (3 - off)].astype(LOW)
    rows_back = Scatter(
        y_at, y_copy, lambda block, part: row_send.at[block, pl.ds(64 * part, 64)], lambda at, part: row_in.at[at, pl.ds(64 * part, 64)]
    )
    start(rows_back.far)
    rows_back.near[0].start()
    run(3)
    rows = row_part(across_block(3), y_at)
    row_send[across_block(3)] = rows[0:128].astype(LOW)
    rows_back.near[1].start()
    own_row[...] = rows[128:256]
    run(4)
    load_pair("bwd", 4, wo_far, weights, 3)
    load_pair("bwd", 2, wq_far, weights, 0)
    load_keys("bwd", weights, 2, 5)

    expert_units(1, 5)
    rows_back.turn()
    expert_units(2, 8)

    def mix_part(part):
        total = None
        for j in range(OWN_EXPERTS):
            piece = dot(slab(6 + j, (256, part))[...].reshape(256, WIDE), wd[j])
            total = piece if total is None else total + piece
        x_all[pl.ds(part * 2, 2)] = total.astype(LOW).reshape(2, 128, 1024)

    loop(2, mix_part)
    run(11)

    def normed_stand(block):
        normed_t[:, lane_block(block)] = normed_all[block].T

    loop(4, normed_stand)
    run(12)

    wait(dots_copies)
    rows_back.finish()
    mix_back = Scatter(
        y_at, y_copy, lambda block, part: x_all.at[block, pl.ds(64 * part, 64)], lambda at, part: mix_in.at[at, pl.ds(64 * part, 64)]
    )
    mix_back.start()
    taken = dots_send[y_at]
    moe_grad = own_row[...]
    for off in (1, 2, 3):
        taken = taken + dots_in[off - 1]
    for at in (1, 2):
        moe_grad = moe_grad + row_in[at].astype(F32)
    taken = jnp.concatenate([taken, jnp.zeros((112, 128), F32)], axis=0).T
    own_probs = probs[y_at]
    select = taken - own_probs * jnp.sum(taken, axis=1, keepdims=True)
    select = select.astype(LOW)
    moe_grad = moe_grad + dot(select, router[...])
    router_grad = dot(x_t[:, lane_block(y_at)], select)
    normal = middle[...]
    ffn_r = lax.rsqrt(jnp.mean(normal * normal, axis=1, keepdims=True) + EPS)
    scaled = moe_grad * ffn_gain[...]
    ffn_gain_grad = jnp.sum(moe_grad * normal * ffn_r, axis=0, keepdims=True)
    shrink = ffn_r * ffn_r * ffn_r * jnp.mean(scaled * normal, axis=1, keepdims=True)
    cot[...] = cot[...] + ffn_r * scaled - normal * shrink
    attn_grad = cot[...].astype(LOW)
    for part in (0, 1):
        loads[("bwd", 4 + part)].wait()
    head_grad = dot_nt(attn_grad[:, 0:WIDE], square(weights, 3)) + dot_nt(attn_grad[:, WIDE:], square(weights, 4))
    head_low = head_grad.astype(LOW).astype(F32)
    run(13)

    def head_ref(c):
        return x_t.at[lane_block(c % 2, 512), lane_block(1 + c // 2)]

    for c in range(4):
        head_ref(c)[...] = four_heads(head_low[:, c * 256 : c * 256 + 128], head_low[:, c * 256 + 128 : c * 256 + 256])
    x_t[:, 0:128] = attn_grad.T
    for part in (0, 1):
        weight_grad(OUT_UNIT + part, x_t.at[:, pl.ds(0, 128)], lambda: joined[:, half[part]])
    run(14)

    extras[0] = mix_back.turn

    key_sums, value_sums = pair_in.at[0], pair_in.at[3]
    def attend_back(c):
        heads = head_ref(c)[...]
        low = prob_ref(c)[...].reshape(512, 512)
        soft = low.astype(F32)
        weighted = soft * dot_nt(value_block(c), heads)
        sums = jnp.sum(weighted, axis=0, keepdims=True)
        score_grad = ((weighted - soft * sums) * 0.125).astype(LOW)
        value_sums[:, :, :, lane_block(c)] = dot(low, heads).astype(LOW).reshape(4, 4, 32, 128)
        key_part = turn(dot(score_grad, q_four[c]), cosine[...], sine[...], -1.0)
        key_sums[:, :, :, lane_block(c)] = key_part.astype(LOW).reshape(4, 4, 32, 128)
        first, second = unfold_heads(dot_tn(key_block(c), score_grad))
        own_cosine, own_sine = cosine[own_rows, :], sine[own_rows, :]
        q_low[:, lane_block(2 * c)] = turn(first, own_cosine, own_sine, -1.0).astype(LOW)
        q_low[:, lane_block(2 * c + 1)] = turn(second, own_cosine, own_sine, -1.0).astype(LOW)

    def kv_columns(part):
        lanes = pl.ds(256 * part, 256)
        return jnp.concatenate([ref[:, :, :, lanes].reshape(512, 256) for ref in (key_sums, value_sums)], axis=1)

    for c in range(4):
        attend_back(c)
        run(15 + c)
        if c % 2 == 1:
            weight_grad(KV_UNIT + c // 2, normed_t, lambda: kv_columns(c // 2))
            run(19 + c // 2)
    q_copies = [y_copy(off, q_low.at[:, lane_block(across_block(off), 256)], q_all.at[y_at]) for off in (1, 3, 2)]
    start(q_copies)
    q_all[y_at] = q_low[:, lane_block(y_at, 256)]

    for part in (0, 1, 2, 3):
        loads[("bwd", part)].wait()
    gain_rows = jnp.zeros((1, 1024), F32)
    for part in (0, 1):
        blocks = pl.ds(2 * part, 2)
        rows = dot_nt(key_sums[blocks].reshape(256, WIDE), square(weights, 2))
        rows = rows + dot_nt(value_sums[blocks].reshape(256, WIDE), square(weights, 5))
        row_send[blocks] = rows.astype(LOW).reshape(2, 128, 1024)
        scaled = rows * normed_all[blocks].reshape(256, 1024).astype(F32)
        gain_rows = gain_rows + jnp.sum(scaled, axis=0, keepdims=True)
        if part == 0:
            run(28)
    grad_back = Scatter(
        y_at, y_copy, lambda block, part: row_send.at[block, pl.ds(64 * part, 64)], lambda at, part: grad_in.at[at, pl.ds(64 * part, 64)]
    )
    grad_back.start()
    run(29)
    rows = dot_nt(q_low[:, 0:WIDE], square(weights, 0)) + dot_nt(q_low[:, WIDE:], square(weights, 1))
    input_grad[...] = rows
    gain_rows = gain_rows + jnp.sum(rows * normed_all[y_at].astype(F32), axis=0, keepdims=True)
    wide_lane = lanes_of((1024, 128))
    gains = jnp.where(
        wide_lane == EXPERTS,
        jnp.broadcast_to(gain_rows / attn_gain[...], (128, 1024)).T,
        jnp.broadcast_to(ffn_gain_grad, (128, 1024)).T,
    )
    gains = jnp.where(wide_lane < EXPERTS, router_grad, gains).astype(LOW)
    misc[0, :, :, :, :, 256:] = gains.reshape(4, 4, 2, 32, 128)
    run(21)
    wait(q_copies)
    misc[0, :, :, :, :, 0:256] = dot(normed_t[...], q_all[...].reshape(512, 256)).astype(LOW).reshape(4, 4, 2, 32, 256)
    units[UNITS].begin()
    run(22)
    grad_back.turn()
    run(23)

    grad_back.finish()
    normed_grad = input_grad[...] + row_send[y_at].astype(F32) + grad_in[1].astype(F32) + grad_in[2].astype(F32)
    hidden = tokens[...].astype(F32)
    attn_r = lax.rsqrt(jnp.mean(hidden * hidden, axis=1, keepdims=True) + EPS)
    scaled = normed_grad * attn_gain[...]
    shrink = attn_r * attn_r * attn_r * jnp.mean(scaled * hidden, axis=1, keepdims=True)
    input_grad[...] = cot[...] + attn_r * scaled - hidden * shrink
    results = {}

    def result(src, dst):
        copy = pltpu.make_async_copy(src, dst, local_sem.at[len(loads) + len(results)])
        results[len(results)] = copy
        copy.start()

    result(input_grad, input_to)

    def finish_mix():
        mix_back.finish()
        total = middle[...] + x_all[y_at].astype(F32)
        for at in (1, 2):
            total = total + mix_in[at].astype(F32)
        hidden_out[...] = total
        result(hidden_out, hidden_to)

    extras[1] = finish_mix
    run(24)
    result(expert_out, expert_to)
    run(25)
    for src, dst in ((query_out, query_to), (key_out, key_to), (value_out, value_to), (out_out, out_to), (misc_out, misc_to)):
        result(src, dst)
    wait(results.values())


def layer(*args):
    smem = pl.BlockSpec(memory_space=pltpu.SMEM)
    far = pl.BlockSpec(memory_space=pl.ANY)
    low = lambda *shape: pltpu.VMEM(shape, LOW)
    wide = lambda *shape: pltpu.VMEM(shape, F32)
    sems = pltpu.SemaphoreType.DMA
    scratch = [
        wide(128, 1024), wide(128, 1024), wide(EXPERT_UNITS, 32, WIDE),
        wide(8, 1024), wide(8, WIDE), wide(8, WIDE), wide(8, 1024), wide(8, 128),
        low(128, 1024), pltpu.VMEM((8, 128), jnp.int32), pltpu.VMEM((1, 128), jnp.int32),
        wide(1, 1024), wide(1, 1024), low(EXPERTS, 1024),
        low(SLOT_COUNT, *BIG), low(6, *BIG), low(3, 512, 1024), low(128, 1024), wide(128, 1024), wide(512, 128), wide(512, 128),
        low(4, 128, 1024), low(128, 1024), low(4, 512, 128),
        low(4, 128, 1024), low(4, 128, 1024), low(4, 128, 1024), low(4, 16, 128), wide(4, 128, 128),
        low(1024, 512), low(1024, 512), wide(4, 128, 128), wide(512, 128), wide(512, 128),
        wide(4, 16, 128), wide(3, 16, 128), low(4, 128, 1024), low(3, 128, 1024), low(3, 128, 1024),
        low(128, 1024), low(4, 128, 256), low(3, 128, 1024),
    ]
    for count, width in ((UNITS, WIDE), (1, NARROW)):
        if count == 1:
            scratch += [low(1, 4, 4, 2, 32, width)]
        scratch += [low(count, 4, 4, 32, width), low(count, 2, 32, width), low(count, 2, 32, width)]
        scratch += [low(count, 4, 32, width), low(count, 4, 32, width)]
        scratch += [low(3, count, 32, width)]
        shared = count - EXPERT_UNITS if count == UNITS else 1
        scratch += [wide(shared, 32, width), wide(3, shared, 8, width)]
    scratch += [sems((48,)), sems((48,)), sems((UNITS + 1, 16)), sems((UNITS + 1, 16)), sems((32,))]
    shape = jax.ShapeDtypeStruct
    return pl.pallas_call(
        layer_kernel,
        out_shape=(
            shape((128, 1024), F32),
            shape((128, 1024), F32),
            shape((EXPERT_UNITS, 32, WIDE), F32),
            shape((8, 1024), F32),
            shape((8, WIDE), F32),
            shape((8, WIDE), F32),
            shape((8, 1024), F32),
            shape((8, 128), F32),
        ),
        in_specs=[smem] + [far] * 16,
        out_specs=(far,) * 8,
        scratch_shapes=scratch,
        compiler_params=pltpu.CompilerParams(
            collective_id=0, has_side_effects=True, vmem_limit_bytes=60 * 2**20
        ),
        name="layer",
    )(*args)


def place_kernel(
    hidden_in, input_in, experts_in, query_in, key_in, value_in, out_in, misc_in,
    hidden_out, input_grad, attn_gain, query, key, value, out, ffn_gain, router, gate, up, down,
):
    hidden_out[...] = hidden_in[...]
    input_grad[...] = input_in[...]
    for kind, to in enumerate((gate, up, down)):
        to[...] = experts_in[3 * kind : 3 * kind + 3]
    for src, to in ((query_in, query), (key_in, key), (value_in, value), (out_in, out)):
        to[...] = src[...]
    router[...] = misc_in[:, 0:EXPERTS]
    flipped = jnp.concatenate([misc_in[...], jnp.zeros((120, 128), F32)], axis=0).T
    attn_gain[...] = flipped[EXPERTS : EXPERTS + 1, 0:8]
    ffn_gain[...] = flipped[EXPERTS + 1 : EXPERTS + 2, 0:8]


def place(*results):
    vmem = pl.BlockSpec(memory_space=pltpu.VMEM)
    shape = lambda *dims: jax.ShapeDtypeStruct(dims, F32)
    return pl.pallas_call(
        place_kernel,
        out_shape=(
            shape(128, 1024), shape(128, 1024), shape(1, 8), shape(8, 1024), shape(8, WIDE), shape(8, WIDE), shape(8, 1024),
            shape(1, 8), shape(8, EXPERTS), shape(3, 32, WIDE), shape(3, 32, WIDE), shape(3, 32, WIDE),
        ),
        in_specs=[vmem] * 8,
        out_specs=(vmem,) * 12,
        name="place",
    )(*results)


def rope_tables(length):
    inverse = np.float32(10000.0) ** (-np.arange(32, dtype=np.float32) / np.float32(32))
    angles = np.arange(length, dtype=np.float32)[:, None] * inverse[None, :]
    cosine, sine = np.cos(angles), np.sin(angles)
    return np.tile(cosine, (1, 4)), np.concatenate([-sine, sine, -sine, sine], axis=1)


def per_device(
    tokens, routes, slot_order, prefix, attn_gain, w_query, w_key, w_value, w_out, ffn_gain, w_router,
    w_gate, w_up, w_down, cotangent,
):
    cosine, sine = rope_tables(512)
    results = layer(
        prefix, tokens, routes[0].T, slot_order[0], attn_gain, ffn_gain, w_router[0].T,
        w_query.reshape(4, 4, 2, 32, 1024), w_key.reshape(BIG), w_value.reshape(BIG), w_out.reshape(4, 4, 2, 32, 1024),
        w_gate.reshape(3, *BIG), w_up.reshape(3, *BIG), w_down[0], cotangent, jnp.asarray(cosine), jnp.asarray(sine),
    )
    hidden_out, input_grad, gain_attn, query, key, value, out, gain_ffn, router, gate, up, down = place(*results)
    return (
        hidden_out, input_grad, gain_attn, query[None], key[None], value[None], out.T[None], gain_ffn, router[None],
        gate[None], up[None], down.transpose(0, 2, 1)[None],
    )


def solution(mesh):
    both = ("group", "expert")
    in_specs = (
        P(both, None), P(None, both, None), P(None, both, None), P("group"), P(), P(), P(), P(), P(), P(), P(),
        P(None, "expert", None, None), P(None, "expert", None, None), P(None, "expert", None, None), P(both, None),
    )
    out_specs = (
        P(both, None), P(both, None), P(None, both), P(None, both, None), P(None, both, None), P(None, both, None),
        P(None, None, both), P(None, both), P(None, both, None), P(None, "expert", "group", None),
        P(None, "expert", "group", None), P(None, "expert", None, "group"),
    )
    return jax.shard_map(per_device, mesh=mesh, in_specs=in_specs, out_specs=out_specs, check_vma=False)
```

```python
import jax
import jax.numpy as jnp
import numpy as np
from jax import lax
from jax.experimental import pallas as pl
from jax.experimental.pallas import tpu as pltpu
from jax.sharding import PartitionSpec as P

MESH = pl.DeviceIdType.MESH
LOW = jnp.bfloat16
F32 = jnp.float32
EPS = 1e-06
CAP = 96
EXPERTS = 12
OWN_EXPERTS = 3
EXPERT_UNITS = 9
UNITS = 13
WIDE, NARROW = 512, 384
KV_UNIT, OUT_UNIT = 9, 11
SLOTS = (0, 1, 2, 3, 4, 5, 6, 7, 8, 9, 10, 13, 14)
PROBS, SLABS, SLOT_COUNT = 9, 11, 16
BIG = (4, 4, 2, 32, WIDE)


PLAN = (
    (),
    (),
    (),
    ((0, 0),),
    ((0, 3),),
    ((0, 6),),
    ((1, 0),),
    (),
    (),
    ((1, 3),),
    ((0, 1),),
    ((1, 6), (0, 4)),
    ((0, 7), (2, 0), (2, 3), (0, 2), (0, 5), (1, 1)),
    ((2, 6),),
    ((0, 8),),
    ((1, 7), (1, 4), (5, 0)),
    ((5, 3),),
    (),
    ((0, 11),),
    ((1, 5), (1, 2)),
    ((0, 12),),
    ((2, 1),),
    (
        (0, 10), (1, 12), (1, 11), (6, 0), (2, 7), (1, 9), (2, 4), (2, 5), (0, 13), (2, 2), (3, 0), (3, 3), (5, 1),
        (2, 8), (3, 6),
    ),
    ((1, 10), (2, 9), (2, 11), (1, 13), (2, 12), (5, 4), (5, 7), (5, 5)),
    (
        (2, 10), (3, 9), (2, 13), (3, 12), (3, 11), (3, 10), (5, 2), (5, 8), (3, 13), (3, 1), (3, 4), (3, 7),
        (3, 5), (3, 2), (3, 8),
    ),
    ((6, 1), (4, 9), (4, 12), (4, 11), (4, 10), (4, 13)),
    (),
    (),
    ((5, 6), (1, 8)),
    ((0, 9),),
)


def group_of(x_at, z_at, core):
    return x_at * 8 + z_at * 2 + core


def dot(first, second):
    return jnp.dot(first, second, preferred_element_type=F32)


def dot_nt(first, second):
    return lax.dot_general(first, second, (((1,), (1,)), ((), ())), preferred_element_type=F32)


def dot_tn(first, second):
    return lax.dot_general(first, second, (((0,), (0,)), ((), ())), preferred_element_type=F32)


def add(first, second):
    return first + second


def lanes_of(shape):
    return lax.broadcasted_iota(jnp.int32, shape, len(shape) - 1)


def turn(values, cosine, sine, sign):
    first = lanes_of((values.shape[0], 128)) % 64 < 32
    parts = []
    for at in range(values.shape[1] // 128):
        part = values[:, at * 128 : at * 128 + 128]
        swapped = jnp.where(first, pltpu.roll(part, 96, 1), pltpu.roll(part, 32, 1))
        parts.append(part * cosine + sign * (swapped * sine))
    return parts[0] if len(parts) == 1 else jnp.concatenate(parts, axis=1)


def four_heads(first, second):
    low_half = lanes_of((128, 128)) < 64
    zero = jnp.zeros((128, 128), F32)
    return jnp.concatenate(
        [
            jnp.where(low_half, first, zero),
            jnp.where(low_half, pltpu.roll(first, 64, 1), zero),
            jnp.where(low_half, zero, pltpu.roll(second, 64, 1)),
            jnp.where(low_half, zero, second),
        ],
        axis=0,
    ).astype(LOW)


def unfold_heads(stood):
    first = jnp.concatenate([stood[0:64, 0:128], stood[0:64, 128:256]], axis=0)
    second = jnp.concatenate([stood[64:128, 256:384], stood[64:128, 384:512]], axis=0)
    return first.T, second.T


def loop(count, body):
    def step(index, carry):
        body(index)
        return carry

    lax.fori_loop(0, count, step, 0)


def lane_block(index, width=128):
    return pl.ds(pl.multiple_of(index * width, width), width)


def layer_kernel(
    prefix, tokens_far, routes_far, order_far, attn_gain_far, ffn_gain_far, w_router_far,
    wq_far, wk_far, wv_far, wo_far, wg_far, wu_far, wd_far, cot_far, cos_far, sin_far,
    hidden_to, input_to, expert_to, query_to, key_to, value_to, out_to, misc_to,
    hidden_out, input_grad, expert_out, query_out, key_out, value_out, out_out, misc_out,
    tokens, routes, order, attn_gain, ffn_gain, w_router,
    grads, weights, wd, router, cot, cosine, sine,
    normed_all, joined, q_four, kv_all, x_all, g_all, code_all, codes,
    x_t, g_t, probs, gates, own_dots, dots_send, dots_in, row_send, row_in, mix_in, q_low, q_all, grad_in,
    pair_in, lo_in, hi_in, minus_in, plus_in, cells_in, last, last_in,
    misc, misc_pair, misc_lo, misc_hi, misc_minus, misc_plus, misc_cells,
    misc_last, misc_last_in,
    y_send, y_recv, send_sem, recv_sem, local_sem,
):
    group = lax.axis_index("group")
    y_at = lax.axis_index("expert")
    x_at, z_at, core = group // 8, (group // 2) % 4, group % 2
    spots = (x_at, z_at)
    own_rows = pl.ds(pl.multiple_of(y_at * 128, 128), 128)
    middle, own_row, normed_t = hidden_out, input_grad, g_t

    def device(axis, offset):
        if axis == 0:
            return (group_of((x_at + offset) % 4, z_at, core), y_at)
        return (group_of(x_at, (z_at + offset) % 4, core), y_at)

    def across(offset):
        return (group, (y_at + offset) % 4)

    partner = (group_of(x_at, z_at, 1 - core), y_at)
    barrier = pltpu.get_barrier_semaphore()
    peers = [partner] + [device(axis, off) for axis in (0, 1) for off in (1, 3)]
    peers += [across(off) for off in (1, 2, 3)]
    for peer in peers:
        pl.semaphore_signal(barrier, inc=1, device_id=peer, device_id_type=MESH)

    half = pl.ds(0, WIDE), pl.ds(WIDE, WIDE)
    loads = {}

    def load(name, src, dst):
        copy = pltpu.make_async_copy(src, dst, local_sem.at[len(loads)])
        loads[name] = copy
        copy.start()

    def load_keys(tag, ref, wk_to, wv_to):
        load((tag, 0), wk_far, ref.at[wk_to])
        load((tag, 1), wv_far, ref.at[wv_to])

    def load_pair(tag, at, src, ref, to):
        for part in (0, 1):
            load((tag, at + part), src.at[:, :, :, :, half[part]], ref.at[to + part])

    small = (
        (tokens_far, tokens), (attn_gain_far, attn_gain), (routes_far, routes), (order_far, order),
        (ffn_gain_far, ffn_gain), (w_router_far, w_router),
    )
    for at, (src, dst) in enumerate(small):
        load(("small", at), src, dst)
    load_pair("fwd", 2, wq_far, grads, 2)
    load("cos", cos_far, cosine)
    load("sin", sin_far, sine)
    load_keys("fwd", grads, 0, 1)

    def square(ref, unit):
        return ref[unit].reshape(1024, WIDE)

    def slab(index, rows=None):
        unit, top = SLABS + index // 2, (index % 2) * 2
        if rows is None:
            return grads.at[unit, pl.ds(top, 2)]
        kind, at = rows
        if kind == 256:
            return grads.at[unit, top + at]
        return grads.at[unit, top + at // 2, pl.ds((at % 2) * 2, 2)]

    for at in (0, 1):
        loads[("small", at)].wait()
    hidden = tokens[...].astype(F32)
    attn_r = lax.rsqrt(jnp.mean(hidden * hidden, axis=1, keepdims=True) + EPS)
    normed_all[y_at] = (hidden * attn_r * attn_gain[...]).astype(LOW)
    for at in (2, 3):
        loads[("small", at)].wait()
    expert_at = lax.broadcasted_iota(jnp.int32, (128, 128), 0)
    member = jnp.zeros((128, 128), F32)
    for pick in range(routes.shape[0]):
        member = member + jnp.where(routes[pick : pick + 1, :] == expert_at, 1.0, 0.0)
    member = member.T
    ranks = jnp.broadcast_to(order[...].astype(F32), (128, 128))
    earlier = jnp.where(ranks < ranks.T, 1.0, 0.0).astype(LOW)
    before = dot(earlier, member.astype(LOW))
    code = jnp.where((member > 0.5) & (before < CAP - 0.5), 2.0, member)
    code_all[y_at] = code.T[0:16].astype(LOW)
    pl.semaphore_wait(barrier, len(peers))

    y_used = []

    def y_copy(off, src, dst):
        at = len(y_used)
        y_used.append(off)
        return pltpu.make_async_remote_copy(
            src_ref=src, dst_ref=dst, send_sem=y_send.at[at], recv_sem=y_recv.at[at],
            device_id=across(off), device_id_type=MESH,
        )

    def start(copies):
        for copy in copies:
            copy.start()

    def wait(copies):
        for copy in copies:
            copy.wait()

    left, right = (y_at + 3) % 4, (y_at + 1) % 4
    low_rows, high_rows = pl.ds(0, 64), pl.ds(64, 64)

    class Gather:
        def __init__(self, ref):
            def pass_on(block, rows, off):
                return y_copy(off, ref.at[block, rows], ref.at[block, rows])

            self.first = [pass_on(y_at, low_rows, 1), pass_on(y_at, high_rows, 3)]
            self.first += [pass_on(y_at, high_rows, 1), pass_on(y_at, low_rows, 3)]
            self.second = [pass_on(left, low_rows, 1), pass_on(right, high_rows, 3)]

        def start(self):
            start(self.first)

        def forward(self):
            for came, on in zip(self.first, self.second):
                came.wait_recv()
                on.start()

        def near(self):
            for copy in self.first[2:]:
                copy.wait_recv()

        def finish(self):
            for copy in self.first:
                copy.wait_send()
            wait(self.second)

    class Scatter:
        def __init__(self, spot, send, block, land):
            self.block, self.land = block, land
            far, self.right, self.left = (spot + 2) % 4, (spot + 1) % 4, (spot + 3) % 4
            self.far = [send(1, block(far, 0), land(0, 0)), send(3, block(far, 1), land(0, 1))]
            self.near = [send(1, block(self.right, 1), land(1, 1)), send(3, block(self.left, 0), land(2, 0))]
            self.last = [send(1, block(self.right, 0), land(1, 0)), send(3, block(self.left, 1), land(2, 1))]

        def start(self):
            start(self.far)
            start(self.near)

        def turn(self):
            for part, to in ((0, self.right), (1, self.left)):
                self.far[part].wait()
                ref = self.block(to, part)
                ref[...] = add(ref[...], self.land(0, part)[...])
                self.last[part].start()

        def finish(self):
            wait(self.near)
            wait(self.last)

    normed_share = Gather(normed_all)
    normed_share.start()
    code_share = [y_copy(off, code_all.at[y_at], code_all.at[y_at]) for off in (1, 3, 2)]
    start(code_share)
    load_pair("fwd", 4, wo_far, grads, 4)
    load("cot", cot_far, cot)
    load("wg", wg_far, weights.at[pl.ds(0, 3)])
    load("wu", wu_far, weights.at[pl.ds(3, 3)])
    load("wd", wd_far, wd)

    for name in ("cos", "sin", ("small", 4), ("small", 5)):
        loads[name].wait()
    for part in (0, 1):
        loads[("fwd", 2 + part)].wait()
        turned = turn(dot(normed_all[y_at], square(grads, 2 + part)), cosine[own_rows, :], sine[own_rows, :], 1.0)
        turned = turned.astype(LOW).astype(F32)
        for c in (0, 1):
            q_four[part * 2 + c] = four_heads(
                turned[:, c * 256 : c * 256 + 128], turned[:, c * 256 + 128 : c * 256 + 256]
            )

    loads["cot"].wait()
    g_all[y_at] = cot[...].astype(LOW)
    router[...] = jnp.zeros_like(router)
    router[0:EXPERTS, :] = w_router[...]
    for part in (0, 1):
        loads[("fwd", part)].wait()
    normed_share.forward()
    g_share = Gather(g_all)
    g_share.start()
    normed_share.near()
    normed_share.finish()

    def keys_values(part):
        lanes = lane_block(part, 256)
        inputs = normed_all[...].reshape(512, 1024)
        keys = turn(dot(inputs, grads[0, :, :, :, :, lanes].reshape(1024, 256)), cosine[...], sine[...], 1.0)
        kv_all[:, :, lanes] = keys.astype(LOW).reshape(4, 128, 256)
        values = dot(inputs, grads[1, :, :, :, :, lanes].reshape(1024, 256))
        kv_all[:, :, lane_block(2 + part, 256)] = values.astype(LOW).reshape(4, 128, 256)

    loop(2, keys_values)

    def visible():
        shape = (512, 512)
        key_at = lax.broadcasted_iota(jnp.int32, shape, 0)
        query_at = y_at * 128 + lanes_of(shape) % 128
        return (key_at < prefix[0]) | (key_at <= query_at)

    def key_block(c):
        return kv_all[:, :, lane_block(c)].reshape(512, 128)

    def value_block(c):
        return kv_all[:, :, lane_block(c + 4)].reshape(512, 128)

    def prob_ref(c):
        return grads.at[PROBS + c // 2, pl.ds((c % 2) * 2, 2)]

    def attend(c):
        scores = jnp.where(visible(), dot_nt(key_block(c), q_four[c]) * 0.125, -1e30)
        raised = jnp.exp(scores - jnp.max(scores, axis=0, keepdims=True))
        soft = (raised * (1.0 / jnp.sum(raised, axis=0, keepdims=True))).astype(LOW)
        prob_ref(c)[...] = soft.reshape(2, 4, 2, 32, WIDE)
        first, second = unfold_heads(dot_tn(value_block(c), soft))
        joined[:, lane_block(2 * c)] = first.astype(LOW)
        joined[:, lane_block(2 * c + 1)] = second.astype(LOW)

    loop(4, attend)
    loads[("fwd", 4)].wait()
    loads[("fwd", 5)].wait()
    for part in (0, 1):
        middle[:, half[part]] = tokens[:, half[part]].astype(F32) + dot(joined[...], square(grads, 4 + part))
    ffn_r = lax.rsqrt(jnp.mean(middle[...] * middle[...], axis=1, keepdims=True) + EPS)
    x_all[y_at] = (middle[...] * ffn_r * ffn_gain[...]).astype(LOW)
    x_share = Gather(x_all)
    x_share.start()

    wait(code_share)
    for block in range(4):
        short = code_all[block].astype(F32)
        codes[block] = jnp.concatenate([short, jnp.zeros((112, 128), F32)], axis=0).T

    def stand(ref, out):
        def body(block):
            out[:, lane_block(block)] = ref[block].T

        loop(4, body)

    x_share.forward()
    g_share.forward()
    for name in ("wg", "wu", "wd"):
        loads[name].wait()
    slab_shape = (2, 4, 2, 32, 256)

    def gate_of(j, rows=pl.ds(0, 512), count=512):
        here = lanes_of((count, 128)) == y_at * OWN_EXPERTS + j
        return here, jnp.sum(jnp.where(here, gates[rows, :], 0.0), axis=1, keepdims=True)

    def expert_forward(blocks):
        def rows_of(ref):
            return jnp.concatenate([ref[block] for block in blocks], axis=0)

        code = rows_of(codes)
        in_use = code > 0.5
        logits = jnp.where(in_use, dot_nt(rows_of(x_all), router[...]), -1e30)
        raised = jnp.where(in_use, jnp.exp(logits - jnp.max(logits, axis=1, keepdims=True)), 0.0)
        soft = raised / jnp.sum(raised, axis=1, keepdims=True)
        kept = jnp.where(code > 1.5, soft, 0.0)
        for at, block in enumerate(blocks):
            probs[block] = soft[128 * at : 128 * at + 128]
            gates[lane_block(block), :] = kept[128 * at : 128 * at + 128]

        def body(step):
            j, lanes = step // 2, lane_block(step % 2, 256)
            inputs = rows_of(x_all)
            gate_lin = dot(inputs, weights[j, :, :, :, :, lanes].reshape(1024, 256))
            up_lin = dot(inputs, weights[3 + j, :, :, :, :, lanes].reshape(1024, 256))
            sig = 1.0 / (1.0 + jnp.exp(-gate_lin))
            silu = gate_lin * sig
            gate = jnp.concatenate([gate_of(j, lane_block(block), 128)[1] for block in blocks], axis=0)
            act = (silu * up_lin).astype(LOW).astype(F32) * gate
            slope = up_lin * sig * (1.0 + gate_lin * (1.0 - sig))
            for index, value in ((6 + j, act), (j, slope), (3 + j, silu)):
                value = value.astype(LOW)
                for at, block in enumerate(blocks):
                    piece = value[128 * at : 128 * at + 128].reshape(2, 2, 32, 256)
                    slab(index, (128, block))[:, :, :, lanes] = piece

        loop(2 * OWN_EXPERTS, body)

    own_dots[...] = jnp.zeros_like(own_dots)
    x_share.near()
    expert_forward((y_at, left, right))
    x_share.finish()
    expert_forward(((y_at + 2) % 4,))

    def expert_back(step):
        j, lanes = step // 2, lane_block(step % 2, 256)
        here, gate = gate_of(j)
        outer = dot_nt(g_all[...].reshape(512, 1024), wd[j, lanes, :])
        act = slab(6 + j)[:, :, :, :, lanes].reshape(512, 256).astype(F32)
        own_dots[...] += jnp.where(here, jnp.sum(act * outer, axis=1, keepdims=True), 0.0)
        outer = outer * gate
        for index in (j, 3 + j):
            slope = slab(index)[:, :, :, :, lanes].reshape(512, 256).astype(F32)
            slab(index)[:, :, :, :, lanes] = (outer * slope).astype(LOW).reshape(slab_shape)

    stand(x_all, x_t)
    g_share.near()
    g_share.finish()
    loop(2, expert_back)

    class Wide:
        src, pair, lo, hi, minus, plus = grads, pair_in, lo_in, hi_in, minus_in, plus_in
        cells = cells_in

    class Narrow:
        src, pair, lo, hi, minus, plus = misc, misc_pair, misc_lo, misc_hi, misc_minus, misc_plus
        cells = misc_cells

    class Unit:
        def __init__(self, unit):
            self.unit, self.axis, self.used = unit, unit % 2, 0
            self.set, self.at = (Wide, unit) if unit < UNITS else (Narrow, 0)
            s = self.set
            ref = s.src.at[SLOTS[unit] if s is Wide else 0]
            self.ref = ref
            self.pair = self.remote(partner, ref.at[:, :, 1 - core], s.pair.at[self.at])

            def block(index, part):
                halves = pl.ds(2 * part, 2)
                return ref.at[index, halves, core] if self.axis == 0 else ref.at[halves, index, core]

            def land(at, part):
                if at == 0:
                    return (s.lo, s.hi)[part].at[self.at]
                return (s.minus, s.plus)[at - 1].at[self.at, pl.ds(2 * part, 2)]

            def cell(index):
                return ref.at[x_at, index, core] if self.axis == 0 else ref.at[index, z_at, core]

            axis = self.axis
            self.ring = Scatter(spots[axis], lambda off, src, dst: self.remote(device(axis, off), src, dst), block, land)
            spot = spots[1 - axis]
            self.cell, self.cells_in = cell(spot), [s.cells.at[off, self.at] for off in range(3)]
            self.direct = unit >= EXPERT_UNITS
            if self.direct:
                self.cells = [
                    self.remote(device(1 - axis, off), cell((spot + off) % 4), self.cells_in[off - 1]) for off in (1, 3, 2)
                ]
            else:
                self.ring_b = Scatter(
                    spot,
                    lambda off, src, dst: self.remote(device(1 - axis, off), src, dst),
                    lambda index, part: cell(index).at[pl.ds(16 * part, 16)],
                    lambda at, part: self.cells_in[at].at[pl.ds(16 * part, 16)],
                )
            self.own = ref.at[spots[0], :, core] if axis == 0 else ref.at[:, spots[1], core]
            if unit >= EXPERT_UNITS:
                src, dst, at = (last, last_in, unit - EXPERT_UNITS) if s is Wide else (misc_last, misc_last_in, 0)
                self.last, self.last_in = src.at[at], [dst.at[off, at] for off in range(3)]
                self.across = [
                    self.remote(across(off), self.last.at[pl.ds((y_at + off) % 4 * 8, 8)], self.last_in[off - 1])
                    for off in (1, 2, 3)
                ]

        def remote(self, to, src, dst):
            self.used += 1
            return pltpu.make_async_remote_copy(
                src_ref=src, dst_ref=dst, send_sem=send_sem.at[self.unit, self.used - 1],
                recv_sem=recv_sem.at[self.unit, self.used - 1], device_id=to, device_id_type=MESH,
            )

        def begin(self):
            self.pair.start()

        def after_pair(self):
            s = self.set
            self.pair.wait()
            for slab_at in range(4):
                ref = self.ref.at[slab_at, :, core]
                ref[...] = add(ref[...], s.pair[self.at, slab_at])
            self.ring.start()

        def turn(self):
            self.ring.turn()

        def after_ring(self):
            s = self.set
            self.ring.finish()
            total = self.own[...].astype(F32) + s.minus[self.at].astype(F32)
            self.own[...] = (total + s.plus[self.at].astype(F32)).astype(LOW)
            (start(self.cells) if self.direct else self.ring_b.start())

        def turn_b(self):
            self.ring_b.turn()

        def after_cells(self):
            if self.direct:
                wait(self.cells)
            else:
                self.ring_b.finish()
            total = self.cell[...].astype(F32)
            for came in self.cells_in if self.direct else self.cells_in[1:]:
                total = total + came[...].astype(F32)
            if self.unit < EXPERT_UNITS:
                expert_out[self.unit] = total
            else:
                self.last[...] = total
                start(self.across)

        def finish(self):
            wait(self.across)
            total = self.last[pl.ds(pl.multiple_of(y_at * 8, 8), 8), :]
            if self.set is Narrow:
                for off in range(4):
                    rows = self.last_in[off - 1][:, 0:256] if off else total[:, 0:256]
                    query_out[:, lane_block((y_at + 4 - off) % 4, 256)] = rows
            for came in self.last_in:
                total = total + came[...]
            if self.unit in (KV_UNIT, KV_UNIT + 1):
                lanes = lane_block(self.unit - KV_UNIT, 256)
                key_out[:, lanes] = total[:, 0:256]
                value_out[:, lanes] = total[:, 256:]
            elif self.set is Wide:
                out_out[:, half[self.unit - OUT_UNIT]] = total
            else:
                misc_out[...] = total[:, 256:]

    extras = {}
    stages = (Unit.after_pair, Unit.turn, Unit.after_ring, Unit.after_cells, Unit.finish, Unit.turn_b)
    units = [Unit(unit) for unit in range(UNITS + 1)]

    def run(point):
        for stage, unit in PLAN[point]:
            if stage < len(stages):
                stages[stage](units[unit])
            else:
                extras[unit]()

    def weight_grad(unit, left, right):
        grads[SLOTS[unit]] = dot(left[...], right()).astype(LOW).reshape(BIG)
        units[unit].begin()

    def slab_value(index):
        return lambda: slab(index)[...].reshape(512, WIDE)

    def expert_units(j, point):
        for at, (kind, turned_rows) in enumerate(((0, x_t), (3, x_t), (6, g_t))):
            if kind + j == 6:
                stand(g_all, g_t)
            weight_grad(kind + j, turned_rows, slab_value(kind + j))
            run(point + at)
            if kind + j == 4:
                rows_back.turn()

    expert_units(0, 0)
    loop(2, lambda step: expert_back(step + 2))
    run(26)
    loop(2, lambda step: expert_back(step + 4))
    run(27)

    dots_copies = [y_copy(off, dots_send.at[(y_at + off) % 4], dots_in.at[off - 1]) for off in (1, 3, 2)]
    for block in range(4):
        dots_send[block] = own_dots[block * 128 : block * 128 + 128, :].T[0:16, :]
    start(dots_copies)

    def row_part(first, second):
        total = None
        for j in range(OWN_EXPERTS):
            for kind in (0, 3):
                pair = [slab(kind + j, (128, block))[...].reshape(128, WIDE) for block in (first, second)]
                part = dot_nt(jnp.concatenate(pair, axis=0), square(weights, kind + j))
                total = part if total is None else total + part
        return total

    def across_block(off):
        return (y_at + off) % 4

    rows = row_part(across_block(2), across_block(1))
    for off in (2, 1):
        row_send[across_block(off)] = rows[128 * (2 - off) : 128 * (3 - off)].astype(LOW)
    rows_back = Scatter(
        y_at, y_copy, lambda block, part: row_send.at[block, pl.ds(64 * part, 64)], lambda at, part: row_in.at[at, pl.ds(64 * part, 64)]
    )
    start(rows_back.far)
    rows_back.near[0].start()
    run(3)
    rows = row_part(across_block(3), y_at)
    row_send[across_block(3)] = rows[0:128].astype(LOW)
    rows_back.near[1].start()
    own_row[...] = rows[128:256]
    run(4)
    load_pair("bwd", 4, wo_far, weights, 3)
    load_pair("bwd", 2, wq_far, weights, 0)
    load_keys("bwd", weights, 2, 5)

    expert_units(1, 5)
    expert_units(2, 8)

    def mix_part(part):
        total = None
        for j in range(OWN_EXPERTS):
            piece = dot(slab(6 + j, (256, part))[...].reshape(256, WIDE), wd[j])
            total = piece if total is None else total + piece
        x_all[pl.ds(part * 2, 2)] = total.astype(LOW).reshape(2, 128, 1024)

    loop(2, mix_part)
    run(11)

    def normed_stand(block):
        normed_t[:, lane_block(block)] = normed_all[block].T

    loop(4, normed_stand)
    run(12)

    wait(dots_copies)
    rows_back.finish()
    mix_back = Scatter(
        y_at, y_copy, lambda block, part: x_all.at[block, pl.ds(64 * part, 64)], lambda at, part: mix_in.at[at, pl.ds(64 * part, 64)]
    )
    mix_back.start()
    taken = dots_send[y_at]
    moe_grad = own_row[...]
    for off in (1, 2, 3):
        taken = taken + dots_in[off - 1]
    for at in (1, 2):
        moe_grad = moe_grad + row_in[at].astype(F32)
    taken = jnp.concatenate([taken, jnp.zeros((112, 128), F32)], axis=0).T
    own_probs = probs[y_at]
    select = taken - own_probs * jnp.sum(taken, axis=1, keepdims=True)
    select = select.astype(LOW)
    moe_grad = moe_grad + dot(select, router[...])
    router_grad = dot(x_t[:, lane_block(y_at)], select)
    normal = middle[...]
    ffn_r = lax.rsqrt(jnp.mean(normal * normal, axis=1, keepdims=True) + EPS)
    scaled = moe_grad * ffn_gain[...]
    ffn_gain_grad = jnp.sum(moe_grad * normal * ffn_r, axis=0, keepdims=True)
    shrink = ffn_r * ffn_r * ffn_r * jnp.mean(scaled * normal, axis=1, keepdims=True)
    cot[...] = cot[...] + ffn_r * scaled - normal * shrink
    attn_grad = cot[...].astype(LOW)
    for part in (0, 1):
        loads[("bwd", 4 + part)].wait()
    head_grad = dot_nt(attn_grad[:, 0:WIDE], square(weights, 3)) + dot_nt(attn_grad[:, WIDE:], square(weights, 4))
    head_low = head_grad.astype(LOW).astype(F32)
    run(13)

    def head_ref(c):
        return x_t.at[lane_block(c % 2, 512), lane_block(1 + c // 2)]

    for c in range(4):
        head_ref(c)[...] = four_heads(head_low[:, c * 256 : c * 256 + 128], head_low[:, c * 256 + 128 : c * 256 + 256])
    x_t[:, 0:128] = attn_grad.T
    for part in (0, 1):
        weight_grad(OUT_UNIT + part, x_t.at[:, pl.ds(0, 128)], lambda: joined[:, half[part]])
    run(14)

    extras[0] = mix_back.turn

    key_sums, value_sums = pair_in.at[0], pair_in.at[3]
    def attend_back(c):
        heads = head_ref(c)[...]
        low = prob_ref(c)[...].reshape(512, 512)
        soft = low.astype(F32)
        weighted = soft * dot_nt(value_block(c), heads)
        sums = jnp.sum(weighted, axis=0, keepdims=True)
        score_grad = ((weighted - soft * sums) * 0.125).astype(LOW)
        value_sums[:, :, :, lane_block(c)] = dot(low, heads).astype(LOW).reshape(4, 4, 32, 128)
        key_part = turn(dot(score_grad, q_four[c]), cosine[...], sine[...], -1.0)
        key_sums[:, :, :, lane_block(c)] = key_part.astype(LOW).reshape(4, 4, 32, 128)
        first, second = unfold_heads(dot_tn(key_block(c), score_grad))
        own_cosine, own_sine = cosine[own_rows, :], sine[own_rows, :]
        q_low[:, lane_block(2 * c)] = turn(first, own_cosine, own_sine, -1.0).astype(LOW)
        q_low[:, lane_block(2 * c + 1)] = turn(second, own_cosine, own_sine, -1.0).astype(LOW)

    def kv_columns(part):
        lanes = pl.ds(256 * part, 256)
        return jnp.concatenate([ref[:, :, :, lanes].reshape(512, 256) for ref in (key_sums, value_sums)], axis=1)

    for c in range(4):
        attend_back(c)
        run(15 + c)
        if c % 2 == 1:
            weight_grad(KV_UNIT + c // 2, normed_t, lambda: kv_columns(c // 2))
            run(19 + c // 2)
    q_copies = [y_copy(off, q_low.at[:, lane_block(across_block(off), 256)], q_all.at[y_at]) for off in (1, 3, 2)]
    start(q_copies)
    q_all[y_at] = q_low[:, lane_block(y_at, 256)]

    for part in (0, 1, 2, 3):
        loads[("bwd", part)].wait()
    gain_rows = jnp.zeros((1, 1024), F32)
    for part in (0, 1):
        blocks = pl.ds(2 * part, 2)
        rows = dot_nt(key_sums[blocks].reshape(256, WIDE), square(weights, 2))
        rows = rows + dot_nt(value_sums[blocks].reshape(256, WIDE), square(weights, 5))
        row_send[blocks] = rows.astype(LOW).reshape(2, 128, 1024)
        scaled = rows * normed_all[blocks].reshape(256, 1024).astype(F32)
        gain_rows = gain_rows + jnp.sum(scaled, axis=0, keepdims=True)
        if part == 0:
            run(28)
    grad_back = Scatter(
        y_at, y_copy, lambda block, part: row_send.at[block, pl.ds(64 * part, 64)], lambda at, part: grad_in.at[at, pl.ds(64 * part, 64)]
    )
    grad_back.start()
    run(29)
    rows = dot_nt(q_low[:, 0:WIDE], square(weights, 0)) + dot_nt(q_low[:, WIDE:], square(weights, 1))
    input_grad[...] = rows
    gain_rows = gain_rows + jnp.sum(rows * normed_all[y_at].astype(F32), axis=0, keepdims=True)
    wide_lane = lanes_of((1024, 128))
    gains = jnp.where(
        wide_lane == EXPERTS,
        jnp.broadcast_to(gain_rows / attn_gain[...], (128, 1024)).T,
        jnp.broadcast_to(ffn_gain_grad, (128, 1024)).T,
    )
    gains = jnp.where(wide_lane < EXPERTS, router_grad, gains).astype(LOW)
    misc[0, :, :, :, :, 256:] = gains.reshape(4, 4, 2, 32, 128)
    run(21)
    wait(q_copies)
    misc[0, :, :, :, :, 0:256] = dot(normed_t[...], q_all[...].reshape(512, 256)).astype(LOW).reshape(4, 4, 2, 32, 256)
    units[UNITS].begin()
    run(22)
    grad_back.turn()
    run(23)

    grad_back.finish()
    normed_grad = input_grad[...] + row_send[y_at].astype(F32) + grad_in[1].astype(F32) + grad_in[2].astype(F32)
    hidden = tokens[...].astype(F32)
    attn_r = lax.rsqrt(jnp.mean(hidden * hidden, axis=1, keepdims=True) + EPS)
    scaled = normed_grad * attn_gain[...]
    shrink = attn_r * attn_r * attn_r * jnp.mean(scaled * hidden, axis=1, keepdims=True)
    input_grad[...] = cot[...] + attn_r * scaled - hidden * shrink
    results = {}

    def result(src, dst):
        copy = pltpu.make_async_copy(src, dst, local_sem.at[len(loads) + len(results)])
        results[len(results)] = copy
        copy.start()

    result(input_grad, input_to)

    def finish_mix():
        mix_back.finish()
        total = middle[...] + x_all[y_at].astype(F32)
        for at in (1, 2):
            total = total + mix_in[at].astype(F32)
        hidden_out[...] = total
        result(hidden_out, hidden_to)

    extras[1] = finish_mix
    run(24)
    result(expert_out, expert_to)
    run(25)
    for src, dst in ((query_out, query_to), (key_out, key_to), (value_out, value_to), (out_out, out_to), (misc_out, misc_to)):
        result(src, dst)
    wait(results.values())


def layer(*args):
    smem = pl.BlockSpec(memory_space=pltpu.SMEM)
    far = pl.BlockSpec(memory_space=pl.ANY)
    low = lambda *shape: pltpu.VMEM(shape, LOW)
    wide = lambda *shape: pltpu.VMEM(shape, F32)
    sems = pltpu.SemaphoreType.DMA
    scratch = [
        wide(128, 1024), wide(128, 1024), wide(EXPERT_UNITS, 32, WIDE),
        wide(8, 1024), wide(8, WIDE), wide(8, WIDE), wide(8, 1024), wide(8, 128),
        low(128, 1024), pltpu.VMEM((8, 128), jnp.int32), pltpu.VMEM((1, 128), jnp.int32),
        wide(1, 1024), wide(1, 1024), low(EXPERTS, 1024),
        low(SLOT_COUNT, *BIG), low(6, *BIG), low(3, 512, 1024), low(128, 1024), wide(128, 1024), wide(512, 128), wide(512, 128),
        low(4, 128, 1024), low(128, 1024), low(4, 512, 128),
        low(4, 128, 1024), low(4, 128, 1024), low(4, 128, 1024), low(4, 16, 128), wide(4, 128, 128),
        low(1024, 512), low(1024, 512), wide(4, 128, 128), wide(512, 128), wide(512, 128),
        wide(4, 16, 128), wide(3, 16, 128), low(4, 128, 1024), low(3, 128, 1024), low(3, 128, 1024),
        low(128, 1024), low(4, 128, 256), low(3, 128, 1024),
    ]
    for count, width in ((UNITS, WIDE), (1, NARROW)):
        if count == 1:
            scratch += [low(1, 4, 4, 2, 32, width)]
        scratch += [low(count, 4, 4, 32, width), low(count, 2, 32, width), low(count, 2, 32, width)]
        scratch += [low(count, 4, 32, width), low(count, 4, 32, width)]
        scratch += [low(3, count, 32, width)]
        shared = count - EXPERT_UNITS if count == UNITS else 1
        scratch += [wide(shared, 32, width), wide(3, shared, 8, width)]
    scratch += [sems((48,)), sems((48,)), sems((UNITS + 1, 16)), sems((UNITS + 1, 16)), sems((32,))]
    shape = jax.ShapeDtypeStruct
    return pl.pallas_call(
        layer_kernel,
        out_shape=(
            shape((128, 1024), F32),
            shape((128, 1024), F32),
            shape((EXPERT_UNITS, 32, WIDE), F32),
            shape((8, 1024), F32),
            shape((8, WIDE), F32),
            shape((8, WIDE), F32),
            shape((8, 1024), F32),
            shape((8, 128), F32),
        ),
        in_specs=[smem] + [far] * 16,
        out_specs=(far,) * 8,
        scratch_shapes=scratch,
        compiler_params=pltpu.CompilerParams(
            collective_id=0, has_side_effects=True, vmem_limit_bytes=60 * 2**20
        ),
        name="layer",
    )(*args)


def place_kernel(
    hidden_in, input_in, experts_in, query_in, key_in, value_in, out_in, misc_in,
    hidden_out, input_grad, attn_gain, query, key, value, out, ffn_gain, router, gate, up, down,
):
    hidden_out[...] = hidden_in[...]
    input_grad[...] = input_in[...]
    for kind, to in enumerate((gate, up, down)):
        to[...] = experts_in[3 * kind : 3 * kind + 3]
    for src, to in ((query_in, query), (key_in, key), (value_in, value), (out_in, out)):
        to[...] = src[...]
    router[...] = misc_in[:, 0:EXPERTS]
    flipped = jnp.concatenate([misc_in[...], jnp.zeros((120, 128), F32)], axis=0).T
    attn_gain[...] = flipped[EXPERTS : EXPERTS + 1, 0:8]
    ffn_gain[...] = flipped[EXPERTS + 1 : EXPERTS + 2, 0:8]


def place(*results):
    vmem = pl.BlockSpec(memory_space=pltpu.VMEM)
    shape = lambda *dims: jax.ShapeDtypeStruct(dims, F32)
    return pl.pallas_call(
        place_kernel,
        out_shape=(
            shape(128, 1024), shape(128, 1024), shape(1, 8), shape(8, 1024), shape(8, WIDE), shape(8, WIDE), shape(8, 1024),
            shape(1, 8), shape(8, EXPERTS), shape(3, 32, WIDE), shape(3, 32, WIDE), shape(3, 32, WIDE),
        ),
        in_specs=[vmem] * 8,
        out_specs=(vmem,) * 12,
        name="place",
    )(*results)


def rope_tables(length):
    inverse = np.float32(10000.0) ** (-np.arange(32, dtype=np.float32) / np.float32(32))
    angles = np.arange(length, dtype=np.float32)[:, None] * inverse[None, :]
    cosine, sine = np.cos(angles), np.sin(angles)
    return np.tile(cosine, (1, 4)), np.concatenate([-sine, sine, -sine, sine], axis=1)


def per_device(
    tokens, routes, slot_order, prefix, attn_gain, w_query, w_key, w_value, w_out, ffn_gain, w_router,
    w_gate, w_up, w_down, cotangent,
):
    cosine, sine = rope_tables(512)
    results = layer(
        prefix, tokens, routes[0].T, slot_order[0], attn_gain, ffn_gain, w_router[0].T,
        w_query.reshape(4, 4, 2, 32, 1024), w_key.reshape(BIG), w_value.reshape(BIG), w_out.reshape(4, 4, 2, 32, 1024),
        w_gate.reshape(3, *BIG), w_up.reshape(3, *BIG), w_down[0], cotangent, jnp.asarray(cosine), jnp.asarray(sine),
    )
    hidden_out, input_grad, gain_attn, query, key, value, out, gain_ffn, router, gate, up, down = place(*results)
    return (
        hidden_out, input_grad, gain_attn, query[None], key[None], value[None], out.T[None], gain_ffn, router[None],
        gate[None], up[None], down.transpose(0, 2, 1)[None],
    )


def solution(mesh):
    both = ("group", "expert")
    in_specs = (
        P(both, None), P(None, both, None), P(None, both, None), P("group"), P(), P(), P(), P(), P(), P(), P(),
        P(None, "expert", None, None), P(None, "expert", None, None), P(None, "expert", None, None), P(both, None),
    )
    out_specs = (
        P(both, None), P(both, None), P(None, both), P(None, both, None), P(None, both, None), P(None, both, None),
        P(None, None, both), P(None, both), P(None, both, None), P(None, "expert", "group", None),
        P(None, "expert", "group", None), P(None, "expert", None, "group"),
    )
    return jax.shard_map(per_device, mesh=mesh, in_specs=in_specs, out_specs=out_specs, check_vma=False)
```
